512 devices in a mesh: dp: 32 (over z, core), proto: 16 (over x, y).
Axes of the slice: x: 4, y: 4, z: 16, core: 2. Of those that a mesh axis runs over, the one named last changes fastest.
Arguments:
- embeddings: bfloat16 [49152, 1536], P('dp'), may hold values from -13 to 13
- centroids: bfloat16 [8192, 1536], P('proto', 'dp'), may hold values from -6 to 6
Outputs:
- new_centroids: float32 [1536, 8192], P('dp', 'proto')
- cluster_mass: float32 [8192], P('proto')
The draws below stay inside these ranges and needn't reach their ends.
All inputs are finite; a program needn't handle non-finite values.
Results may differ from the reference program's by a relative error of at most 0.00031.
Values may be sent and summed in bfloat16 or wider, within the bound.
A program may use at most 64 MiB of HBM per device.

```python
import jax
import jax.numpy as jnp
from jax import lax

D = 1536
ROWS = 1536
SWEEPS = 3
N_ROWS = 49152
CENTROIDS = 8192
N_DP = 32


def cluster_axes(key):
    return jnp.clip(jax.random.normal(key, (8, D), jnp.float32), -4.0, 4.0)


def skewed_labels(key, count):
    first_key, second_key, third_key = jax.random.split(key, 3)
    first_pick = jax.random.randint(first_key, (count,), 0, 8)
    second_pick = jax.random.randint(second_key, (count,), 0, 8)
    third_pick = jax.random.randint(third_key, (count,), 0, 8)
    return jnp.minimum(jnp.minimum(first_pick, second_pick), third_pick)


def draw_embeddings(key, part):
    axes_table = cluster_axes(key)
    key = jax.random.fold_in(key, 11)
    label_key, strength_key, noise_key, pair_key = jax.random.split(key, 4)
    labels = skewed_labels(label_key, N_ROWS)
    strength = jax.random.uniform(strength_key, (N_ROWS, 1), jnp.float32, 0.1, 0.7)
    noise_part = jnp.clip(jax.random.normal(noise_key, (N_ROWS, D), jnp.float32), -4.0, 4.0)
    pairing = jax.random.permutation(pair_key, N_DP)
    row_owner = pairing[jnp.arange(N_ROWS) // ROWS]
    feature_block = jnp.arange(D) // (D // N_DP)
    boost_factor = jnp.where(row_owner[:, None] == feature_block[None, :], 3.0, 1.0)
    centers = jnp.take(axes_table, labels, axis=0)
    drawn_rows = strength * centers + jnp.sqrt(1.0 - strength * strength) * noise_part * boost_factor
    return drawn_rows.astype(jnp.bfloat16)


def draw_centroids(key, part):
    axes_table = cluster_axes(key)
    key = jax.random.fold_in(key, 23)
    label_key, strength_key, noise_key = jax.random.split(key, 3)
    labels = jax.random.randint(label_key, (CENTROIDS,), 0, 8)
    strength = jax.random.uniform(strength_key, (CENTROIDS, 1), jnp.float32, 0.3, 0.9)
    noise_part = jnp.clip(jax.random.normal(noise_key, (CENTROIDS, D), jnp.float32), -4.0, 4.0)
    centers = jnp.take(axes_table, labels, axis=0)
    drawn_rows = strength * centers + jnp.sqrt(1.0 - strength * strength) * noise_part
    return drawn_rows.astype(jnp.bfloat16)


def setup_inputs(seed: int = 0) -> dict:
    key_list = jax.random.split(jax.random.key(seed), 3)
    return {
        "embeddings": draw_embeddings(jax.random.fold_in(key_list[2], 71), 0),
        "centroids": draw_centroids(jax.random.fold_in(key_list[2], 71), 0),
    }


logit_scale = 40.0

def reference(embeddings, centroids):
    values = embeddings.astype(jnp.float32)
    unit_rows = (values / jnp.sqrt(lax.optimization_barrier(jnp.sum(values * values, axis=1, keepdims=True)) + 1e-06)).astype(jnp.bfloat16)
    cent_vals = centroids.astype(jnp.float32)
    inv_norm = 1.0 / jnp.sqrt(lax.optimization_barrier(jnp.sum(cent_vals * cent_vals, axis=1)) + 1e-06)
    raw_scores = lax.dot_general(unit_rows, centroids, (((1,), (1,)), ((), ())), preferred_element_type=jnp.float32)
    exp_scores = jnp.exp(logit_scale * raw_scores * inv_norm[None, :])
    row_scale = jnp.ones((N_ROWS,), jnp.float32)
    col_scale = jnp.ones((CENTROIDS,), jnp.float32)
    for sweep_index in range(SWEEPS):
        col_total = lax.optimization_barrier(jnp.sum(exp_scores * row_scale[:, None], axis=0))
        col_scale = 1.0 / (CENTROIDS * col_total)
        row_total = lax.optimization_barrier(jnp.sum(exp_scores * col_scale[None, :], axis=1))
        row_scale = 1.0 / (N_ROWS * row_total)
    assign = N_ROWS * exp_scores * row_scale[:, None] * col_scale[None, :]
    cluster_mass = lax.optimization_barrier(jnp.sum(assign, axis=0)) * (CENTROIDS / N_ROWS)
    weights = assign.astype(jnp.bfloat16)
    centroid_sums = lax.dot_general(unit_rows, weights, (((0,), (0,)), ((), ())), preferred_element_type=jnp.float32)
    new_centroids = centroid_sums / jnp.sqrt(lax.optimization_barrier(jnp.sum(centroid_sums * centroid_sums, axis=0, keepdims=True)) + 1e-06)
    return (new_centroids, cluster_mass)
```

```python
import functools

import jax
import jax.numpy as jnp
from jax import lax
from jax.experimental import pallas as pl
from jax.experimental.pallas import tpu as pltpu
from jax.sharding import PartitionSpec as P

SWEEPS = 3
LOGIT_SCALE = 40.0
F32, BF16 = jnp.float32, jnp.bfloat16
MESH = pl.DeviceIdType.MESH
GROUP = 8


def dot(a, b, dims):
    return lax.dot_general(a, b, (dims, ((), ())), preferred_element_type=F32)


def kernel(sizes, emb, cen, out, mass_out, x, ut, ct, e, w, s, cvec, rvec, cpart, col_a, col_b, row_x,
           fin_a, fin_b, sib, ring, sem_in, sib_sem, g_send, g_recv, gs_send, gs_recv, ca_sem, cb_sem, rx_sem,
           fa_sem, fb_sem, sx_send, sx_recv, r_send, r_recv):
    n_dp, n_proto, rows, feat, cent = sizes
    nz = n_dp // 2
    half = nz // 2
    own = feat // n_dp
    n_rows = rows * n_dp
    n_cent = cent * n_proto
    levels = n_dp // GROUP
    lanes = 128

    d = lax.axis_index("dp")
    p = lax.axis_index("proto")
    z, c = d // 2, d % 2
    other = d + 1 - 2 * c
    right = ((z + 1) % nz) * 2 + c
    left = ((z + nz - 1) % nz) * 2 + c
    base = (d // GROUP) * GROUP

    def in_group(j):
        return base + (d - base + j) % GROUP

    def in_level(j):
        return (d + GROUP * j) % n_dp

    barrier = pltpu.get_barrier_semaphore()
    for j in range(1, GROUP):
        pl.semaphore_signal(barrier, inc=1, device_id={"dp": in_group(j)}, device_id_type=MESH)
    for j in range(1, levels):
        pl.semaphore_signal(barrier, inc=1, device_id={"dp": in_level(j)}, device_id_type=MESH)
    for t in (left, right):
        pl.semaphore_signal(barrier, inc=1, device_id={"dp": t}, device_id_type=MESH)

    def greet(j, carry):
        pl.semaphore_signal(barrier, inc=1, device_id={"proto": (p + j) % n_proto}, device_id_type=MESH)
        return carry

    lax.fori_loop(1, n_proto, greet, 0)

    load = pltpu.make_async_copy(emb, x, sem_in)
    load.start()

    def eye(n):
        return (
            lax.broadcasted_iota(jnp.int32, (n, n), 0) == lax.broadcasted_iota(jnp.int32, (n, n), 1)
        ).astype(BF16)

    def block_rows(o, core):
        return pl.ds(pl.multiple_of((o * 2 + core) * own, own), own)

    ct[block_rows(z, c), :] = dot(eye(own), cen[...], ((1,), (1,))).astype(BF16)
    pl.semaphore_wait(barrier, (GROUP - 1) + (levels - 1) + 2 + (n_proto - 1))

    def hop(o, way, step):
        return pltpu.make_async_remote_copy(
            src_ref=ct.at[block_rows(o, c)], dst_ref=ct.at[block_rows(o, c)],
            send_sem=g_send.at[way, step], recv_sem=g_recv.at[way, step],
            device_id={"dp": right if way == 0 else left}, device_id_type=MESH)

    def across(o, slot):
        return pltpu.make_async_remote_copy(
            src_ref=ct.at[block_rows(o, c)], dst_ref=ct.at[block_rows(o, c)],
            send_sem=gs_send.at[slot], recv_sem=gs_recv.at[slot],
            device_id={"dp": other}, device_id_type=MESH)

    sent = []
    for desc in (hop(z, 0, 0), hop(z, 1, 0), across(z, 0)):
        desc.start()
        sent.append(desc)

    load.wait()
    tile = 256
    eye_t = eye(tile)

    def prepare(b):
        at = pl.ds(b * tile, tile)
        v = x[at, :].astype(F32)
        u = (v / jnp.sqrt(jnp.sum(v * v, axis=1, keepdims=True) + 1e-06)).astype(BF16)
        x[at, :] = u
        for f in range(feat // tile):
            ut[pl.ds(f * tile, tile), at] = dot(
                eye_t, u[:, f * tile:(f + 1) * tile], ((1,), (1,))).astype(BF16)

    for step in range(half):
        if step < rows // tile:
            prepare(step)
        for way in (0, 1):
            last = half - 1 if way == 0 else half - 2
            if step > last:
                continue
            o = (z - 1 - step + nz) % nz if way == 0 else (z + 1 + step) % nz
            hop(o, way, step).wait_recv()
            if step < last:
                desc = hop(o, way, step + 1)
                desc.start()
                sent.append(desc)
            desc = across(o, 1 + 2 * step + way)
            desc.start()
            sent.append(desc)
    for slot in range(nz):
        across(z, slot).wait_recv()
    for desc in sent:
        desc.wait_send()

    def square(b, acc):
        v = ct[pl.ds(pl.multiple_of(b * own, own), own), :].astype(F32)
        return acc + jnp.sum((v * v).reshape(own // 8, 8, cent), axis=0)

    squares = jnp.sum(lax.fori_loop(0, n_dp, square, jnp.zeros((8, cent), F32)), axis=0, keepdims=True)
    scale = LOGIT_SCALE * (1.0 / jnp.sqrt(squares + 1e-06))

    m_tile = rows // 4

    def score(b, acc):
        at = pl.ds(pl.multiple_of(b * m_tile, m_tile), m_tile)
        v = jnp.exp(dot(x[at, :], ct[...], ((1,), (0,))) * scale)
        e[at, :] = v
        return acc + jnp.sum(v.reshape(m_tile // 8, 8, cent), axis=0)

    cpart[...] = jnp.sum(lax.fori_loop(0, 4, score, jnp.zeros((8, cent), F32)), axis=0, keepdims=True)

    def exchange(buf, sem, n, target):
        def copy(j):
            return pltpu.make_async_remote_copy(
                src_ref=buf.at[0], dst_ref=buf.at[j], send_sem=sem.at[0], recv_sem=sem.at[1],
                device_id=target(j), device_id_type=MESH)

        def go(j, carry):
            copy(j).start()
            return carry

        lax.fori_loop(1, n, go, 0)
        whole = buf.at[pl.ds(1, n - 1)]
        done = pltpu.make_async_remote_copy(
            src_ref=whole, dst_ref=whole, send_sem=sem.at[0], recv_sem=sem.at[1],
            device_id=target(1), device_id_type=MESH)
        done.wait_recv()
        done.wait_send()

    def total(buf, n, me):
        acc = buf[(me + n) % n]
        for src in range(1, n):
            acc = acc + buf[(me - src + n) % n]
        return acc

    def sum_dp(first, second, first_sem, second_sem):
        exchange(first, first_sem, GROUP, lambda j: {"dp": in_group(j)})
        second[0] = total(first, GROUP, d % GROUP)
        exchange(second, second_sem, levels, lambda j: {"dp": in_level(j)})
        return total(second, levels, d // GROUP)

    lane = lax.broadcasted_iota(jnp.int32, (8, lanes), 1)
    unit = 16

    def sweep(i, carry):
        col_a[i, 0] = cpart[...]
        col_total = sum_dp(col_a.at[i], col_b.at[i], ca_sem.at[i], cb_sem.at[i])
        cv = 1.0 / (n_cent * col_total)
        cvec[...] = cv
        cb = jnp.broadcast_to(cv, (8, cent))
        for h in range(2):
            def row_step(g, acc):
                for k in range(unit):
                    at = pl.multiple_of((h * (rows // 2)) + g * (unit * 8) + k * 8, 8)
                    q = e[pl.ds(at, 8), :] * cb
                    q = functools.reduce(lambda a, b: a + b,
                                         [q[:, t * lanes:(t + 1) * lanes] for t in range(cent // lanes)])
                    acc = jnp.where(lane == g * unit + k, jnp.sum(q, axis=1, keepdims=True), acc)
                return acc

            row_x[i, 0, h] = lax.fori_loop(0, rows // 16 // unit, row_step, jnp.zeros((8, lanes), F32))
        exchange(row_x.at[i], rx_sem.at[i], n_proto, lambda j: {"proto": (p + j) % n_proto})
        rv = 1.0 / (n_rows * total(row_x.at[i], n_proto, p))
        rvec[...] = rv

        acc = jnp.zeros((8, cent), F32)
        for h in range(2):
            def col_step(g, st):
                acc, r = st
                for k in range(unit):
                    at = pl.multiple_of((h * (rows // 2)) + g * (unit * 8) + k * 8, 8)
                    acc = acc + e[pl.ds(at, 8), :] * jnp.broadcast_to(r[:, k:k + 1], (8, cent))
                return acc, pltpu.roll(r, lanes - unit, 1)

            acc, _ = lax.fori_loop(0, rows // 16 // unit, col_step, (acc, rv[h]))
        cpart[...] = jnp.sum(acc, axis=0, keepdims=True)
        return carry

    lax.fori_loop(0, SWEEPS, sweep, 0)

    nc = jnp.broadcast_to(n_rows * cvec[...], (8, cent))
    for h in range(2):
        def weigh(g, r):
            for k in range(0, unit, 2):
                at = pl.multiple_of((h * (rows // 2)) + g * (unit * 8) + k * 8, 16)
                pair = [
                    e[pl.ds(at + 8 * m, 8), :] * jnp.broadcast_to(r[:, k + m:k + m + 1], (8, cent)) * nc
                    for m in range(2)
                ]
                w[pl.ds(at, 16), :] = jnp.concatenate(pair, axis=0).astype(BF16)
            return pltpu.roll(r, lanes - unit, 1)

        lax.fori_loop(0, rows // 16 // unit, weigh, rvec[h])

    def gather_sums(b, carry):
        at = pl.ds(pl.multiple_of(b * m_tile, m_tile), m_tile)
        s[at, :] = dot(ut[at, :], w[...], ((1,), (0,)))
        return carry

    lax.fori_loop(0, 4, gather_sums, 0)

    order = [half]
    for q in range(1, half):
        order += [half - q, half + q]
    order += [0]

    def swap(rel):
        return pltpu.make_async_remote_copy(
            src_ref=s.at[block_rows((z + rel) % nz, 1 - c)], dst_ref=sib.at[rel],
            send_sem=sx_send.at[rel], recv_sem=sx_recv.at[rel],
            device_id={"dp": other}, device_id_type=MESH)

    for rel in order:
        swap(rel).start()

    wide = cent // 2
    flows = [(0, 0, half), (1, 1, half), (0, 1, half - 1), (1, 0, half - 1)]

    def link(way, part, t):
        return pltpu.make_async_remote_copy(
            src_ref=ring.at[way, part, t], dst_ref=ring.at[way, part, t + 1],
            send_sem=r_send.at[way, part, t], recv_sem=r_recv.at[way, part, t],
            device_id={"dp": right if way == 0 else left}, device_id_type=MESH)

    ready = set()
    moves = []
    for t in range(half):
        for way, part, hops in flows:
            if t >= hops:
                continue
            rel = hops - t if way == 0 else nz - (hops - t)
            if rel not in ready:
                swap(rel).wait_recv()
                ready.add(rel)
            cols = pl.ds(part * wide, wide)
            v = s[block_rows((z + rel) % nz, c), cols] + sib[rel, :, cols]
            if t > 0:
                link(way, part, t - 1).wait_recv()
                v = v + ring[way, part, t]
            ring[way, part, t] = v
            desc = link(way, part, t)
            desc.start()
            moves.append(desc)
    swap(0).wait_recv()
    for way, part, hops in flows:
        link(way, part, hops - 1).wait_recv()
    parts = []
    for part in range(2):
        cols = pl.ds(part * wide, wide)
        v = s[block_rows(z, c), cols] + sib[0, :, cols]
        for way, q, hops in flows:
            if q == part:
                v = v + ring[way, q, hops]
        parts.append(v)
    sums = jnp.concatenate(parts, axis=1)

    fin_a[0, :, 0:cent] = cpart[...]
    fin_a[0, :, cent:2 * cent] = jnp.sum(sums * sums, axis=0, keepdims=True)
    tot = sum_dp(fin_a, fin_b, fa_sem, fb_sem)
    mass_out[...] = n_cent * cvec[...] * tot[:, 0:cent]
    out[...] = sums / jnp.sqrt(tot[:, cent:2 * cent] + 1e-06)

    for rel in order:
        swap(rel).wait_send()
    for desc in moves:
        desc.wait_send()


def solution(mesh):
    n_dp, n_proto = mesh.shape["dp"], mesh.shape["proto"]
    nz = n_dp // 2
    half = nz // 2
    levels = n_dp // GROUP

    def per_device(embeddings, centroids):
        rows, feat = embeddings.shape
        cent = centroids.shape[0]
        own = feat // n_dp
        dma, vmem = pltpu.SemaphoreType.DMA, pltpu.VMEM
        new_centroids, mass = pl.pallas_call(
            functools.partial(kernel, (n_dp, n_proto, rows, feat, cent)),
            out_shape=(jax.ShapeDtypeStruct((own, cent), F32), jax.ShapeDtypeStruct((1, cent), F32)),
            in_specs=[pl.BlockSpec(memory_space=pl.ANY), pl.BlockSpec(memory_space=pltpu.VMEM)],
            out_specs=(pl.BlockSpec(memory_space=pltpu.VMEM), pl.BlockSpec(memory_space=pltpu.VMEM)),
            scratch_shapes=[
                vmem((rows, feat), BF16),
                vmem((feat, rows), BF16),
                vmem((feat, cent), BF16),
                vmem((rows, cent), F32),
                vmem((rows, cent), BF16),
                vmem((feat, cent), F32),
                vmem((1, cent), F32),
                vmem((2, 8, 128), F32),
                vmem((1, cent), F32),
                vmem((SWEEPS, GROUP, 1, cent), F32),
                vmem((SWEEPS, levels, 1, cent), F32),
                vmem((SWEEPS, n_proto, 2, 8, 128), F32),
                vmem((GROUP, 1, 2 * cent), F32),
                vmem((levels, 1, 2 * cent), F32),
                vmem((nz, own, cent), F32),
                vmem((2, 2, half + 1, own, cent // 2), F32),
                dma, dma((1,)),
                dma((2, half)), dma((2, half)), dma((nz,)), dma((nz,)),
                dma((SWEEPS, 2)), dma((SWEEPS, 2)), dma((SWEEPS, 2)),
                dma((2,)), dma((2,)),
                dma((nz,)), dma((nz,)),
                dma((2, 2, half)), dma((2, 2, half)),
            ],
            compiler_params=pltpu.CompilerParams(
                collective_id=0, has_side_effects=True, vmem_limit_bytes=56 * 1024 * 1024),
            cost_estimate=pl.CostEstimate(
                flops=4 * rows * feat * cent, bytes_accessed=2 * rows * feat, transcendentals=rows * cent),
        )(embeddings, centroids)
        return new_centroids, mass.reshape(cent)

    return jax.shard_map(
        per_device,
        mesh=mesh,
        in_specs=(P("dp", None), P("proto", "dp")),
        out_specs=(P("dp", "proto"), P("proto")),
        check_vma=False,
    )
```

```python
import functools

import jax
import jax.numpy as jnp
from jax import lax
from jax.experimental import pallas as pl
from jax.experimental.pallas import tpu as pltpu
from jax.sharding import PartitionSpec as P

SWEEPS = 3
LOGIT_SCALE = 40.0
F32, BF16 = jnp.float32, jnp.bfloat16
MESH = pl.DeviceIdType.MESH
GROUP = 8
SUBS = 3
PARTS = 4
UNIT = 16
LANES = 128


def dot(a, b, dims):
    return lax.dot_general(a, b, (dims, ((), ())), preferred_element_type=F32)


def kernel(sizes, emb, cen, out, mass_out, x, ut, ct, e, w, s, col_a, col_b, row_x,
           fin_a, fin_b, sib, ring, sem_in, g_send, g_recv, gs_send, gs_recv, ca_sem, cb_sem, rx_sem,
           fa_sem, fb_sem, sx_send, sx_recv, r_send, r_recv):
    n_dp, n_proto, rows, feat, cent = sizes
    nz = n_dp // 2
    half = nz // 2
    own = feat // n_dp
    n_rows = rows * n_dp
    n_cent = cent * n_proto
    levels = n_dp // GROUP

    d = lax.axis_index("dp")
    p = lax.axis_index("proto")
    z, c = d // 2, d % 2
    other = d + 1 - 2 * c
    right = ((z + 1) % nz) * 2 + c
    left = ((z + nz - 1) % nz) * 2 + c
    in_group = d % GROUP
    level = d // GROUP
    group_ids = [{"dp": level * GROUP + (in_group + j) % GROUP} for j in range(1, GROUP)]
    level_ids = [{"dp": (d + GROUP * j) % n_dp} for j in range(1, levels)]
    proto_ids = [{"proto": (p + j) % n_proto} for j in range(1, n_proto)]

    barrier = pltpu.get_barrier_semaphore()
    partners = [{"dp": left}, {"dp": right}] + group_ids + level_ids + proto_ids
    for t in partners:
        pl.semaphore_signal(barrier, inc=1, device_id=t, device_id_type=MESH)

    load = pltpu.make_async_copy(emb, x, sem_in)
    load.start()

    def block_rows(o, core):
        return pl.ds(pl.multiple_of((o * 2 + core) * own, own), own)

    ct[block_rows(z, c), :] = cen[...]
    pl.semaphore_wait(barrier, len(partners))

    piece = own // SUBS

    def hop(o, way, step, sub):
        at = ct.at[pl.ds(pl.multiple_of((o * 2 + c) * own + sub * piece, piece), piece)]
        return pltpu.make_async_remote_copy(
            src_ref=at, dst_ref=at, send_sem=g_send.at[way, step, sub], recv_sem=g_recv.at[way, step, sub],
            device_id={"dp": right if way == 0 else left}, device_id_type=MESH)

    def across(o, slot):
        at = ct.at[block_rows(o, c)]
        return pltpu.make_async_remote_copy(
            src_ref=at, dst_ref=at, send_sem=gs_send.at[slot], recv_sem=gs_recv.at[slot],
            device_id={"dp": other}, device_id_type=MESH)

    pending = []

    def launch(desc):
        desc.start()
        pending.append(desc)

    for sub in range(SUBS):
        launch(hop(z, 0, 0, sub))
        launch(hop(z, 1, 0, sub))
    launch(across(z, 0))

    def square(o, core):
        v = ct[block_rows(o, core), :].astype(F32)
        return jnp.sum((v * v).reshape(own // 8, 8, cent), axis=0)

    load.wait()
    tile, short = 256, 128
    eye = (
        lax.broadcasted_iota(jnp.int32, (tile, tile), 0) == lax.broadcasted_iota(jnp.int32, (tile, tile), 1)
    ).astype(BF16)

    def prepare(b):
        at = pl.ds(b * short, short)
        v = x[at, :].astype(F32)
        u = (v * (1.0 / jnp.sqrt(jnp.sum(v * v, axis=1, keepdims=True) + 1e-06))).astype(BF16)
        x[at, :] = u
        for f in range(feat // tile):
            ut[pl.ds(f * tile, tile), at] = dot(
                eye, u[:, f * tile:(f + 1) * tile], ((1,), (1,))).astype(BF16)

    squares = square(z, c)
    behind = [(z, 0)]
    unit = 0
    for step in range(half):
        came = []
        for sub in range(SUBS):
            if unit < rows // short:
                prepare(unit)
                unit += 1
            for way in (0, 1):
                last = half - 1 if way == 0 else half - 2
                if step > last:
                    continue
                o = (z - 1 - step + nz) % nz if way == 0 else (z + 1 + step) % nz
                hop(o, way, step, sub).wait_recv()
                if step < last:
                    launch(hop(o, way, step + 1, sub))
                if sub == SUBS - 1:
                    launch(across(o, 1 + 2 * step + way))
                    came.append((o, 1 + 2 * step + way))
        for o, slot in behind:
            across(o, slot).wait_recv()
            squares = squares + square(o, 1 - c)
        for o, slot in came:
            squares = squares + square(o, c)
        behind = came
    for o, slot in behind:
        across(o, slot).wait_recv()
        squares = squares + square(o, 1 - c)

    scale = LOGIT_SCALE * (1.0 / jnp.sqrt(jnp.sum(squares, axis=0, keepdims=True) + 1e-06))
    m_tile = rows // 4

    def score(b, acc):
        at = pl.ds(pl.multiple_of(b * m_tile, m_tile), m_tile)
        v = jnp.exp(dot(x[at, :], ct[...], ((1,), (0,))) * scale)
        e[at, :] = v
        return acc + jnp.sum(v.reshape(m_tile // 8, 8, cent), axis=0)

    acc = lax.fori_loop(0, 4, score, jnp.zeros((8, cent), F32))

    def exchange(buf, sem, me, ids):
        for t in ids:
            pltpu.make_async_remote_copy(
                src_ref=buf.at[me], dst_ref=buf.at[me], send_sem=sem.at[0], recv_sem=sem.at[1],
                device_id=t, device_id_type=MESH).start()
        whole = buf.at[pl.ds(0, len(ids))]
        done = pltpu.make_async_remote_copy(
            src_ref=whole, dst_ref=whole, send_sem=sem.at[0], recv_sem=sem.at[1],
            device_id=ids[0], device_id_type=MESH)
        pending.append(done)
        done.wait_recv()
        return functools.reduce(lambda a, b: a + b, [buf[k] for k in range(len(ids) + 1)])

    def sum_dp(first, second, first_sem, second_sem):
        second[level] = exchange(first, first_sem, in_group, group_ids)
        return exchange(second, second_sem, level, level_ids)

    lane = lax.broadcasted_iota(jnp.int32, (8, LANES), 1)
    tiles = [(0, LANES), (LANES, rows // 8)]

    for i in range(SWEEPS):
        col_a[i, in_group] = jnp.sum(acc, axis=0, keepdims=True)
        cv = 1.0 / (n_cent * sum_dp(col_a.at[i], col_b.at[i], ca_sem.at[i], cb_sem.at[i]))
        cb = jnp.broadcast_to(cv, (8, cent))

        totals = []
        for lo, hi in tiles:
            def row_step(g, t):
                for k in range(UNIT):
                    q = e[pl.ds(pl.multiple_of((lo + g * UNIT + k) * 8, 8), 8), :] * cb
                    q = functools.reduce(
                        lambda a, b: a + b, [q[:, m * LANES:(m + 1) * LANES] for m in range(cent // LANES)])
                    t = jnp.where(lane == g * UNIT + k, jnp.sum(q, axis=1, keepdims=True), t)
                return t

            totals.append(lax.fori_loop(0, (hi - lo) // UNIT, row_step, jnp.zeros((8, LANES), F32)))
        row_x[i, p, 0] = totals[0][0:4]
        row_x[i, p, 1] = totals[0][4:8]
        row_x[i, p, 2] = totals[1][0:4] + pltpu.roll(totals[1], LANES // 2, 1)[4:8]
        rv = 1.0 / (n_rows * exchange(row_x.at[i], rx_sem.at[i], p, proto_ids))
        r0 = jnp.concatenate([rv[0], rv[1]], axis=0)
        r1 = jnp.concatenate([rv[2], pltpu.roll(rv[2], LANES // 2, 1)], axis=0)

        final = i == SWEEPS - 1
        nc = jnp.broadcast_to(n_rows * cv, (8, cent))
        acc = jnp.zeros((8, cent), F32)
        for (lo, hi), r in zip(tiles, (r0, r1)):
            def col_step(g, st):
                a, r = st
                for k in range(0, UNIT, 2):
                    at = pl.multiple_of((lo + g * UNIT + k) * 8, 16)
                    pair = [e[pl.ds(at + 8 * m, 8), :] * jnp.broadcast_to(r[:, k + m:k + m + 1], (8, cent))
                            for m in range(2)]
                    a = a + pair[0] + pair[1]
                    if final:
                        w[pl.ds(at, 16), :] = jnp.concatenate([v * nc for v in pair], axis=0).astype(BF16)
                return a, pltpu.roll(r, LANES - UNIT, 1)

            acc, _ = lax.fori_loop(0, (hi - lo) // UNIT, col_step, (acc, r))

    def swap(rel):
        return pltpu.make_async_remote_copy(
            src_ref=s.at[rel, pl.ds(pl.multiple_of((1 - c) * own, own), own)], dst_ref=sib.at[rel],
            send_sem=sx_send.at[rel], recv_sem=sx_recv.at[rel],
            device_id={"dp": other}, device_id_type=MESH)

    def make_sums(rels):
        u = [ut[pl.ds(pl.multiple_of(((z + rel) % nz) * 2 * own, 2 * own), 2 * own), :] for rel in rels]
        v = dot(jnp.concatenate(u, axis=0) if len(u) > 1 else u[0], w[...], ((1,), (0,)))
        for k, rel in enumerate(rels):
            s[rel] = v[k * 2 * own:(k + 1) * 2 * own]
            launch(swap(rel))

    wide = cent // PARTS
    flows = []
    for hops in (half, half - 1):
        for m in range(PARTS // 2):
            for way in (0, 1):
                first = way == (0 if hops == half else 1)
                flows.append((way, m if first else PARTS // 2 + m, hops))

    def link(way, part, t):
        return pltpu.make_async_remote_copy(
            src_ref=ring.at[way, part, t], dst_ref=ring.at[way, part, t + 1],
            send_sem=r_send.at[way, part, t], recv_sem=r_recv.at[way, part, t],
            device_id={"dp": right if way == 0 else left}, device_id_type=MESH)

    own_rows = pl.ds(pl.multiple_of(c * own, own), own)

    def pair_sum(rel, part):
        cols = pl.ds(part * wide, wide)
        return s[rel, own_rows, cols] + sib[rel, :, cols]

    orders = [[half]] + [[half - q, half + q] for q in range(1, half)] + [[0]]
    for k in range(3):
        make_sums(orders[k])
    ready = set()
    for t in range(half):
        for way, part, hops in flows:
            if t >= hops:
                continue
            rel = hops - t if way == 0 else nz - (hops - t)
            if rel not in ready:
                swap(rel).wait_recv()
                ready.add(rel)
            v = pair_sum(rel, part)
            if t > 0:
                link(way, part, t - 1).wait_recv()
                v = v + ring[way, part, t]
            ring[way, part, t] = v
            launch(link(way, part, t))
        if t + 3 < len(orders):
            make_sums(orders[t + 3])
    swap(0).wait_recv()
    for way, part, hops in flows:
        link(way, part, hops - 1).wait_recv()
    parts = []
    for part in range(PARTS):
        v = pair_sum(0, part)
        for way, q, hops in flows:
            if q == part:
                v = v + ring[way, q, hops]
        parts.append(v)
    sums = jnp.concatenate(parts, axis=1)

    fin_a[in_group, :, 0:cent] = jnp.sum(acc, axis=0, keepdims=True)
    fin_a[in_group, :, cent:2 * cent] = jnp.sum(sums * sums, axis=0, keepdims=True)
    tot = sum_dp(fin_a, fin_b, fa_sem, fb_sem)
    mass_out[...] = n_cent * cv * tot[:, 0:cent]
    out[...] = sums * (1.0 / jnp.sqrt(tot[:, cent:2 * cent] + 1e-06))

    for desc in pending:
        desc.wait_send()


def hand_over(sums, mass, sums_out, mass_out):
    sums_out[...] = sums[...]
    mass_out[...] = mass[...]


def solution(mesh):
    n_dp, n_proto = mesh.shape["dp"], mesh.shape["proto"]
    nz = n_dp // 2
    half = nz // 2
    levels = n_dp // GROUP

    def per_device(embeddings, centroids):
        rows, feat = embeddings.shape
        cent = centroids.shape[0]
        own = feat // n_dp
        dma, vmem = pltpu.SemaphoreType.DMA, pltpu.VMEM
        whole = pl.BlockSpec(memory_space=pltpu.VMEM)
        shapes = (jax.ShapeDtypeStruct((own, cent), F32), jax.ShapeDtypeStruct((1, cent), F32))
        sums, mass = pl.pallas_call(
            functools.partial(kernel, (n_dp, n_proto, rows, feat, cent)),
            out_shape=shapes,
            in_specs=[pl.BlockSpec(memory_space=pl.ANY), whole],
            out_specs=(whole, whole),
            scratch_shapes=[
                vmem((rows, feat), BF16),
                vmem((feat, rows), BF16),
                vmem((feat, cent), BF16),
                vmem((rows, cent), F32),
                vmem((rows, cent), BF16),
                vmem((nz, 2 * own, cent), F32),
                vmem((SWEEPS, GROUP, 1, cent), F32),
                vmem((SWEEPS, levels, 1, cent), F32),
                vmem((SWEEPS, n_proto, 3, 4, LANES), F32),
                vmem((GROUP, 1, 2 * cent), F32),
                vmem((levels, 1, 2 * cent), F32),
                vmem((nz, own, cent), F32),
                vmem((2, PARTS, half + 1, own, cent // PARTS), F32),
                dma,
                dma((2, half, SUBS)), dma((2, half, SUBS)), dma((nz,)), dma((nz,)),
                dma((SWEEPS, 2)), dma((SWEEPS, 2)), dma((SWEEPS, 2)),
                dma((2,)), dma((2,)),
                dma((nz,)), dma((nz,)),
                dma((2, PARTS, half)), dma((2, PARTS, half)),
            ],
            compiler_params=pltpu.CompilerParams(
                collective_id=0, has_side_effects=True, vmem_limit_bytes=56 * 1024 * 1024),
            cost_estimate=pl.CostEstimate(
                flops=4 * rows * feat * cent, bytes_accessed=2 * rows * feat, transcendentals=rows * cent),
        )(embeddings, centroids.T)
        new_centroids, mass = pl.pallas_call(
            hand_over, out_shape=shapes, in_specs=[whole, whole], out_specs=(whole, whole))(sums, mass)
        return new_centroids, mass.reshape(cent)

    return jax.shard_map(
        per_device,
        mesh=mesh,
        in_specs=(P("dp", None), P("proto", "dp")),
        out_specs=(P("dp", "proto"), P("proto")),
        check_vma=False,
    )
```

```python
import functools

import jax
import jax.numpy as jnp
from jax import lax
from jax.experimental import pallas as pl
from jax.experimental.pallas import tpu as pltpu
from jax.sharding import PartitionSpec as P

SWEEPS = 3
LOGIT_SCALE = 40.0
F32, BF16 = jnp.float32, jnp.bfloat16
MESH = pl.DeviceIdType.MESH
GROUP = 8
SUBS = 3
PARTS = 4
UNIT = 16
LANES = 128


def dot(a, b, dims):
    return lax.dot_general(a, b, (dims, ((), ())), preferred_element_type=F32)


def kernel(sizes, emb, cen, out, mass_out, x, ut, ct, e, w, s, acc, cvec, rvec, col_a, col_b, row_x,
           fin_a, fin_b, sib, ring, sem_in, g_send, g_recv, gs_recv, c_sem, rx_sem, f_sem,
           sx_send, sx_recv, r_send, r_recv):
    n_dp, n_proto, rows, feat, cent = sizes
    nz = n_dp // 2
    half = nz // 2
    own = feat // n_dp
    n_rows = rows * n_dp
    n_cent = cent * n_proto
    levels = n_dp // GROUP

    d = lax.axis_index("dp")
    p = lax.axis_index("proto")
    z, c = d // 2, d % 2
    other = d + 1 - 2 * c
    right = ((z + 1) % nz) * 2 + c
    left = ((z + nz - 1) % nz) * 2 + c
    in_group = d % GROUP
    level = d // GROUP
    group_ids = [{"dp": level * GROUP + (in_group + j) % GROUP} for j in range(1, GROUP)]
    level_ids = [{"dp": (d + GROUP * j) % n_dp} for j in range(1, levels)]
    proto_ids = [{"proto": (p + j) % n_proto} for j in range(1, n_proto)]

    barrier = pltpu.get_barrier_semaphore()
    partners = [{"dp": left}, {"dp": right}] + group_ids + level_ids + proto_ids
    for t in partners:
        pl.semaphore_signal(barrier, inc=1, device_id=t, device_id_type=MESH)

    load = pltpu.make_async_copy(emb, x, sem_in)
    load.start()

    def block_rows(o, core):
        return pl.ds(pl.multiple_of((o * 2 + core) * own, own), own)

    ct[block_rows(z, c), :] = cen[...]
    pl.semaphore_wait(barrier, len(partners))

    piece = own // SUBS

    def hop(o, way, step, sub):
        at = ct.at[pl.ds(pl.multiple_of((o * 2 + c) * own + sub * piece, piece), piece)]
        return pltpu.make_async_remote_copy(
            src_ref=at, dst_ref=at, send_sem=g_send, recv_sem=g_recv.at[way, step, sub],
            device_id={"dp": right if way == 0 else left}, device_id_type=MESH)

    def across(o, slot):
        at = ct.at[block_rows(o, c)]
        return pltpu.make_async_remote_copy(
            src_ref=at, dst_ref=at, send_sem=g_send, recv_sem=gs_recv.at[slot],
            device_id={"dp": other}, device_id_type=MESH)

    def square(o, core):
        v = ct[block_rows(o, core), :].astype(F32)
        acc[...] += jnp.sum((v * v).reshape(own // 8, 8, cent), axis=0)

    def start(step, sub):
        hop(z, 0, 0, sub).start()
        hop(z, 1, 0, sub).start()
        return step

    lax.fori_loop(0, SUBS, lambda sub, carry: start(carry, sub), 0)
    across(z, 0).start()

    acc[...] = jnp.zeros((8, cent), F32)
    square(z, c)
    load.wait()
    tile, short, thin = 256, 128, 32
    eye = (
        lax.broadcasted_iota(jnp.int32, (tile, tile), 0) == lax.broadcasted_iota(jnp.int32, (tile, tile), 1)
    ).astype(BF16)

    def prepare(b):
        def norm(k, carry):
            at = pl.ds(pl.multiple_of(b * short + k * thin, thin), thin)
            v = x[at, :].astype(F32)
            x[at, :] = (v * (1.0 / jnp.sqrt(jnp.sum(v * v, axis=1, keepdims=True) + 1e-06))).astype(BF16)
            return carry

        lax.fori_loop(0, short // thin, norm, 0)
        at = pl.ds(pl.multiple_of(b * short, short), short)

        def turn(f, carry):
            cols = pl.ds(pl.multiple_of(f * tile, tile), tile)
            ut[cols, at] = dot(eye, x[at, cols], ((1,), (1,))).astype(BF16)
            return carry

        lax.fori_loop(0, feat // tile, turn, 0)

    def gather_step(step, carry):
        o_right = (z - 1 - step + nz) % nz
        o_left = (z + 1 + step) % nz

        def gather_piece(sub, carry):
            unit = step * SUBS + sub

            @pl.when(unit < rows // short)
            def _():
                prepare(unit)

            hop(o_right, 0, step, sub).wait_recv()

            @pl.when(step < half - 1)
            def _():
                hop(o_right, 0, step + 1, sub).start()
                hop(o_left, 1, step, sub).wait_recv()

            @pl.when(step < half - 2)
            def _():
                hop(o_left, 1, step + 1, sub).start()

            return carry

        lax.fori_loop(0, SUBS, gather_piece, 0)
        across(o_right, 1 + 2 * step).start()
        square(o_right, c)

        @pl.when(step < half - 1)
        def _():
            across(o_left, 2 + 2 * step).start()
            square(o_left, c)

        @pl.when(step == 0)
        def _():
            across(z, 0).wait_recv()
            square(z, 1 - c)

        @pl.when(step > 0)
        def _():
            across(o_right, 2 * step - 1).wait_recv()
            across(o_left, 2 * step).wait_recv()
            square((o_right + 1) % nz, 1 - c)
            square((o_left + nz - 1) % nz, 1 - c)

        return carry

    lax.fori_loop(0, half, gather_step, 0)
    across(z, nz - 1).wait_recv()
    square((z + half) % nz, 1 - c)

    scale = LOGIT_SCALE * (1.0 / jnp.sqrt(jnp.sum(acc[...], axis=0, keepdims=True) + 1e-06))
    m_tile = rows // 4

    def score(b, total):
        at = pl.ds(pl.multiple_of(b * m_tile, m_tile), m_tile)
        v = jnp.exp(dot(x[at, :], ct[...], ((1,), (0,))) * scale)
        e[at, :] = v
        return total + jnp.sum(v.reshape(m_tile // 8, 8, cent), axis=0)

    acc[...] = lax.fori_loop(0, 4, score, jnp.zeros((8, cent), F32))

    def exchange(buf, send, recv, me, ids):
        for t in ids:
            pltpu.make_async_remote_copy(
                src_ref=buf.at[me], dst_ref=buf.at[me], send_sem=send, recv_sem=recv,
                device_id=t, device_id_type=MESH).start()
        whole = buf.at[pl.ds(0, len(ids))]
        done = pltpu.make_async_remote_copy(
            src_ref=whole, dst_ref=whole, send_sem=send, recv_sem=recv,
            device_id=ids[0], device_id_type=MESH)
        done.wait_recv()
        return functools.reduce(lambda a, b: a + b, [buf[k] for k in range(len(ids) + 1)]), done

    def sum_dp(first, second, sem):
        second[level], sent_first = exchange(first, sem.at[0], sem.at[1], in_group, group_ids)
        result, sent_second = exchange(second, sem.at[2], sem.at[3], level, level_ids)
        return result, (sent_first, sent_second)

    lane = lax.broadcasted_iota(jnp.int32, (8, LANES), 1)
    tiles = [(0, LANES), (LANES, rows // 8)]

    def column_pass(scaled):
        total = jnp.zeros((8, cent), F32)
        for m, (lo, hi) in enumerate(tiles):
            def col_step(g, st):
                a, r = st
                for k in range(0, UNIT, 2):
                    at = pl.multiple_of((lo + g * UNIT + k) * 8, 16)
                    pair = [e[pl.ds(at + 8 * m, 8), :] * jnp.broadcast_to(r[:, k + m:k + m + 1], (8, cent))
                            for m in range(2)]
                    a = a + pair[0] + pair[1]
                    if scaled is not None:
                        w[pl.ds(at, 16), :] = jnp.concatenate([v * scaled for v in pair], axis=0).astype(BF16)
                return a, pltpu.roll(r, LANES - UNIT, 1)

            total, _ = lax.fori_loop(0, (hi - lo) // UNIT, col_step, (total, rvec[m]))
        acc[...] = total

    def sweep(i, carry):
        col_a[i, in_group] = jnp.sum(acc[...], axis=0, keepdims=True)
        col_total, sent = sum_dp(col_a.at[i], col_b.at[i], c_sem.at[i])
        cv = 1.0 / (n_cent * col_total)
        cvec[...] = cv
        cb = jnp.broadcast_to(cv, (8, cent))

        totals = []
        for lo, hi in tiles:
            def row_step(g, t):
                for k in range(UNIT):
                    q = e[pl.ds(pl.multiple_of((lo + g * UNIT + k) * 8, 8), 8), :] * cb
                    q = functools.reduce(
                        lambda a, b: a + b, [q[:, m * LANES:(m + 1) * LANES] for m in range(cent // LANES)])
                    t = jnp.where(lane == g * UNIT + k, jnp.sum(q, axis=1, keepdims=True), t)
                return t

            totals.append(lax.fori_loop(0, (hi - lo) // UNIT, row_step, jnp.zeros((8, LANES), F32)))
        row_x[i, p, 0] = totals[0][0:4]
        row_x[i, p, 1] = totals[0][4:8]
        row_x[i, p, 2] = totals[1][0:4] + pltpu.roll(totals[1], LANES // 2, 1)[4:8]
        row_total, sent_row = exchange(row_x.at[i], rx_sem.at[i, 0], rx_sem.at[i, 1], p, proto_ids)
        rv = 1.0 / (n_rows * row_total)
        rvec[0] = jnp.concatenate([rv[0], rv[1]], axis=0)
        rvec[1] = jnp.concatenate([rv[2], pltpu.roll(rv[2], LANES // 2, 1)], axis=0)

        @pl.when(i < SWEEPS - 1)
        def _():
            column_pass(None)

        for desc in sent + (sent_row,):
            desc.wait_send()
        return carry

    lax.fori_loop(0, SWEEPS, sweep, 0)
    column_pass(jnp.broadcast_to(n_rows * cvec[...], (8, cent)))

    def swap(rel):
        return pltpu.make_async_remote_copy(
            src_ref=s.at[rel, pl.ds(pl.multiple_of((1 - c) * own, own), own)], dst_ref=sib.at[rel],
            send_sem=sx_send, recv_sem=sx_recv.at[rel],
            device_id={"dp": other}, device_id_type=MESH)

    def make_sums(q):
        rels = (half - q, lax.select(q == 0, 0, half + q))
        u = [ut[pl.ds(pl.multiple_of(((z + rel) % nz) * 2 * own, 2 * own), 2 * own), :] for rel in rels]
        v = dot(jnp.concatenate(u, axis=0), w[...], ((1,), (0,)))
        for k, rel in enumerate(rels):
            s[rel] = v[k * 2 * own:(k + 1) * 2 * own]
            swap(rel).start()

    wide = cent // PARTS
    flows = []
    for hops in (half, half - 1):
        for m in range(PARTS // 2):
            for way in (0, 1):
                first = way == (0 if hops == half else 1)
                flows.append((way, m if first else PARTS // 2 + m, hops))

    def link(way, part, t):
        return pltpu.make_async_remote_copy(
            src_ref=ring.at[way, part, t], dst_ref=ring.at[way, part, t + 1],
            send_sem=r_send, recv_sem=r_recv.at[way, part, t],
            device_id={"dp": right if way == 0 else left}, device_id_type=MESH)

    own_rows = pl.ds(pl.multiple_of(c * own, own), own)

    def pair_sum(rel, part):
        cols = pl.ds(part * wide, wide)
        return s[rel, own_rows, cols] + sib[rel, :, cols]

    def flow(way, part, hops, t):
        rel = hops - t if way == 0 else nz - hops + t

        @pl.when(t == 0)
        def _():
            ring[way, part, 0] = pair_sum(rel, part)

        @pl.when(t > 0)
        def _():
            link(way, part, t - 1).wait_recv()
            ring[way, part, t] = pair_sum(rel, part) + ring[way, part, t]

        link(way, part, t).start()

    ahead = 3

    def ring_step(k, carry):
        t = k - ahead

        @pl.when(t == 0)
        def _():
            swap(half).wait_recv()

        @pl.when(t >= 0)
        def _():
            for way, part, hops in flows:
                if hops == half:
                    flow(way, part, hops, t)

        @pl.when((t >= 0) & (t < half - 1))
        def _():
            swap(half - 1 - t).wait_recv()
            swap(half + 1 + t).wait_recv()
            for way, part, hops in flows:
                if hops < half:
                    flow(way, part, hops, t)

        @pl.when(k < half)
        def _():
            make_sums(k)

        return carry

    lax.fori_loop(0, half + ahead, ring_step, 0)
    swap(0).wait_recv()
    for way, part, hops in flows:
        link(way, part, hops - 1).wait_recv()
    parts = []
    for part in range(PARTS):
        v = pair_sum(0, part)
        for way, q, hops in flows:
            if q == part:
                v = v + ring[way, q, hops]
        parts.append(v)
    sums = jnp.concatenate(parts, axis=1)

    fin_a[in_group, :, 0:cent] = jnp.sum(acc[...], axis=0, keepdims=True)
    fin_a[in_group, :, cent:2 * cent] = jnp.sum(sums * sums, axis=0, keepdims=True)
    tot, sent = sum_dp(fin_a, fin_b, f_sem)
    mass_out[...] = n_cent * cvec[...] * tot[:, 0:cent]
    out[...] = sums * (1.0 / jnp.sqrt(tot[:, cent:2 * cent] + 1e-06))

    for desc in sent:
        desc.wait_send()
    for ref, sem in ((ct.at[pl.ds(0, (2 * nz - 1) * own)], g_send), (sib, sx_send), (sib.at[pl.ds(0, nz - 1)], r_send)):
        pltpu.make_async_remote_copy(
            src_ref=ref, dst_ref=ref, send_sem=sem, recv_sem=sem,
            device_id={"dp": other}, device_id_type=MESH).wait_send()


def hand_over(sums, mass, sums_out, mass_out):
    sums_out[...] = sums[...]
    mass_out[...] = mass[...]


def solution(mesh):
    n_dp, n_proto = mesh.shape["dp"], mesh.shape["proto"]
    nz = n_dp // 2
    half = nz // 2
    levels = n_dp // GROUP

    def per_device(embeddings, centroids):
        rows, feat = embeddings.shape
        cent = centroids.shape[0]
        own = feat // n_dp
        dma, vmem = pltpu.SemaphoreType.DMA, pltpu.VMEM
        whole = pl.BlockSpec(memory_space=pltpu.VMEM)
        shapes = (jax.ShapeDtypeStruct((own, cent), F32), jax.ShapeDtypeStruct((1, cent), F32))
        sums, mass = pl.pallas_call(
            functools.partial(kernel, (n_dp, n_proto, rows, feat, cent)),
            out_shape=shapes,
            in_specs=[pl.BlockSpec(memory_space=pl.ANY), whole],
            out_specs=(whole, whole),
            scratch_shapes=[
                vmem((rows, feat), BF16),
                vmem((feat, rows), BF16),
                vmem((feat, cent), BF16),
                vmem((rows, cent), F32),
                vmem((rows, cent), BF16),
                vmem((nz, 2 * own, cent), F32),
                vmem((8, cent), F32),
                vmem((1, cent), F32),
                vmem((2, 8, LANES), F32),
                vmem((SWEEPS, GROUP, 1, cent), F32),
                vmem((SWEEPS, levels, 1, cent), F32),
                vmem((SWEEPS, n_proto, 3, 4, LANES), F32),
                vmem((GROUP, 1, 2 * cent), F32),
                vmem((levels, 1, 2 * cent), F32),
                vmem((nz, own, cent), F32),
                vmem((2, PARTS, half + 1, own, cent // PARTS), F32),
                dma, dma, dma((2, half, SUBS)), dma((nz,)),
                dma((SWEEPS, 4)), dma((SWEEPS, 2)), dma((4,)),
                dma, dma((nz,)), dma, dma((2, PARTS, half)),
            ],
            compiler_params=pltpu.CompilerParams(
                collective_id=0, has_side_effects=True, vmem_limit_bytes=56 * 1024 * 1024),
            cost_estimate=pl.CostEstimate(
                flops=4 * rows * feat * cent, bytes_accessed=2 * rows * feat, transcendentals=rows * cent),
        )(embeddings, centroids.T)
        new_centroids, mass = pl.pallas_call(
            hand_over, out_shape=shapes, in_specs=[whole, whole], out_specs=(whole, whole))(sums, mass)
        return new_centroids, mass.reshape(cent)

    return jax.shard_map(
        per_device,
        mesh=mesh,
        in_specs=(P("dp", None), P("proto", "dp")),
        out_specs=(P("dp", "proto"), P("proto")),
        check_vma=False,
    )
```

```python
import functools

import jax
import jax.numpy as jnp
from jax import lax
from jax.experimental import pallas as pl
from jax.experimental.pallas import tpu as pltpu
from jax.sharding import PartitionSpec as P

SWEEPS = 3
LOGIT_SCALE = 40.0
F32, BF16 = jnp.float32, jnp.bfloat16
MESH = pl.DeviceIdType.MESH
GROUP = 8
SUBS = 3
PARTS = 4
UNIT = 32
LANES = 128


def dot(a, b, dims):
    return lax.dot_general(a, b, (dims, ((), ())), preferred_element_type=F32)


def kernel(sizes, emb, cen, out, mass_out, x, ut, ct, e, w, s, col_a, col_b, row_x, row_y,
           fin_a, fin_b, sib, ring, sem_in, g_send, g_recv, gs_send, gs_recv, ca_sem, cb_sem, rx_sem, ry_sem,
           fa_sem, fb_sem, sx_send, sx_recv, r_send, r_recv):
    n_dp, n_proto, rows, feat, cent = sizes
    nz = n_dp // 2
    half = nz // 2
    own = feat // n_dp
    n_rows = rows * n_dp
    n_cent = cent * n_proto
    levels = n_dp // GROUP
    side = int(n_proto**0.5)

    d = lax.axis_index("dp")
    p = lax.axis_index("proto")
    z, c = d // 2, d % 2
    other = d + 1 - 2 * c
    right = ((z + 1) % nz) * 2 + c
    left = ((z + nz - 1) % nz) * 2 + c
    in_group = d % GROUP
    level = d // GROUP
    group_ids = [{"dp": level * GROUP + (in_group + j) % GROUP} for j in range(1, GROUP)]
    level_ids = [{"dp": (d + GROUP * j) % n_dp} for j in range(1, levels)]
    px, py = p // side, p % side
    x_ids = [{"proto": (p + side * j) % n_proto} for j in range(1, side)]
    y_ids = [{"proto": px * side + (py + j) % side} for j in range(1, side)]

    barrier = pltpu.get_barrier_semaphore()
    partners = [{"dp": left}, {"dp": right}] + group_ids + level_ids + x_ids + y_ids
    for t in partners:
        pl.semaphore_signal(barrier, inc=1, device_id=t, device_id_type=MESH)

    load = pltpu.make_async_copy(emb, x, sem_in)
    load.start()

    def block_rows(o, core):
        return pl.ds(pl.multiple_of((o * 2 + core) * own, own), own)

    ct[block_rows(z, c), :] = cen[...]
    pl.semaphore_wait(barrier, len(partners))

    piece = own // SUBS

    def hop(o, way, step, sub):
        at = ct.at[pl.ds(pl.multiple_of((o * 2 + c) * own + sub * piece, piece), piece)]
        return pltpu.make_async_remote_copy(
            src_ref=at, dst_ref=at, send_sem=g_send.at[way, step, sub], recv_sem=g_recv.at[way, step, sub],
            device_id={"dp": right if way == 0 else left}, device_id_type=MESH)

    def across(o, slot):
        at = ct.at[block_rows(o, c)]
        return pltpu.make_async_remote_copy(
            src_ref=at, dst_ref=at, send_sem=gs_send.at[slot], recv_sem=gs_recv.at[slot],
            device_id={"dp": other}, device_id_type=MESH)

    pending = []

    def launch(desc):
        desc.start()
        pending.append(desc)

    for sub in range(SUBS):
        launch(hop(z, 0, 0, sub))
        launch(hop(z, 1, 0, sub))
    launch(across(z, 0))

    def square(o, core):
        v = ct[block_rows(o, core), :].astype(F32)
        return jnp.sum((v * v).reshape(own // 8, 8, cent), axis=0)

    load.wait()
    tile, short = 256, 128
    eye = (
        lax.broadcasted_iota(jnp.int32, (tile, tile), 0) == lax.broadcasted_iota(jnp.int32, (tile, tile), 1)
    ).astype(BF16)

    def prepare(b):
        at = pl.ds(b * short, short)
        v = x[at, :].astype(F32)
        u = (v * (1.0 / jnp.sqrt(jnp.sum(v * v, axis=1, keepdims=True) + 1e-06))).astype(BF16)
        x[at, :] = u

    def turn(b):
        at = pl.ds(b * short, short)
        for f in range(feat // tile):
            ut[pl.ds(f * tile, tile), at] = dot(
                eye, x[at, f * tile:(f + 1) * tile], ((1,), (1,))).astype(BF16)

    squares = square(z, c)
    behind = [(z, 0)]
    unit = 0
    for step in range(half):
        came = []
        for sub in range(SUBS):
            if unit < rows // short:
                prepare(unit)
                unit += 1
            for way in (0, 1):
                last = half - 1 if way == 0 else half - 2
                if step > last:
                    continue
                o = (z - 1 - step + nz) % nz if way == 0 else (z + 1 + step) % nz
                hop(o, way, step, sub).wait_recv()
                if step < last:
                    launch(hop(o, way, step + 1, sub))
                if sub == SUBS - 1:
                    launch(across(o, 1 + 2 * step + way))
                    came.append((o, 1 + 2 * step + way))
        for o, slot in behind:
            across(o, slot).wait_recv()
            squares = squares + square(o, 1 - c)
        for o, slot in came:
            squares = squares + square(o, c)
        behind = came
    for o, slot in behind:
        across(o, slot).wait_recv()
        squares = squares + square(o, 1 - c)

    scale = LOGIT_SCALE * (1.0 / jnp.sqrt(jnp.sum(squares, axis=0, keepdims=True) + 1e-06))
    m_tile = rows // 4

    def score(b, acc):
        at = pl.ds(pl.multiple_of(b * m_tile, m_tile), m_tile)
        v = jnp.exp(dot(x[at, :], ct[...], ((1,), (0,))) * scale)
        e[at, :] = v
        return acc + jnp.sum(v.reshape(m_tile // 8, 8, cent), axis=0)

    acc = lax.fori_loop(0, 4, score, jnp.zeros((8, cent), F32))

    def exchange(buf, sem, me, ids, units=()):
        for t in ids:
            pltpu.make_async_remote_copy(
                src_ref=buf.at[me], dst_ref=buf.at[me], send_sem=sem.at[0], recv_sem=sem.at[1],
                device_id=t, device_id_type=MESH).start()
        whole = buf.at[pl.ds(0, len(ids))]
        done = pltpu.make_async_remote_copy(
            src_ref=whole, dst_ref=whole, send_sem=sem.at[0], recv_sem=sem.at[1],
            device_id=ids[0], device_id_type=MESH)
        pending.append(done)
        for b in units:
            turn(b)
        done.wait_recv()
        return functools.reduce(lambda a, b: a + b, [buf[k] for k in range(len(ids) + 1)])

    def sum_dp(first, second, first_sem, second_sem, units=((), ())):
        second[level] = exchange(first, first_sem, in_group, group_ids, units[0])
        return exchange(second, second_sem, level, level_ids, units[1])

    lane = lax.broadcasted_iota(jnp.int32, (8, LANES), 1)
    tiles = [(0, LANES), (LANES, rows // 8)]

    per_sweep = rows // short // SWEEPS
    for i in range(SWEEPS):
        turns = range(i * per_sweep, (i + 1) * per_sweep)
        col_a[i, in_group] = jnp.sum(acc, axis=0, keepdims=True)
        cv = 1.0 / (n_cent * sum_dp(
            col_a.at[i], col_b.at[i], ca_sem.at[i], cb_sem.at[i], (turns[0:1], turns[1:2])))
        cb = jnp.broadcast_to(cv, (8, cent))

        totals = []
        for lo, hi in tiles:
            def row_step(g, t):
                for k in range(UNIT):
                    q = e[pl.ds(pl.multiple_of((lo + g * UNIT + k) * 8, 8), 8), :] * cb
                    q = functools.reduce(
                        lambda a, b: a + b, [q[:, m * LANES:(m + 1) * LANES] for m in range(cent // LANES)])
                    t = jnp.where(lane == g * UNIT + k, jnp.sum(q, axis=1, keepdims=True), t)
                return t

            totals.append(lax.fori_loop(0, (hi - lo) // UNIT, row_step, jnp.zeros((8, LANES), F32)))
        row_x[i, px, 0] = totals[0][0:4]
        row_x[i, px, 1] = totals[0][4:8]
        row_x[i, px, 2] = totals[1][0:4] + pltpu.roll(totals[1], LANES // 2, 1)[4:8]
        row_y[i, py] = exchange(row_x.at[i], rx_sem.at[i], px, x_ids, turns[2:3])
        rv = 1.0 / (n_rows * exchange(row_y.at[i], ry_sem.at[i], py, y_ids, turns[3:]))
        r0 = jnp.concatenate([rv[0], rv[1]], axis=0)
        r1 = jnp.concatenate([rv[2], pltpu.roll(rv[2], LANES // 2, 1)], axis=0)

        final = i == SWEEPS - 1
        nc = jnp.broadcast_to(n_rows * cv, (8, cent))
        acc = jnp.zeros((8, cent), F32)
        for (lo, hi), r in zip(tiles, (r0, r1)):
            def col_step(g, st):
                a, r = st
                for k in range(0, UNIT, 2):
                    at = pl.multiple_of((lo + g * UNIT + k) * 8, 16)
                    pair = [e[pl.ds(at + 8 * m, 8), :] * jnp.broadcast_to(r[:, k + m:k + m + 1], (8, cent))
                            for m in range(2)]
                    a = a + pair[0] + pair[1]
                    if final:
                        w[pl.ds(at, 16), :] = jnp.concatenate([v * nc for v in pair], axis=0).astype(BF16)
                return a, pltpu.roll(r, LANES - UNIT, 1)

            acc, _ = lax.fori_loop(0, (hi - lo) // UNIT, col_step, (acc, r))

    def swap(rel):
        return pltpu.make_async_remote_copy(
            src_ref=s.at[rel, pl.ds(pl.multiple_of((1 - c) * own, own), own)], dst_ref=sib.at[rel],
            send_sem=sx_send.at[rel], recv_sem=sx_recv.at[rel],
            device_id={"dp": other}, device_id_type=MESH)

    def make_sums(rels):
        u = [ut[pl.ds(pl.multiple_of(((z + rel) % nz) * 2 * own, 2 * own), 2 * own), :] for rel in rels]
        v = dot(jnp.concatenate(u, axis=0) if len(u) > 1 else u[0], w[...], ((1,), (0,)))
        for k, rel in enumerate(rels):
            s[rel] = v[k * 2 * own:(k + 1) * 2 * own]
            launch(swap(rel))

    wide = cent // PARTS
    flows = []
    for hops in (half, half - 1):
        for m in range(PARTS // 2):
            for way in (0, 1):
                first = way == (0 if hops == half else 1)
                flows.append((way, m if first else PARTS // 2 + m, hops))

    def link(way, part, t):
        return pltpu.make_async_remote_copy(
            src_ref=ring.at[way, part, t], dst_ref=ring.at[way, part, t + 1],
            send_sem=r_send.at[way, part, t], recv_sem=r_recv.at[way, part, t],
            device_id={"dp": right if way == 0 else left}, device_id_type=MESH)

    own_rows = pl.ds(pl.multiple_of(c * own, own), own)

    def pair_sum(rel, part):
        cols = pl.ds(part * wide, wide)
        return s[rel, own_rows, cols] + sib[rel, :, cols]

    orders = [[half]] + [[half - q, half + q] for q in range(1, half)] + [[0]]
    for k in range(3):
        make_sums(orders[k])
    ready = set()
    for t in range(half):
        for way, part, hops in flows:
            if t >= hops:
                continue
            rel = hops - t if way == 0 else nz - (hops - t)
            if rel not in ready:
                swap(rel).wait_recv()
                ready.add(rel)
            v = pair_sum(rel, part)
            if t > 0:
                link(way, part, t - 1).wait_recv()
                v = v + ring[way, part, t]
            ring[way, part, t] = v
            launch(link(way, part, t))
        if t + 3 < len(orders):
            make_sums(orders[t + 3])
    swap(0).wait_recv()
    for way, part, hops in flows:
        link(way, part, hops - 1).wait_recv()
    parts = []
    for part in range(PARTS):
        v = pair_sum(0, part)
        for way, q, hops in flows:
            if q == part:
                v = v + ring[way, q, hops]
        parts.append(v)
    sums = jnp.concatenate(parts, axis=1)

    fin_a[in_group, :, 0:cent] = jnp.sum(acc, axis=0, keepdims=True)
    fin_a[in_group, :, cent:2 * cent] = jnp.sum(sums * sums, axis=0, keepdims=True)
    tot = sum_dp(fin_a, fin_b, fa_sem, fb_sem)
    mass_out[...] = n_cent * cv * tot[:, 0:cent]
    out[...] = sums * (1.0 / jnp.sqrt(tot[:, cent:2 * cent] + 1e-06))

    for desc in pending:
        desc.wait_send()


def hand_over(sums, mass, sums_out, mass_out):
    sums_out[...] = sums[...]
    mass_out[...] = mass[...]


def solution(mesh):
    n_dp, n_proto = mesh.shape["dp"], mesh.shape["proto"]
    nz = n_dp // 2
    half = nz // 2
    levels = n_dp // GROUP
    side = int(n_proto**0.5)

    def per_device(embeddings, centroids):
        rows, feat = embeddings.shape
        cent = centroids.shape[0]
        own = feat // n_dp
        dma, vmem = pltpu.SemaphoreType.DMA, pltpu.VMEM
        whole = pl.BlockSpec(memory_space=pltpu.VMEM)
        shapes = (jax.ShapeDtypeStruct((own, cent), F32), jax.ShapeDtypeStruct((1, cent), F32))
        sums, mass = pl.pallas_call(
            functools.partial(kernel, (n_dp, n_proto, rows, feat, cent)),
            out_shape=shapes,
            in_specs=[pl.BlockSpec(memory_space=pl.ANY), whole],
            out_specs=(whole, whole),
            scratch_shapes=[
                vmem((rows, feat), BF16),
                vmem((feat, rows), BF16),
                vmem((feat, cent), BF16),
                vmem((rows, cent), F32),
                vmem((rows, cent), BF16),
                vmem((nz, 2 * own, cent), F32),
                vmem((SWEEPS, GROUP, 1, cent), F32),
                vmem((SWEEPS, levels, 1, cent), F32),
                vmem((SWEEPS, side, 3, 4, LANES), F32),
                vmem((SWEEPS, side, 3, 4, LANES), F32),
                vmem((GROUP, 1, 2 * cent), F32),
                vmem((levels, 1, 2 * cent), F32),
                vmem((nz, own, cent), F32),
                vmem((2, PARTS, half + 1, own, cent // PARTS), F32),
                dma,
                dma((2, half, SUBS)), dma((2, half, SUBS)), dma((nz,)), dma((nz,)),
                dma((SWEEPS, 2)), dma((SWEEPS, 2)), dma((SWEEPS, 2)), dma((SWEEPS, 2)),
                dma((2,)), dma((2,)),
                dma((nz,)), dma((nz,)),
                dma((2, PARTS, half)), dma((2, PARTS, half)),
            ],
            compiler_params=pltpu.CompilerParams(
                collective_id=0, has_side_effects=True, vmem_limit_bytes=56 * 1024 * 1024),
            cost_estimate=pl.CostEstimate(
                flops=4 * rows * feat * cent, bytes_accessed=2 * rows * feat, transcendentals=rows * cent),
        )(embeddings, centroids.T)
        new_centroids, mass = pl.pallas_call(
            hand_over, out_shape=shapes, in_specs=[whole, whole], out_specs=(whole, whole))(sums, mass)
        return new_centroids, mass.reshape(cent)

    return jax.shard_map(
        per_device,
        mesh=mesh,
        in_specs=(P("dp", None), P("proto", "dp")),
        out_specs=(P("dp", "proto"), P("proto")),
        check_vma=False,
    )
```

```python
import functools

import jax
import jax.numpy as jnp
from jax import lax
from jax.experimental import pallas as pl
from jax.experimental.pallas import tpu as pltpu
from jax.sharding import PartitionSpec as P

SWEEPS = 3
LOGIT_SCALE = 40.0
F32, BF16 = jnp.float32, jnp.bfloat16
MESH = pl.DeviceIdType.MESH
GROUP = 8
SUBS = 3
PARTS = 4
UNIT = 32
LANES = 128


def dot(a, b, dims):
    return lax.dot_general(a, b, (dims, ((), ())), preferred_element_type=F32)


def kernel(sizes, emb, cen, out, mass_out, x, ut, ct, e, w, s, col_a, col_b, row_x,
           fin_a, fin_b, sib, ring, sem_in, g_send, g_recv, gs_send, gs_recv, ca_sem, cb_sem, rx_sem,
           fa_sem, fb_sem, sx_send, sx_recv, r_send, r_recv):
    n_dp, n_proto, rows, feat, cent = sizes
    nz = n_dp // 2
    half = nz // 2
    own = feat // n_dp
    n_rows = rows * n_dp
    n_cent = cent * n_proto
    levels = n_dp // GROUP

    d = lax.axis_index("dp")
    p = lax.axis_index("proto")
    z, c = d // 2, d % 2
    other = d + 1 - 2 * c
    right = ((z + 1) % nz) * 2 + c
    left = ((z + nz - 1) % nz) * 2 + c
    near = (right, left)
    far = ((d + 4) % n_dp, (d + n_dp - 4) % n_dp)
    in_group = d % GROUP
    level = d // GROUP
    group_ids = [{"dp": level * GROUP + (in_group + j) % GROUP} for j in range(1, GROUP)]
    level_ids = [{"dp": (d + GROUP * j) % n_dp} for j in range(1, levels)]
    proto_ids = [{"proto": (p + j) % n_proto} for j in range(1, n_proto)]

    barrier = pltpu.get_barrier_semaphore()
    partners = [{"dp": t} for t in far + near] + group_ids + level_ids + proto_ids
    for t in partners:
        pl.semaphore_signal(barrier, inc=1, device_id=t, device_id_type=MESH)

    load = pltpu.make_async_copy(emb, x, sem_in)
    load.start()

    def block_rows(o, core):
        return pl.ds(pl.multiple_of((o * 2 + core) * own, own), own)

    ct[block_rows(z, c), :] = cen[...]
    pl.semaphore_wait(barrier, len(partners))

    piece = own // SUBS
    stages = half // 2

    def far_hop(o, way, stage, sub):
        at = ct.at[pl.ds(pl.multiple_of((o * 2 + c) * own + sub * piece, piece), piece)]
        return pltpu.make_async_remote_copy(
            src_ref=at, dst_ref=at, send_sem=g_send.at[way, stage, sub], recv_sem=g_recv.at[way, stage, sub],
            device_id={"dp": far[way]}, device_id_type=MESH)

    def near_hop(o, way, stage):
        at = ct.at[block_rows(o, c)]
        return pltpu.make_async_remote_copy(
            src_ref=at, dst_ref=at, send_sem=g_send.at[way, stage, SUBS], recv_sem=g_recv.at[way, stage, SUBS],
            device_id={"dp": near[way]}, device_id_type=MESH)

    def source(way, distance):
        return (z - distance + nz) % nz if way == 0 else (z + distance) % nz

    def across(o, slot):
        at = ct.at[block_rows(o, c)]
        return pltpu.make_async_remote_copy(
            src_ref=at, dst_ref=at, send_sem=gs_send.at[slot], recv_sem=gs_recv.at[slot],
            device_id={"dp": other}, device_id_type=MESH)

    pending = []

    def launch(desc):
        desc.start()
        pending.append(desc)

    for sub in range(SUBS):
        for way in (0, 1):
            launch(far_hop(z, way, 0, sub))
    for way in (0, 1):
        launch(near_hop(z, way, 0))
    launch(across(z, 0))

    def square(o, core):
        v = ct[block_rows(o, core), :].astype(F32)
        return jnp.sum((v * v).reshape(own // 8, 8, cent), axis=0)

    load.wait()
    tile, short = 256, 128
    eye = (
        lax.broadcasted_iota(jnp.int32, (tile, tile), 0) == lax.broadcasted_iota(jnp.int32, (tile, tile), 1)
    ).astype(BF16)

    def prepare(b):
        at = pl.ds(b * short, short)
        v = x[at, :].astype(F32)
        u = (v * (1.0 / jnp.sqrt(jnp.sum(v * v, axis=1, keepdims=True) + 1e-06))).astype(BF16)
        x[at, :] = u

    def turn(b):
        at = pl.ds(b * short, short)
        for f in range(feat // tile):
            ut[pl.ds(f * tile, tile), at] = dot(
                eye, x[at, f * tile:(f + 1) * tile], ((1,), (1,))).astype(BF16)

    squares = square(z, c)
    behind = [(z, 0)]
    unit = 0
    for stage in range(stages):
        came = []
        for sub in range(SUBS):
            if unit < rows // short:
                prepare(unit)
                unit += 1
            for way in (0, 1):
                if stage == stages - 1 and way == 1:
                    continue
                o = source(way, 2 * stage + 2)
                far_hop(o, way, stage, sub).wait_recv()
                if stage < stages - 1 and (stage < stages - 2 or way == 0):
                    launch(far_hop(o, way, stage + 1, sub))
                if sub == SUBS - 1:
                    if stage < stages - 1:
                        launch(near_hop(o, way, stage + 1))
                    launch(across(o, 2 + 4 * stage + way))
                    came.append((o, 2 + 4 * stage + way))
        for way in (0, 1):
            o = source(way, 2 * stage + 1)
            near_hop(o, way, stage).wait_recv()
            slot = 4 * stage + 4 + way if stage < stages - 1 else (1, 2 * half - 1)[way]
            launch(across(o, slot))
            came.append((o, slot))
        for o, slot in behind:
            across(o, slot).wait_recv()
            squares = squares + square(o, 1 - c)
        for o, slot in came:
            squares = squares + square(o, c)
        behind = came
    for o, slot in behind:
        across(o, slot).wait_recv()
        squares = squares + square(o, 1 - c)

    scale = LOGIT_SCALE * (1.0 / jnp.sqrt(jnp.sum(squares, axis=0, keepdims=True) + 1e-06))
    m_tile = rows // 4

    def score(b, acc):
        at = pl.ds(pl.multiple_of(b * m_tile, m_tile), m_tile)
        v = jnp.exp(dot(x[at, :], ct[...], ((1,), (0,))) * scale)
        e[at, :] = v
        return acc + jnp.sum(v.reshape(m_tile // 8, 8, cent), axis=0)

    acc = lax.fori_loop(0, 4, score, jnp.zeros((8, cent), F32))

    def exchange(buf, sem, me, ids, units=()):
        for t in ids:
            pltpu.make_async_remote_copy(
                src_ref=buf.at[me], dst_ref=buf.at[me], send_sem=sem.at[0], recv_sem=sem.at[1],
                device_id=t, device_id_type=MESH).start()
        whole = buf.at[pl.ds(0, len(ids))]
        done = pltpu.make_async_remote_copy(
            src_ref=whole, dst_ref=whole, send_sem=sem.at[0], recv_sem=sem.at[1],
            device_id=ids[0], device_id_type=MESH)
        pending.append(done)
        for b in units:
            turn(b)
        done.wait_recv()
        return functools.reduce(lambda a, b: a + b, [buf[k] for k in range(len(ids) + 1)])

    def sum_dp(first, second, first_sem, second_sem, units=((), ())):
        second[level] = exchange(first, first_sem, in_group, group_ids, units[0])
        return exchange(second, second_sem, level, level_ids, units[1])

    lane = lax.broadcasted_iota(jnp.int32, (8, LANES), 1)
    tiles = [(0, LANES), (LANES, rows // 8)]

    per_sweep = rows // short // SWEEPS
    for i in range(SWEEPS):
        turns = range(i * per_sweep, (i + 1) * per_sweep)
        col_a[i, in_group] = jnp.sum(acc, axis=0, keepdims=True)
        cv = 1.0 / (n_cent * sum_dp(
            col_a.at[i], col_b.at[i], ca_sem.at[i], cb_sem.at[i], (turns[0:1], turns[1:2])))
        cb = jnp.broadcast_to(cv, (8, cent))

        totals = []
        for lo, hi in tiles:
            def row_step(g, t):
                for k in range(UNIT):
                    q = e[pl.ds(pl.multiple_of((lo + g * UNIT + k) * 8, 8), 8), :] * cb
                    q = functools.reduce(
                        lambda a, b: a + b, [q[:, m * LANES:(m + 1) * LANES] for m in range(cent // LANES)])
                    t = jnp.where(lane == g * UNIT + k, jnp.sum(q, axis=1, keepdims=True), t)
                return t

            totals.append(lax.fori_loop(0, (hi - lo) // UNIT, row_step, jnp.zeros((8, LANES), F32)))
        row_x[i, p, 0] = totals[0][0:4]
        row_x[i, p, 1] = totals[0][4:8]
        row_x[i, p, 2] = totals[1][0:4] + pltpu.roll(totals[1], LANES // 2, 1)[4:8]
        rv = 1.0 / (n_rows * exchange(row_x.at[i], rx_sem.at[i], p, proto_ids, turns[2:]))
        r0 = jnp.concatenate([rv[0], rv[1]], axis=0)
        r1 = jnp.concatenate([rv[2], pltpu.roll(rv[2], LANES // 2, 1)], axis=0)

        final = i == SWEEPS - 1
        nc = jnp.broadcast_to(n_rows * cv, (8, cent))
        acc = jnp.zeros((8, cent), F32)
        for (lo, hi), r in zip(tiles, (r0, r1)):
            def col_step(g, st):
                a, r = st
                for k in range(0, UNIT, 2):
                    at = pl.multiple_of((lo + g * UNIT + k) * 8, 16)
                    pair = [e[pl.ds(at + 8 * m, 8), :] * jnp.broadcast_to(r[:, k + m:k + m + 1], (8, cent))
                            for m in range(2)]
                    a = a + pair[0] + pair[1]
                    if final:
                        w[pl.ds(at, 16), :] = jnp.concatenate([v * nc for v in pair], axis=0).astype(BF16)
                return a, pltpu.roll(r, LANES - UNIT, 1)

            acc, _ = lax.fori_loop(0, (hi - lo) // UNIT, col_step, (acc, r))

    def swap(rel):
        return pltpu.make_async_remote_copy(
            src_ref=s.at[rel, pl.ds(pl.multiple_of((1 - c) * own, own), own)], dst_ref=sib.at[rel],
            send_sem=sx_send.at[rel], recv_sem=sx_recv.at[rel],
            device_id={"dp": other}, device_id_type=MESH)

    def make_sums(rels):
        u = [ut[pl.ds(pl.multiple_of(((z + rel) % nz) * 2 * own, 2 * own), 2 * own), :] for rel in rels]
        v = dot(jnp.concatenate(u, axis=0) if len(u) > 1 else u[0], w[...], ((1,), (0,)))
        for k, rel in enumerate(rels):
            s[rel] = v[k * 2 * own:(k + 1) * 2 * own]
            launch(swap(rel))

    wide = cent // PARTS
    flows = []
    for hops in (half, half - 1):
        for m in range(PARTS // 2):
            for way in (0, 1):
                first = way == (0 if hops == half else 1)
                flows.append((way, m if first else PARTS // 2 + m, hops))

    def link(way, part, t):
        return pltpu.make_async_remote_copy(
            src_ref=ring.at[way, part, t], dst_ref=ring.at[way, part, t + 1],
            send_sem=r_send.at[way, part, t], recv_sem=r_recv.at[way, part, t],
            device_id={"dp": right if way == 0 else left}, device_id_type=MESH)

    own_rows = pl.ds(pl.multiple_of(c * own, own), own)

    def pair_sum(rel, part):
        cols = pl.ds(part * wide, wide)
        return s[rel, own_rows, cols] + sib[rel, :, cols]

    orders = [[half]] + [[half - q, half + q] for q in range(1, half)] + [[0]]
    for k in range(3):
        make_sums(orders[k])
    ready = set()
    for t in range(half):
        for way, part, hops in flows:
            if t >= hops:
                continue
            rel = hops - t if way == 0 else nz - (hops - t)
            if rel not in ready:
                swap(rel).wait_recv()
                ready.add(rel)
            v = pair_sum(rel, part)
            if t > 0:
                link(way, part, t - 1).wait_recv()
                v = v + ring[way, part, t]
            ring[way, part, t] = v
            launch(link(way, part, t))
        if t + 3 < len(orders):
            make_sums(orders[t + 3])
    swap(0).wait_recv()
    for way, part, hops in flows:
        link(way, part, hops - 1).wait_recv()
    parts = []
    for part in range(PARTS):
        v = pair_sum(0, part)
        for way, q, hops in flows:
            if q == part:
                v = v + ring[way, q, hops]
        parts.append(v)
    sums = jnp.concatenate(parts, axis=1)

    fin_a[in_group, :, 0:cent] = jnp.sum(acc, axis=0, keepdims=True)
    fin_a[in_group, :, cent:2 * cent] = jnp.sum(sums * sums, axis=0, keepdims=True)
    tot = sum_dp(fin_a, fin_b, fa_sem, fb_sem)
    mass_out[...] = n_cent * cv * tot[:, 0:cent]
    out[...] = sums * (1.0 / jnp.sqrt(tot[:, cent:2 * cent] + 1e-06))

    for desc in pending:
        desc.wait_send()


def hand_over(sums, mass, sums_out, mass_out):
    sums_out[...] = sums[...]
    mass_out[...] = mass[...]


def solution(mesh):
    n_dp, n_proto = mesh.shape["dp"], mesh.shape["proto"]
    nz = n_dp // 2
    half = nz // 2
    levels = n_dp // GROUP

    def per_device(embeddings, centroids):
        rows, feat = embeddings.shape
        cent = centroids.shape[0]
        own = feat // n_dp
        dma, vmem = pltpu.SemaphoreType.DMA, pltpu.VMEM
        whole = pl.BlockSpec(memory_space=pltpu.VMEM)
        shapes = (jax.ShapeDtypeStruct((own, cent), F32), jax.ShapeDtypeStruct((1, cent), F32))
        sums, mass = pl.pallas_call(
            functools.partial(kernel, (n_dp, n_proto, rows, feat, cent)),
            out_shape=shapes,
            in_specs=[pl.BlockSpec(memory_space=pl.ANY), whole],
            out_specs=(whole, whole),
            scratch_shapes=[
                vmem((rows, feat), BF16),
                vmem((feat, rows), BF16),
                vmem((feat, cent), BF16),
                vmem((rows, cent), F32),
                vmem((rows, cent), BF16),
                vmem((nz, 2 * own, cent), F32),
                vmem((SWEEPS, GROUP, 1, cent), F32),
                vmem((SWEEPS, levels, 1, cent), F32),
                vmem((SWEEPS, n_proto, 3, 4, LANES), F32),
                vmem((GROUP, 1, 2 * cent), F32),
                vmem((levels, 1, 2 * cent), F32),
                vmem((nz, own, cent), F32),
                vmem((2, PARTS, half + 1, own, cent // PARTS), F32),
                dma,
                dma((2, half // 2, SUBS + 1)), dma((2, half // 2, SUBS + 1)), dma((nz,)), dma((nz,)),
                dma((SWEEPS, 2)), dma((SWEEPS, 2)), dma((SWEEPS, 2)),
                dma((2,)), dma((2,)),
                dma((nz,)), dma((nz,)),
                dma((2, PARTS, half)), dma((2, PARTS, half)),
            ],
            compiler_params=pltpu.CompilerParams(
                collective_id=0, has_side_effects=True, vmem_limit_bytes=56 * 1024 * 1024),
            cost_estimate=pl.CostEstimate(
                flops=4 * rows * feat * cent, bytes_accessed=2 * rows * feat, transcendentals=rows * cent),
        )(embeddings, centroids.T)
        new_centroids, mass = pl.pallas_call(
            hand_over, out_shape=shapes, in_specs=[whole, whole], out_specs=(whole, whole))(sums, mass)
        return new_centroids, mass.reshape(cent)

    return jax.shard_map(
        per_device,
        mesh=mesh,
        in_specs=(P("dp", None), P("proto", "dp")),
        out_specs=(P("dp", "proto"), P("proto")),
        check_vma=False,
    )
```

```python
import functools

import jax
import jax.numpy as jnp
from jax import lax
from jax.experimental import pallas as pl
from jax.experimental.pallas import tpu as pltpu
from jax.sharding import PartitionSpec as P

SWEEPS = 3
LOGIT_SCALE = 40.0
F32, BF16 = jnp.float32, jnp.bfloat16
MESH = pl.DeviceIdType.MESH
GROUP = 8
SUBS = 3
PARTS = 4
JOINS = 2
UNIT = 32
LANES = 128


def dot(a, b, dims):
    return lax.dot_general(a, b, (dims, ((), ())), preferred_element_type=F32)


def kernel(sizes, emb, cen, out, mass_out, x, ut, ct, e, w, s, col_x, row_x, mass_a, mass_b, len_x, sib, leave, ring,
           sem_in, g_send, g_recv, gs_send, gs_recv, cx_sem, rx_sem, ma_sem, mb_sem, lx_sem,
           sx_send, sx_recv, r_send, r_recv):
    n_dp, n_proto, rows, feat, cent = sizes
    nz = n_dp // 2
    half = nz // 2
    own = feat // n_dp
    n_rows = rows * n_dp
    n_cent = cent * n_proto
    levels = n_dp // GROUP

    d = lax.axis_index("dp")
    p = lax.axis_index("proto")
    z, c = d // 2, d % 2
    other = d + 1 - 2 * c
    right = ((z + 1) % nz) * 2 + c
    left = ((z + nz - 1) % nz) * 2 + c
    near = (right, left)
    far = ((d + 4) % n_dp, (d + n_dp - 4) % n_dp)
    in_group = d % GROUP
    level = d // GROUP
    group_ids = [{"dp": level * GROUP + (in_group + j) % GROUP} for j in range(1, GROUP)]
    level_ids = [{"dp": (d + GROUP * j) % n_dp} for j in range(1, levels)]
    dp_ids = [{"dp": (d + j) % n_dp} for j in sorted(range(1, n_dp), key=lambda j: -min(j, n_dp - j))]
    proto_ids = [{"proto": (p + j) % n_proto} for j in range(1, n_proto)]

    barrier = pltpu.get_barrier_semaphore()
    partners = dp_ids[::-1] + proto_ids
    for t in partners:
        pl.semaphore_signal(barrier, inc=1, device_id=t, device_id_type=MESH)

    load = pltpu.make_async_copy(emb, x, sem_in)
    load.start()

    def block_rows(o, core):
        return pl.ds(pl.multiple_of((o * 2 + core) * own, own), own)

    ct[block_rows(z, c), :] = cen[...]
    pl.semaphore_wait(barrier, len(partners))

    piece = own // SUBS
    stages = half // 2

    def far_hop(o, way, stage, sub):
        at = ct.at[pl.ds(pl.multiple_of((o * 2 + c) * own + sub * piece, piece), piece)]
        return pltpu.make_async_remote_copy(
            src_ref=at, dst_ref=at, send_sem=g_send.at[way, stage, sub], recv_sem=g_recv.at[way, stage, sub],
            device_id={"dp": far[way]}, device_id_type=MESH)

    def near_hop(o, way, stage):
        at = ct.at[block_rows(o, c)]
        return pltpu.make_async_remote_copy(
            src_ref=at, dst_ref=at, send_sem=g_send.at[way, stage, SUBS], recv_sem=g_recv.at[way, stage, SUBS],
            device_id={"dp": near[way]}, device_id_type=MESH)

    def source(way, distance):
        return (z - distance + nz) % nz if way == 0 else (z + distance) % nz

    def across(o, slot):
        at = ct.at[block_rows(o, c)]
        return pltpu.make_async_remote_copy(
            src_ref=at, dst_ref=at, send_sem=gs_send.at[slot], recv_sem=gs_recv.at[slot],
            device_id={"dp": other}, device_id_type=MESH)

    pending = []

    def launch(desc):
        desc.start()
        pending.append(desc)

    for sub in range(SUBS):
        for way in (0, 1):
            launch(far_hop(z, way, 0, sub))
    for way in (0, 1):
        launch(near_hop(z, way, 0))
    launch(across(z, 0))

    def square(o, core):
        v = ct[block_rows(o, core), :].astype(F32)
        return jnp.sum((v * v).reshape(own // 8, 8, cent), axis=0)

    load.wait()
    tile, short = 256, 128
    eye = (
        lax.broadcasted_iota(jnp.int32, (tile, tile), 0) == lax.broadcasted_iota(jnp.int32, (tile, tile), 1)
    ).astype(BF16)

    def prepare(b):
        at = pl.ds(b * short, short)
        v = x[at, :].astype(F32)
        u = (v * (1.0 / jnp.sqrt(jnp.sum(v * v, axis=1, keepdims=True) + 1e-06))).astype(BF16)
        x[at, :] = u

    def turn(b):
        at = pl.ds(b * short, short)
        for f in range(feat // tile):
            ut[pl.ds(f * tile, tile), at] = dot(
                eye, x[at, f * tile:(f + 1) * tile], ((1,), (1,))).astype(BF16)

    squares = square(z, c)
    behind = [(z, 0)]
    unit = 0
    for stage in range(stages):
        came = []
        for sub in range(SUBS):
            if unit < rows // short:
                prepare(unit)
                unit += 1
            for way in (0, 1):
                if stage == stages - 1 and way == 1:
                    continue
                o = source(way, 2 * stage + 2)
                far_hop(o, way, stage, sub).wait_recv()
                if stage < stages - 1 and (stage < stages - 2 or way == 0):
                    launch(far_hop(o, way, stage + 1, sub))
                if sub == SUBS - 1:
                    if stage < stages - 1:
                        launch(near_hop(o, way, stage + 1))
                    launch(across(o, 2 + 4 * stage + way))
                    came.append((o, 2 + 4 * stage + way))
        for way in (0, 1):
            o = source(way, 2 * stage + 1)
            near_hop(o, way, stage).wait_recv()
            slot = 4 * stage + 4 + way if stage < stages - 1 else (1, 2 * half - 1)[way]
            launch(across(o, slot))
            came.append((o, slot))
        for o, slot in behind:
            across(o, slot).wait_recv()
            squares = squares + square(o, 1 - c)
        for o, slot in came:
            squares = squares + square(o, c)
        behind = came
    for o, slot in behind:
        across(o, slot).wait_recv()
        squares = squares + square(o, 1 - c)

    scale = LOGIT_SCALE * (1.0 / jnp.sqrt(jnp.sum(squares, axis=0, keepdims=True) + 1e-06))
    m_tile = rows // 4

    def score(b, acc):
        at = pl.ds(pl.multiple_of(b * m_tile, m_tile), m_tile)
        v = jnp.exp(dot(x[at, :], ct[...], ((1,), (0,))) * scale)
        e[at, :] = v
        return acc + jnp.sum(v.reshape(m_tile // 8, 8, cent), axis=0)

    acc = lax.fori_loop(0, 4, score, jnp.zeros((8, cent), F32))

    def send_all(buf, sem, me, ids):
        for t in ids:
            pltpu.make_async_remote_copy(
                src_ref=buf.at[me], dst_ref=buf.at[me], send_sem=sem.at[0], recv_sem=sem.at[1],
                device_id=t, device_id_type=MESH).start()
        whole = buf.at[pl.ds(0, len(ids))]
        done = pltpu.make_async_remote_copy(
            src_ref=whole, dst_ref=whole, send_sem=sem.at[0], recv_sem=sem.at[1],
            device_id=ids[0], device_id_type=MESH)
        pending.append(done)
        return done

    def total(buf, ids):
        terms = [buf[k] for k in range(len(ids) + 1)]
        while len(terms) > 1:
            terms = [terms[k] + terms[k + 1] for k in range(0, len(terms), 2)]
        return terms[0]

    def exchange(buf, sem, me, ids, units=()):
        done = send_all(buf, sem, me, ids)
        for b in units:
            turn(b)
        done.wait_recv()
        return total(buf, ids)

    lane = lax.broadcasted_iota(jnp.int32, (8, LANES), 1)
    tiles = [(0, LANES), (LANES, rows // 8)]

    per_sweep = rows // short // SWEEPS
    for i in range(SWEEPS):
        turns = range(i * per_sweep, (i + 1) * per_sweep)
        col_x[i, d] = jnp.sum(acc, axis=0, keepdims=True)
        cv = 1.0 / (n_cent * exchange(col_x.at[i], cx_sem.at[i], d, dp_ids, turns[0:2]))
        cb = jnp.broadcast_to(cv, (8, cent))

        totals = []
        for lo, hi in tiles:
            def row_step(g, t):
                for k in range(UNIT):
                    q = e[pl.ds(pl.multiple_of((lo + g * UNIT + k) * 8, 8), 8), :] * cb
                    q = functools.reduce(
                        lambda a, b: a + b, [q[:, m * LANES:(m + 1) * LANES] for m in range(cent // LANES)])
                    t = jnp.where(lane == g * UNIT + k, jnp.sum(q, axis=1, keepdims=True), t)
                return t

            totals.append(lax.fori_loop(0, (hi - lo) // UNIT, row_step, jnp.zeros((8, LANES), F32)))
        row_x[i, p, 0] = totals[0][0:4]
        row_x[i, p, 1] = totals[0][4:8]
        row_x[i, p, 2] = totals[1][0:4] + pltpu.roll(totals[1], LANES // 2, 1)[4:8]
        rv = 1.0 / (n_rows * exchange(row_x.at[i], rx_sem.at[i], p, proto_ids, turns[2:]))
        r0 = jnp.concatenate([rv[0], rv[1]], axis=0)
        r1 = jnp.concatenate([rv[2], pltpu.roll(rv[2], LANES // 2, 1)], axis=0)

        final = i == SWEEPS - 1
        nc = jnp.broadcast_to(n_rows * cv, (8, cent))
        acc = jnp.zeros((8, cent), F32)
        for (lo, hi), r in zip(tiles, (r0, r1)):
            def col_step(g, st):
                a, r = st
                for k in range(0, UNIT, 2):
                    at = pl.multiple_of((lo + g * UNIT + k) * 8, 16)
                    pair = [e[pl.ds(at + 8 * m, 8), :] * jnp.broadcast_to(r[:, k + m:k + m + 1], (8, cent))
                            for m in range(2)]
                    a = a + pair[0] + pair[1]
                    if final:
                        w[pl.ds(at, 16), :] = jnp.concatenate([v * nc for v in pair], axis=0).astype(BF16)
                return a, pltpu.roll(r, LANES - UNIT, 1)

            acc, _ = lax.fori_loop(0, (hi - lo) // UNIT, col_step, (acc, r))

    def swap(rel):
        return pltpu.make_async_remote_copy(
            src_ref=s.at[rel, pl.ds(pl.multiple_of((1 - c) * own, own), own)], dst_ref=sib.at[rel],
            send_sem=sx_send.at[rel], recv_sem=sx_recv.at[rel],
            device_id={"dp": other}, device_id_type=MESH)

    def make_sums(rels):
        u = [ut[pl.ds(pl.multiple_of(((z + rel) % nz) * 2 * own, 2 * own), 2 * own), :] for rel in rels]
        v = dot(jnp.concatenate(u, axis=0) if len(u) > 1 else u[0], w[...], ((1,), (0,)))
        for k, rel in enumerate(rels):
            s[rel] = v[k * 2 * own:(k + 1) * 2 * own]
            launch(swap(rel))

    wide = cent // PARTS
    flows = []
    for hops in (half, half - 1):
        for m in range(PARTS // 2):
            for way in (0, 1):
                first = way == (0 if hops == half else 1)
                flows.append((way, m if first else PARTS // 2 + m, hops))

    def parent(q, hops):
        up = (hops - q) // 2
        return hops - 2 * up - 2 if up < JOINS else q - 1

    def link(way, part, hops, q):
        step = q - parent(q, hops)
        return pltpu.make_async_remote_copy(
            src_ref=leave.at[way, part, q - 1], dst_ref=ring.at[way, part, q - 1],
            send_sem=r_send.at[way, part, q - 1], recv_sem=r_recv.at[way, part, q - 1],
            device_id={"dp": (near if step == 1 else far)[way]}, device_id_type=MESH)

    own_rows = pl.ds(pl.multiple_of(c * own, own), own)
    ready = set()

    def gathered(way, part, hops, q):
        rel = (q if way == 0 else nz - q) % nz
        if rel not in ready:
            swap(rel).wait_recv()
            ready.add(rel)
        cols = pl.ds(part * wide, wide)
        v = s[rel, own_rows, cols] + sib[rel, :, cols]
        return v + children(way, part, hops, q) if q else v

    def children(way, part, hops, q):
        v = 0.0
        for child in range(1, hops + 1):
            if parent(child, hops) == q:
                link(way, part, hops, child).wait_recv()
                v = v + ring[way, part, child - 1]
        return v

    def pass_on(distances):
        for way, part, hops in flows:
            for q in distances(hops):
                leave[way, part, q - 1] = gathered(way, part, hops, q)
                launch(link(way, part, hops, q))

    mass_a[in_group] = jnp.sum(acc, axis=0, keepdims=True)
    mass_first = send_all(mass_a, ma_sem, in_group, group_ids)
    make_sums([half])
    make_sums([half - 1, half + 1])
    make_sums([half - 2, half + 2])
    make_sums([half - 3, half + 3])
    make_sums([half - 4, half + 4])
    pass_on(lambda hops: (hops, hops - 1))
    pass_on(lambda hops: (hops - 3,))
    mass_first.wait_recv()
    mass_b[level] = total(mass_a, group_ids)
    mass_second = send_all(mass_b, mb_sem, level, level_ids)
    make_sums([half - 5, half + 5])
    make_sums([half - 6, half + 6])
    pass_on(lambda hops: (hops - 2,))
    make_sums([half - 7, half + 7])
    make_sums([0])
    for up in range(4, half):
        pass_on(lambda hops: (hops - up,) if hops > up else ())
    parts = []
    for part in range(PARTS):
        v = gathered(0, part, half, 0)
        for way, q, hops in flows:
            if q == part:
                v = v + children(way, part, hops, 0)
        parts.append(v)
    sums = jnp.concatenate(parts, axis=1)
    len_x[d] = jnp.sum(sums * sums, axis=0, keepdims=True)
    lengths = exchange(len_x, lx_sem, d, dp_ids)
    out[...] = sums * (1.0 / jnp.sqrt(lengths + 1e-06))
    mass_second.wait_recv()
    mass_out[...] = n_cent * cv * total(mass_b, level_ids)

    for desc in pending:
        desc.wait_send()


def hand_over(sums, mass, sums_out, mass_out):
    sums_out[...] = sums[...]
    mass_out[...] = mass[...]


def solution(mesh):
    n_dp, n_proto = mesh.shape["dp"], mesh.shape["proto"]
    nz = n_dp // 2
    half = nz // 2
    levels = n_dp // GROUP

    def per_device(embeddings, centroids):
        rows, feat = embeddings.shape
        cent = centroids.shape[0]
        own = feat // n_dp
        dma, vmem = pltpu.SemaphoreType.DMA, pltpu.VMEM
        whole = pl.BlockSpec(memory_space=pltpu.VMEM)
        shapes = (jax.ShapeDtypeStruct((own, cent), F32), jax.ShapeDtypeStruct((1, cent), F32))
        sums, mass = pl.pallas_call(
            functools.partial(kernel, (n_dp, n_proto, rows, feat, cent)),
            out_shape=shapes,
            in_specs=[pl.BlockSpec(memory_space=pl.ANY), whole],
            out_specs=(whole, whole),
            scratch_shapes=[
                vmem((rows, feat), BF16),
                vmem((feat, rows), BF16),
                vmem((feat, cent), BF16),
                vmem((rows, cent), F32),
                vmem((rows, cent), BF16),
                vmem((nz, 2 * own, cent), F32),
                vmem((SWEEPS, n_dp, 1, cent), F32),
                vmem((SWEEPS, n_proto, 3, 4, LANES), F32),
                vmem((GROUP, 1, cent), F32),
                vmem((levels, 1, cent), F32),
                vmem((n_dp, 1, cent), F32),
                vmem((nz, own, cent), F32),
                vmem((2, PARTS, half, own, cent // PARTS), F32),
                vmem((2, PARTS, half, own, cent // PARTS), F32),
                dma,
                dma((2, half // 2, SUBS + 1)), dma((2, half // 2, SUBS + 1)), dma((nz,)), dma((nz,)),
                dma((SWEEPS, 2)), dma((SWEEPS, 2)), dma((2,)), dma((2,)), dma((2,)),
                dma((nz,)), dma((nz,)),
                dma((2, PARTS, half)), dma((2, PARTS, half)),
            ],
            compiler_params=pltpu.CompilerParams(
                collective_id=0, has_side_effects=True, vmem_limit_bytes=56 * 1024 * 1024),
            cost_estimate=pl.CostEstimate(
                flops=4 * rows * feat * cent, bytes_accessed=2 * rows * feat, transcendentals=rows * cent),
        )(embeddings, centroids.T)
        new_centroids, mass = pl.pallas_call(
            hand_over, out_shape=shapes, in_specs=[whole, whole], out_specs=(whole, whole))(sums, mass)
        return new_centroids, mass.reshape(cent)

    return jax.shard_map(
        per_device,
        mesh=mesh,
        in_specs=(P("dp", None), P("proto", "dp")),
        out_specs=(P("dp", "proto"), P("proto")),
        check_vma=False,
    )
```

```python
import functools

import jax
import jax.numpy as jnp
from jax import lax
from jax.experimental import pallas as pl
from jax.experimental.pallas import tpu as pltpu
from jax.sharding import PartitionSpec as P

SWEEPS = 3
LOGIT_SCALE = 40.0
F32, BF16 = jnp.float32, jnp.bfloat16
MESH = pl.DeviceIdType.MESH
GROUP = 8
SUBS = 3
PARTS = 4
JOINS = 2
UNIT = 32
LANES = 128


def dot(a, b, dims):
    return lax.dot_general(a, b, (dims, ((), ())), preferred_element_type=F32)


def kernel(sizes, emb, cen, out, mass_out, x, ut, ct, e, w, s, col_x, row_x, mass_a, mass_b, len_x, sib, leave, ring,
           sem_in, g_send, g_recv, gs_recv, cx_sem, rx_sem, ma_sem, mb_sem, lx_sem,
           sx_send, sx_recv, r_send, r_recv):
    n_dp, n_proto, rows, feat, cent = sizes
    nz = n_dp // 2
    half = nz // 2
    own = feat // n_dp
    n_rows = rows * n_dp
    n_cent = cent * n_proto
    levels = n_dp // GROUP

    d = lax.axis_index("dp")
    p = lax.axis_index("proto")
    z, c = d // 2, d % 2
    other = d + 1 - 2 * c
    right = ((z + 1) % nz) * 2 + c
    left = ((z + nz - 1) % nz) * 2 + c
    near = (right, left)
    far = ((d + 4) % n_dp, (d + n_dp - 4) % n_dp)
    in_group = d % GROUP
    level = d // GROUP
    group_ids = [{"dp": level * GROUP + (in_group + j) % GROUP} for j in range(1, GROUP)]
    level_ids = [{"dp": (d + GROUP * j) % n_dp} for j in range(1, levels)]
    dp_ids = [{"dp": (d + j) % n_dp} for j in sorted(range(1, n_dp), key=lambda j: -min(j, n_dp - j))]
    proto_ids = [{"proto": (p + j) % n_proto} for j in range(1, n_proto)]

    load = pltpu.make_async_copy(emb, x, sem_in)
    load.start()

    barrier = pltpu.get_barrier_semaphore()
    partners = dp_ids[::-1] + proto_ids
    for t in partners:
        pl.semaphore_signal(barrier, inc=1, device_id=t, device_id_type=MESH)

    def block_rows(o, core):
        return pl.ds(pl.multiple_of((o * 2 + core) * own, own), own)

    ct[block_rows(z, c), :] = cen[...]
    pl.semaphore_wait(barrier, len(partners))

    piece = own // SUBS
    stages = half // 2

    def far_hop(o, way, stage, sub):
        at = ct.at[pl.ds(pl.multiple_of((o * 2 + c) * own + sub * piece, piece), piece)]
        return pltpu.make_async_remote_copy(
            src_ref=at, dst_ref=at, send_sem=g_send, recv_sem=g_recv.at[way, stage, sub],
            device_id={"dp": far[way]}, device_id_type=MESH)

    def near_hop(o, way, stage):
        at = ct.at[block_rows(o, c)]
        return pltpu.make_async_remote_copy(
            src_ref=at, dst_ref=at, send_sem=g_send, recv_sem=g_recv.at[way, stage, SUBS],
            device_id={"dp": near[way]}, device_id_type=MESH)

    def source(way, distance):
        return (z - distance + nz) % nz if way == 0 else (z + distance) % nz

    def across(o, slot):
        at = ct.at[block_rows(o, c)]
        return pltpu.make_async_remote_copy(
            src_ref=at, dst_ref=at, send_sem=g_send, recv_sem=gs_recv.at[slot],
            device_id={"dp": other}, device_id_type=MESH)

    pending = []

    def launch(desc):
        desc.start()

    for sub in range(SUBS):
        for way in (0, 1):
            launch(far_hop(z, way, 0, sub))
    for way in (0, 1):
        launch(near_hop(z, way, 0))
    launch(across(z, 0))

    def square(o, core):
        v = ct[block_rows(o, core), :].astype(F32)
        return jnp.sum((v * v).reshape(own // 8, 8, cent), axis=0)

    load.wait()
    tile, short = 256, 128
    eye = (
        lax.broadcasted_iota(jnp.int32, (tile, tile), 0) == lax.broadcasted_iota(jnp.int32, (tile, tile), 1)
    ).astype(BF16)

    def prepare(b):
        at = pl.ds(b * short, short)
        v = x[at, :].astype(F32)
        u = (v * (1.0 / jnp.sqrt(jnp.sum(v * v, axis=1, keepdims=True) + 1e-06))).astype(BF16)
        x[at, :] = u

    def turn(b):
        at = pl.ds(b * short, short)
        for f in range(feat // tile):
            ut[pl.ds(f * tile, tile), at] = dot(
                eye, x[at, f * tile:(f + 1) * tile], ((1,), (1,))).astype(BF16)

    squares = square(z, c)
    behind = [(z, 0)]
    unit = 0
    for stage in range(stages):
        came = []
        for sub in range(SUBS):
            if unit < rows // short:
                prepare(unit)
                unit += 1
            for way in (0, 1):
                if stage == stages - 1 and way == 1:
                    continue
                o = source(way, 2 * stage + 2)
                far_hop(o, way, stage, sub).wait_recv()
                if stage < stages - 1 and (stage < stages - 2 or way == 0):
                    launch(far_hop(o, way, stage + 1, sub))
                if sub == SUBS - 1:
                    if stage < stages - 1:
                        launch(near_hop(o, way, stage + 1))
                    launch(across(o, 2 + 4 * stage + way))
                    came.append((o, 2 + 4 * stage + way))
        for way in (0, 1):
            o = source(way, 2 * stage + 1)
            near_hop(o, way, stage).wait_recv()
            slot = 4 * stage + 4 + way if stage < stages - 1 else (1, 2 * half - 1)[way]
            launch(across(o, slot))
            came.append((o, slot))
        for o, slot in behind:
            across(o, slot).wait_recv()
            squares = squares + square(o, 1 - c)
        for o, slot in came:
            squares = squares + square(o, c)
        behind = came
    for o, slot in behind:
        across(o, slot).wait_recv()
        squares = squares + square(o, 1 - c)

    scale = LOGIT_SCALE * (1.0 / jnp.sqrt(jnp.sum(squares, axis=0, keepdims=True) + 1e-06))
    m_tile = rows // 4

    def product(b):
        return dot(x[b * m_tile:(b + 1) * m_tile, :], ct[...], ((1,), (0,)))

    acc = jnp.zeros((8, cent), F32)
    raw = product(0)
    for b in range(4):
        ahead = product(b + 1) if b < 3 else None
        v = jnp.exp(raw * scale)
        e[b * m_tile:(b + 1) * m_tile, :] = v
        acc = acc + jnp.sum(v.reshape(m_tile // 8, 8, cent), axis=0)
        raw = ahead

    def send_all(buf, sem, me, ids):
        for t in ids:
            pltpu.make_async_remote_copy(
                src_ref=buf.at[me], dst_ref=buf.at[me], send_sem=sem.at[0], recv_sem=sem.at[1],
                device_id=t, device_id_type=MESH).start()
        whole = buf.at[pl.ds(0, len(ids))]
        done = pltpu.make_async_remote_copy(
            src_ref=whole, dst_ref=whole, send_sem=sem.at[0], recv_sem=sem.at[1],
            device_id=ids[0], device_id_type=MESH)
        pending.append(done)
        return done

    def total(buf, ids):
        terms = [buf[k] for k in range(len(ids) + 1)]
        while len(terms) > 1:
            terms = [terms[k] + terms[k + 1] for k in range(0, len(terms), 2)]
        return terms[0]

    def exchange(buf, sem, me, ids, units=(), drain=None):
        done = send_all(buf, sem, me, ids)
        for b in units:
            turn(b)
        if drain:
            drain()
        done.wait_recv()
        return total(buf, ids)

    lane = lax.broadcasted_iota(jnp.int32, (8, LANES), 1)
    tiles = [(0, LANES), (LANES, rows // 8)]

    per_sweep = rows // short // SWEEPS
    for i in range(SWEEPS):
        turns = range(i * per_sweep, (i + 1) * per_sweep)
        col_x[i, d] = jnp.sum(acc, axis=0, keepdims=True)
        cv = 1.0 / (n_cent * exchange(col_x.at[i], cx_sem.at[i], d, dp_ids, turns[0:2]))
        cb = jnp.broadcast_to(cv, (8, cent))

        totals = []
        for lo, hi in tiles:
            def row_step(g, t):
                for k in range(UNIT):
                    q = e[pl.ds(pl.multiple_of((lo + g * UNIT + k) * 8, 8), 8), :] * cb
                    q = functools.reduce(
                        lambda a, b: a + b, [q[:, m * LANES:(m + 1) * LANES] for m in range(cent // LANES)])
                    t = jnp.where(lane == g * UNIT + k, jnp.sum(q, axis=1, keepdims=True), t)
                return t

            totals.append(lax.fori_loop(0, (hi - lo) // UNIT, row_step, jnp.zeros((8, LANES), F32)))
        row_x[i, p, 0] = totals[0][0:4]
        row_x[i, p, 1] = totals[0][4:8]
        row_x[i, p, 2] = totals[1][0:4] + pltpu.roll(totals[1], LANES // 2, 1)[4:8]
        rv = 1.0 / (n_rows * exchange(row_x.at[i], rx_sem.at[i], p, proto_ids, turns[2:]))
        r0 = jnp.concatenate([rv[0], rv[1]], axis=0)
        r1 = jnp.concatenate([rv[2], pltpu.roll(rv[2], LANES // 2, 1)], axis=0)

        final = i == SWEEPS - 1
        nc = jnp.broadcast_to(n_rows * cv, (8, cent))
        acc = jnp.zeros((8, cent), F32)
        for (lo, hi), r in zip(tiles, (r0, r1)):
            def col_step(g, st):
                a, r = st
                for k in range(0, UNIT, 2):
                    at = pl.multiple_of((lo + g * UNIT + k) * 8, 16)
                    pair = [e[pl.ds(at + 8 * m, 8), :] * jnp.broadcast_to(r[:, k + m:k + m + 1], (8, cent))
                            for m in range(2)]
                    a = a + pair[0] + pair[1]
                    if final:
                        w[pl.ds(at, 16), :] = jnp.concatenate([v * nc for v in pair], axis=0).astype(BF16)
                return a, pltpu.roll(r, LANES - UNIT, 1)

            acc, _ = lax.fori_loop(0, (hi - lo) // UNIT, col_step, (acc, r))

    def swap(rel):
        return pltpu.make_async_remote_copy(
            src_ref=s.at[rel, pl.ds(pl.multiple_of((1 - c) * own, own), own)], dst_ref=sib.at[rel],
            send_sem=sx_send, recv_sem=sx_recv.at[rel],
            device_id={"dp": other}, device_id_type=MESH)

    def make_sums(rels):
        u = [ut[pl.ds(pl.multiple_of(((z + rel) % nz) * 2 * own, 2 * own), 2 * own), :] for rel in rels]
        v = dot(jnp.concatenate(u, axis=0) if len(u) > 1 else u[0], w[...], ((1,), (0,)))
        for k, rel in enumerate(rels):
            s[rel] = v[k * 2 * own:(k + 1) * 2 * own]
            launch(swap(rel))

    wide = cent // PARTS
    flows = []
    for hops in (half, half - 1):
        for m in range(PARTS // 2):
            for way in (0, 1):
                first = way == (0 if hops == half else 1)
                flows.append((way, m if first else PARTS // 2 + m, hops))

    def parent(q, hops):
        up = (hops - q) // 2
        return hops - 2 * up - 2 if up < JOINS else q - 1

    def link(way, part, hops, q):
        step = q - parent(q, hops)
        return pltpu.make_async_remote_copy(
            src_ref=leave.at[way, part, q - 1], dst_ref=ring.at[way, part, q - 1],
            send_sem=r_send, recv_sem=r_recv.at[way, part, q - 1],
            device_id={"dp": (near if step == 1 else far)[way]}, device_id_type=MESH)

    own_rows = pl.ds(pl.multiple_of(c * own, own), own)
    ready = set()

    def gathered(way, part, hops, q):
        rel = (q if way == 0 else nz - q) % nz
        if rel not in ready:
            swap(rel).wait_recv()
            ready.add(rel)
        cols = pl.ds(part * wide, wide)
        v = s[rel, own_rows, cols] + sib[rel, :, cols]
        return v + children(way, part, hops, q) if q else v

    def children(way, part, hops, q):
        v = 0.0
        for child in range(1, hops + 1):
            if parent(child, hops) == q:
                link(way, part, hops, child).wait_recv()
                v = v + ring[way, part, child - 1]
        return v

    def pass_on(distances):
        for way, part, hops in flows:
            for q in distances(hops):
                leave[way, part, q - 1] = gathered(way, part, hops, q)
                launch(link(way, part, hops, q))

    mass_a[in_group] = jnp.sum(acc, axis=0, keepdims=True)
    mass_first = send_all(mass_a, ma_sem, in_group, group_ids)
    make_sums([half])
    make_sums([half - 1, half + 1])
    make_sums([half - 2, half + 2])
    make_sums([half - 3, half + 3])
    make_sums([half - 4, half + 4])
    pass_on(lambda hops: (hops, hops - 1))
    pass_on(lambda hops: (hops - 3,))
    mass_first.wait_recv()
    mass_b[level] = total(mass_a, group_ids)
    mass_second = send_all(mass_b, mb_sem, level, level_ids)
    make_sums([half - 5, half + 5])
    make_sums([half - 6, half + 6])
    pass_on(lambda hops: (hops - 2,))
    make_sums([half - 7, half + 7])
    make_sums([0])
    for up in range(4, half):
        pass_on(lambda hops: (hops - up,) if hops > up else ())
    parts = []
    for part in range(PARTS):
        v = gathered(0, part, half, 0)
        for way, q, hops in flows:
            if q == part:
                v = v + children(way, part, hops, 0)
        parts.append(v)
    sums = jnp.concatenate(parts, axis=1)
    len_x[d] = jnp.sum(sums * sums, axis=0, keepdims=True)

    def drain():
        for ref, sem in ((ct.at[pl.ds(0, (2 * nz - 1) * own)], g_send), (sib, sx_send),
                         (sib.at[pl.ds(0, nz - 1)], r_send)):
            pltpu.make_async_remote_copy(
                src_ref=ref, dst_ref=ref, send_sem=sem, recv_sem=sem,
                device_id={"dp": other}, device_id_type=MESH).wait_send()
        for desc in pending:
            desc.wait_send()
        pending.clear()

    lengths = exchange(len_x, lx_sem, d, dp_ids, drain=drain)
    out[...] = sums * (1.0 / jnp.sqrt(lengths + 1e-06))
    mass_second.wait_recv()
    mass_out[...] = n_cent * cv * total(mass_b, level_ids)


def hand_over(sums, mass, sums_out, mass_out, sems):
    copies = [pltpu.make_async_copy(sums, sums_out, sems.at[0]), pltpu.make_async_copy(mass, mass_out, sems.at[1])]
    for copy in copies:
        copy.start()
    for copy in copies:
        copy.wait()


def solution(mesh):
    n_dp, n_proto = mesh.shape["dp"], mesh.shape["proto"]
    nz = n_dp // 2
    half = nz // 2
    levels = n_dp // GROUP

    def per_device(embeddings, centroids):
        rows, feat = embeddings.shape
        cent = centroids.shape[0]
        own = feat // n_dp
        dma, vmem = pltpu.SemaphoreType.DMA, pltpu.VMEM
        whole, anywhere = pl.BlockSpec(memory_space=pltpu.VMEM), pl.BlockSpec(memory_space=pl.ANY)
        shapes = (jax.ShapeDtypeStruct((own, cent), F32), jax.ShapeDtypeStruct((1, cent), F32))
        sums, mass = pl.pallas_call(
            functools.partial(kernel, (n_dp, n_proto, rows, feat, cent)),
            out_shape=shapes,
            in_specs=[anywhere, whole],
            out_specs=(whole, whole),
            scratch_shapes=[
                vmem((rows, feat), BF16),
                vmem((feat, rows), BF16),
                vmem((feat, cent), BF16),
                vmem((rows, cent), F32),
                vmem((rows, cent), BF16),
                vmem((nz, 2 * own, cent), F32),
                vmem((SWEEPS, n_dp, 1, cent), F32),
                vmem((SWEEPS, n_proto, 3, 4, LANES), F32),
                vmem((GROUP, 1, cent), F32),
                vmem((levels, 1, cent), F32),
                vmem((n_dp, 1, cent), F32),
                vmem((nz, own, cent), F32),
                vmem((2, PARTS, half, own, cent // PARTS), F32),
                vmem((2, PARTS, half, own, cent // PARTS), F32),
                dma,
                dma, dma((2, half // 2, SUBS + 1)), dma((nz,)),
                dma((SWEEPS, 2)), dma((SWEEPS, 2)), dma((2,)), dma((2,)), dma((2,)),
                dma, dma((nz,)), dma, dma((2, PARTS, half)),
            ],
            compiler_params=pltpu.CompilerParams(
                collective_id=0, has_side_effects=True, vmem_limit_bytes=56 * 1024 * 1024),
            cost_estimate=pl.CostEstimate(
                flops=4 * rows * feat * cent, bytes_accessed=2 * rows * feat, transcendentals=rows * cent),
        )(embeddings, centroids.T)
        new_centroids, mass = pl.pallas_call(
            hand_over, out_shape=shapes, in_specs=[anywhere, anywhere], out_specs=(anywhere, anywhere),
            scratch_shapes=[dma((2,))])(sums, mass)
        return new_centroids, mass.reshape(cent)

    return jax.shard_map(
        per_device,
        mesh=mesh,
        in_specs=(P("dp", None), P("proto", "dp")),
        out_specs=(P("dp", "proto"), P("proto")),
        check_vma=False,
    )
```

```python
import functools

import jax
import jax.numpy as jnp
from jax import lax
from jax.experimental import pallas as pl
from jax.experimental.pallas import tpu as pltpu
from jax.sharding import PartitionSpec as P

SWEEPS = 3
LOGIT_SCALE = 40.0
F32, BF16 = jnp.float32, jnp.bfloat16
MESH = pl.DeviceIdType.MESH
GROUP = 8
SUBS = 3
PARTS = 4
JOINS = 2
UNIT = 64
LANES = 128


def dot(a, b, dims):
    return lax.dot_general(a, b, (dims, ((), ())), preferred_element_type=F32)


def kernel(sizes, emb, cen, out, mass_out, x, ut, ct, e, w, s, col_x, row_x, mass_a, mass_b, len_x, sib, leave, ring,
           sem_in, g_send, g_recv, gs_recv, cx_sem, rx_sem, ma_sem, mb_sem, lx_sem,
           sx_send, sx_recv, r_send, r_recv):
    n_dp, n_proto, rows, feat, cent = sizes
    nz = n_dp // 2
    half = nz // 2
    own = feat // n_dp
    n_rows = rows * n_dp
    n_cent = cent * n_proto
    levels = n_dp // GROUP

    d = lax.axis_index("dp")
    p = lax.axis_index("proto")
    z, c = d // 2, d % 2
    other = d + 1 - 2 * c
    right = ((z + 1) % nz) * 2 + c
    left = ((z + nz - 1) % nz) * 2 + c
    near = (right, left)
    far = ((d + 4) % n_dp, (d + n_dp - 4) % n_dp)
    in_group = d % GROUP
    level = d // GROUP
    group_ids = [{"dp": level * GROUP + (in_group + j) % GROUP} for j in range(1, GROUP)]
    level_ids = [{"dp": (d + GROUP * j) % n_dp} for j in range(1, levels)]
    dp_ids = [{"dp": (d + j) % n_dp} for j in sorted(range(1, n_dp), key=lambda j: -min(j, n_dp - j))]
    side = int(n_proto**0.5)
    moves = [(a, b) for a in range(side) for b in range(side) if a or b]
    moves.sort(key=lambda m: -sum(min(k, side - k) for k in m))
    proto_ids = [{"proto": (p // side + a) % side * side + (p % side + b) % side} for a, b in moves]

    load = pltpu.make_async_copy(emb, x, sem_in)
    load.start()

    barrier = pltpu.get_barrier_semaphore()
    partners = dp_ids[::-1] + proto_ids
    for t in partners:
        pl.semaphore_signal(barrier, inc=1, device_id=t, device_id_type=MESH)

    def block_rows(o, core):
        return pl.ds(pl.multiple_of((o * 2 + core) * own, own), own)

    ct[block_rows(z, c), :] = cen[...]
    pl.semaphore_wait(barrier, len(partners))

    piece = own // SUBS
    stages = half // 2

    def far_hop(o, way, stage, sub):
        at = ct.at[pl.ds(pl.multiple_of((o * 2 + c) * own + sub * piece, piece), piece)]
        return pltpu.make_async_remote_copy(
            src_ref=at, dst_ref=at, send_sem=g_send, recv_sem=g_recv.at[way, stage, sub],
            device_id={"dp": far[way]}, device_id_type=MESH)

    def near_hop(o, way, stage):
        at = ct.at[block_rows(o, c)]
        return pltpu.make_async_remote_copy(
            src_ref=at, dst_ref=at, send_sem=g_send, recv_sem=g_recv.at[way, stage, SUBS],
            device_id={"dp": near[way]}, device_id_type=MESH)

    def source(way, distance):
        return (z - distance + nz) % nz if way == 0 else (z + distance) % nz

    def across(o, slot):
        at = ct.at[block_rows(o, c)]
        return pltpu.make_async_remote_copy(
            src_ref=at, dst_ref=at, send_sem=g_send, recv_sem=gs_recv.at[slot],
            device_id={"dp": other}, device_id_type=MESH)

    pending = []

    def launch(desc):
        desc.start()

    for sub in range(SUBS):
        for way in (0, 1):
            launch(far_hop(z, way, 0, sub))
    for way in (0, 1):
        launch(near_hop(z, way, 0))
    launch(across(z, 0))

    def square(o, core):
        v = ct[block_rows(o, core), :].astype(F32)
        return jnp.sum((v * v).reshape(own // 8, 8, cent), axis=0)

    load.wait()
    tile, short = 256, 128
    eye = (
        lax.broadcasted_iota(jnp.int32, (tile, tile), 0) == lax.broadcasted_iota(jnp.int32, (tile, tile), 1)
    ).astype(BF16)

    def prepare(b):
        at = pl.ds(b * short, short)
        v = x[at, :].astype(F32)
        u = (v * (1.0 / jnp.sqrt(jnp.sum(v * v, axis=1, keepdims=True) + 1e-06))).astype(BF16)
        x[at, :] = u

    def turn(b):
        at = pl.ds(b * short, short)
        for f in range(feat // tile):
            ut[pl.ds(f * tile, tile), at] = dot(
                eye, x[at, f * tile:(f + 1) * tile], ((1,), (1,))).astype(BF16)

    squares = square(z, c)
    behind = [(z, 0)]
    unit = 0
    for stage in range(stages):
        came = []
        for _ in range(rows // short // stages):
            prepare(unit)
            unit += 1
        for sub in range(SUBS):
            for way in (0, 1):
                if stage == stages - 1 and way == 1:
                    continue
                o = source(way, 2 * stage + 2)
                far_hop(o, way, stage, sub).wait_recv()
                if stage < stages - 1 and (stage < stages - 2 or way == 0):
                    launch(far_hop(o, way, stage + 1, sub))
                if sub == SUBS - 1:
                    if stage < stages - 1:
                        launch(near_hop(o, way, stage + 1))
                    launch(across(o, 2 + 4 * stage + way))
                    came.append((o, 2 + 4 * stage + way))
        for way in (0, 1):
            o = source(way, 2 * stage + 1)
            near_hop(o, way, stage).wait_recv()
            slot = 4 * stage + 4 + way if stage < stages - 1 else (1, 2 * half - 1)[way]
            launch(across(o, slot))
            came.append((o, slot))
        for o, slot in behind:
            across(o, slot).wait_recv()
            squares = squares + square(o, 1 - c)
        for o, slot in came:
            squares = squares + square(o, c)
        behind = came
    for o, slot in behind:
        across(o, slot).wait_recv()
        squares = squares + square(o, 1 - c)

    scale = LOGIT_SCALE * (1.0 / jnp.sqrt(jnp.sum(squares, axis=0, keepdims=True) + 1e-06))
    m_tile = rows // 4

    def product(b):
        return dot(x[b * m_tile:(b + 1) * m_tile, :], ct[...], ((1,), (0,)))

    acc = jnp.zeros((8, cent), F32)
    raw = product(0)
    for b in range(4):
        ahead = product(b + 1) if b < 3 else None
        v = jnp.exp(raw * scale)
        e[b * m_tile:(b + 1) * m_tile, :] = v
        acc = acc + jnp.sum(v.reshape(m_tile // 8, 8, cent), axis=0)
        raw = ahead

    def send_all(buf, sem, me, ids):
        for t in ids:
            pltpu.make_async_remote_copy(
                src_ref=buf.at[me], dst_ref=buf.at[me], send_sem=sem.at[0], recv_sem=sem.at[1],
                device_id=t, device_id_type=MESH).start()
        whole = buf.at[pl.ds(0, len(ids))]
        done = pltpu.make_async_remote_copy(
            src_ref=whole, dst_ref=whole, send_sem=sem.at[0], recv_sem=sem.at[1],
            device_id=ids[0], device_id_type=MESH)
        pending.append(done)
        return done

    def total(buf, ids):
        terms = [buf[k] for k in range(len(ids) + 1)]
        while len(terms) > 1:
            terms = [terms[k] + terms[k + 1] for k in range(0, len(terms), 2)]
        return terms[0]

    def exchange(buf, sem, me, ids, units=(), drain=None):
        done = send_all(buf, sem, me, ids)
        for b in units:
            turn(b)
        if drain:
            drain()
        done.wait_recv()
        return total(buf, ids)

    lane = lax.broadcasted_iota(jnp.int32, (8, LANES), 1)
    tiles = [(0, LANES), (LANES, rows // 8)]

    per_sweep = rows // short // SWEEPS
    for i in range(SWEEPS):
        turns = range(i * per_sweep, (i + 1) * per_sweep)
        col_x[i, d] = jnp.sum(acc, axis=0, keepdims=True)
        cv = 1.0 / (n_cent * exchange(col_x.at[i], cx_sem.at[i], d, dp_ids, turns[0:2]))
        cb = jnp.broadcast_to(cv, (8, cent))

        totals = []
        for lo, hi in tiles:
            def row_step(g, t):
                for k in range(UNIT):
                    q = e[pl.ds(pl.multiple_of((lo + g * UNIT + k) * 8, 8), 8), :] * cb
                    q = functools.reduce(
                        lambda a, b: a + b, [q[:, m * LANES:(m + 1) * LANES] for m in range(cent // LANES)])
                    t = jnp.where(lane == g * UNIT + k, jnp.sum(q, axis=1, keepdims=True), t)
                return t

            totals.append(lax.fori_loop(0, (hi - lo) // UNIT, row_step, jnp.zeros((8, LANES), F32)))
        row_x[i, p, 0] = totals[0][0:4]
        row_x[i, p, 1] = totals[0][4:8]
        row_x[i, p, 2] = totals[1][0:4] + pltpu.roll(totals[1], LANES // 2, 1)[4:8]
        rv = 1.0 / (n_rows * exchange(row_x.at[i], rx_sem.at[i], p, proto_ids, turns[2:]))
        r0 = jnp.concatenate([rv[0], rv[1]], axis=0)
        r1 = jnp.concatenate([rv[2], pltpu.roll(rv[2], LANES // 2, 1)], axis=0)

        final = i == SWEEPS - 1
        nc = jnp.broadcast_to(n_rows * cv, (8, cent))
        acc = jnp.zeros((8, cent), F32)
        for (lo, hi), r in zip(tiles, (r0, r1)):
            def col_step(g, st):
                a, r = st
                for k in range(0, UNIT, 2):
                    at = pl.multiple_of((lo + g * UNIT + k) * 8, 16)
                    pair = [e[pl.ds(at + 8 * m, 8), :] * jnp.broadcast_to(r[:, k + m:k + m + 1], (8, cent))
                            for m in range(2)]
                    a = a + pair[0] + pair[1]
                    if final:
                        w[pl.ds(at, 16), :] = jnp.concatenate([v * nc for v in pair], axis=0).astype(BF16)
                return a, pltpu.roll(r, LANES - UNIT, 1)

            acc, _ = lax.fori_loop(0, (hi - lo) // UNIT, col_step, (acc, r))

    def swap(rel):
        return pltpu.make_async_remote_copy(
            src_ref=s.at[rel, pl.ds(pl.multiple_of((1 - c) * own, own), own)], dst_ref=sib.at[rel],
            send_sem=sx_send, recv_sem=sx_recv.at[rel],
            device_id={"dp": other}, device_id_type=MESH)

    def make_sums(rels):
        u = [ut[pl.ds(pl.multiple_of(((z + rel) % nz) * 2 * own, 2 * own), 2 * own), :] for rel in rels]
        v = dot(jnp.concatenate(u, axis=0) if len(u) > 1 else u[0], w[...], ((1,), (0,)))
        for k, rel in enumerate(rels):
            s[rel] = v[k * 2 * own:(k + 1) * 2 * own]
            launch(swap(rel))

    wide = cent // PARTS
    flows = []
    for hops in (half, half - 1):
        for m in range(PARTS // 2):
            for way in (0, 1):
                first = way == (0 if hops == half else 1)
                flows.append((way, m if first else PARTS // 2 + m, hops))

    def parent(q, hops):
        up = (hops - q) // 2
        return hops - 2 * up - 2 if up < JOINS else q - 1

    def link(way, part, hops, q):
        step = q - parent(q, hops)
        return pltpu.make_async_remote_copy(
            src_ref=leave.at[way, part, q - 1], dst_ref=ring.at[way, part, q - 1],
            send_sem=r_send, recv_sem=r_recv.at[way, part, q - 1],
            device_id={"dp": (near if step == 1 else far)[way]}, device_id_type=MESH)

    own_rows = pl.ds(pl.multiple_of(c * own, own), own)
    ready = set()

    def gathered(way, part, hops, q):
        rel = (q if way == 0 else nz - q) % nz
        if rel not in ready:
            swap(rel).wait_recv()
            ready.add(rel)
        cols = pl.ds(part * wide, wide)
        v = s[rel, own_rows, cols] + sib[rel, :, cols]
        return v + children(way, part, hops, q) if q else v

    def children(way, part, hops, q):
        v = 0.0
        for child in range(1, hops + 1):
            if parent(child, hops) == q:
                link(way, part, hops, child).wait_recv()
                v = v + ring[way, part, child - 1]
        return v

    def pass_on(distances):
        for way, part, hops in flows:
            for q in distances(hops):
                leave[way, part, q - 1] = gathered(way, part, hops, q)
                launch(link(way, part, hops, q))

    mass_a[in_group] = jnp.sum(acc, axis=0, keepdims=True)
    mass_first = send_all(mass_a, ma_sem, in_group, group_ids)
    make_sums([half])
    make_sums([half - 1, half + 1])
    make_sums([half - 2, half + 2])
    make_sums([half - 3, half + 3])
    make_sums([half - 4, half + 4])
    pass_on(lambda hops: (hops, hops - 1))
    pass_on(lambda hops: (hops - 3,))
    mass_first.wait_recv()
    mass_b[level] = total(mass_a, group_ids)
    mass_second = send_all(mass_b, mb_sem, level, level_ids)
    make_sums([half - 5, half + 5])
    make_sums([half - 6, half + 6])
    pass_on(lambda hops: (hops - 2,))
    make_sums([half - 7, half + 7])
    make_sums([0])
    for up in range(4, half):
        pass_on(lambda hops: (hops - up,) if hops > up else ())
    parts = []
    for part in range(PARTS):
        v = gathered(0, part, half, 0)
        for way, q, hops in flows:
            if q == part:
                v = v + children(way, part, hops, 0)
        parts.append(v)
    sums = jnp.concatenate(parts, axis=1)
    len_x[d] = jnp.sum(sums * sums, axis=0, keepdims=True)

    def drain():
        for ref, sem in ((ct.at[pl.ds(0, (2 * nz - 1) * own)], g_send), (sib, sx_send),
                         (sib.at[pl.ds(0, nz - 1)], r_send)):
            pltpu.make_async_remote_copy(
                src_ref=ref, dst_ref=ref, send_sem=sem, recv_sem=sem,
                device_id={"dp": other}, device_id_type=MESH).wait_send()
        for desc in pending:
            desc.wait_send()
        pending.clear()

    lengths = exchange(len_x, lx_sem, d, dp_ids, drain=drain)
    out[...] = sums * (1.0 / jnp.sqrt(lengths + 1e-06))
    mass_second.wait_recv()
    mass_out[...] = n_cent * cv * total(mass_b, level_ids)


def hand_over(sums, mass, sums_out, mass_out):
    sums_out[...] = sums[...]
    mass_out[...] = mass[...]


def solution(mesh):
    n_dp, n_proto = mesh.shape["dp"], mesh.shape["proto"]
    nz = n_dp // 2
    half = nz // 2
    levels = n_dp // GROUP

    def per_device(embeddings, centroids):
        rows, feat = embeddings.shape
        cent = centroids.shape[0]
        own = feat // n_dp
        dma, vmem = pltpu.SemaphoreType.DMA, pltpu.VMEM
        whole, anywhere = pl.BlockSpec(memory_space=pltpu.VMEM), pl.BlockSpec(memory_space=pl.ANY)
        shapes = (jax.ShapeDtypeStruct((own, cent), F32), jax.ShapeDtypeStruct((1, cent), F32))
        sums, mass = pl.pallas_call(
            functools.partial(kernel, (n_dp, n_proto, rows, feat, cent)),
            out_shape=shapes,
            in_specs=[anywhere, whole],
            out_specs=(whole, whole),
            scratch_shapes=[
                vmem((rows, feat), BF16),
                vmem((feat, rows), BF16),
                vmem((feat, cent), BF16),
                vmem((rows, cent), F32),
                vmem((rows, cent), BF16),
                vmem((nz, 2 * own, cent), F32),
                vmem((SWEEPS, n_dp, 1, cent), F32),
                vmem((SWEEPS, n_proto, 3, 4, LANES), F32),
                vmem((GROUP, 1, cent), F32),
                vmem((levels, 1, cent), F32),
                vmem((n_dp, 1, cent), F32),
                vmem((nz, own, cent), F32),
                vmem((2, PARTS, half, own, cent // PARTS), F32),
                vmem((2, PARTS, half, own, cent // PARTS), F32),
                dma,
                dma, dma((2, half // 2, SUBS + 1)), dma((nz,)),
                dma((SWEEPS, 2)), dma((SWEEPS, 2)), dma((2,)), dma((2,)), dma((2,)),
                dma, dma((nz,)), dma, dma((2, PARTS, half)),
            ],
            compiler_params=pltpu.CompilerParams(
                collective_id=0, has_side_effects=True, vmem_limit_bytes=56 * 1024 * 1024),
            cost_estimate=pl.CostEstimate(
                flops=4 * rows * feat * cent, bytes_accessed=2 * rows * feat, transcendentals=rows * cent),
        )(embeddings, centroids.T)
        new_centroids, mass = pl.pallas_call(
            hand_over, out_shape=shapes, in_specs=[whole, whole], out_specs=(whole, whole))(sums, mass)
        return new_centroids, mass.reshape(cent)

    return jax.shard_map(
        per_device,
        mesh=mesh,
        in_specs=(P("dp", None), P("proto", "dp")),
        out_specs=(P("dp", "proto"), P("proto")),
        check_vma=False,
    )
```

```python
import functools

import jax
import jax.numpy as jnp
from jax import lax
from jax.experimental import pallas as pl
from jax.experimental.pallas import tpu as pltpu
from jax.sharding import PartitionSpec as P

SWEEPS = 3
LOGIT_SCALE = 40.0
F32, BF16 = jnp.float32, jnp.bfloat16
MESH = pl.DeviceIdType.MESH
GROUP = 8
SUBS = 3
PARTS = 4
JOINS = 3
UNIT = 64
LANES = 128


def dot(a, b, dims):
    return lax.dot_general(a, b, (dims, ((), ())), preferred_element_type=F32)


def kernel(sizes, emb, cen, out, mass_out, x, ut, ct, e, w, s, col_x, row_x, mass_a, mass_b, len_x, sib, leave, ring,
           sem_in, g_send, g_recv, gs_recv, cx_sem, rx_sem, ma_sem, mb_sem, lx_sem,
           sx_send, sx_recv, r_send, r_recv):
    n_dp, n_proto, rows, feat, cent = sizes
    nz = n_dp // 2
    half = nz // 2
    own = feat // n_dp
    n_rows = rows * n_dp
    n_cent = cent * n_proto
    levels = n_dp // GROUP

    d = lax.axis_index("dp")
    p = lax.axis_index("proto")
    z, c = d // 2, d % 2
    other = d + 1 - 2 * c
    right = ((z + 1) % nz) * 2 + c
    left = ((z + nz - 1) % nz) * 2 + c
    near = (right, left)
    far = ((d + 4) % n_dp, (d + n_dp - 4) % n_dp)
    in_group = d % GROUP
    level = d // GROUP
    group_ids = [{"dp": level * GROUP + (in_group + j) % GROUP} for j in range(1, GROUP)]
    level_ids = [{"dp": (d + GROUP * j) % n_dp} for j in range(1, levels)]
    dp_ids = [{"dp": (d + j) % n_dp} for j in sorted(range(1, n_dp), key=lambda j: -min(j, n_dp - j))]
    side = int(n_proto**0.5)
    moves = [(a, b) for a in range(side) for b in range(side) if a or b]
    moves.sort(key=lambda m: -sum(min(k, side - k) for k in m))
    proto_ids = [{"proto": (p // side + a) % side * side + (p % side + b) % side} for a, b in moves]

    load = pltpu.make_async_copy(emb, x, sem_in)
    load.start()

    barrier = pltpu.get_barrier_semaphore()
    partners = [{"dp": t} for t in near + far + (other,)] + proto_ids
    for t in partners:
        pl.semaphore_signal(barrier, inc=1, device_id=t, device_id_type=MESH)

    def block_rows(o, core):
        return pl.ds(pl.multiple_of((o * 2 + core) * own, own), own)

    ct[block_rows(z, c), :] = cen[...]
    pl.semaphore_wait(barrier, len(partners))

    piece = own // SUBS
    stages = half // 2

    def far_hop(o, way, stage, sub):
        at = ct.at[pl.ds(pl.multiple_of((o * 2 + c) * own + sub * piece, piece), piece)]
        return pltpu.make_async_remote_copy(
            src_ref=at, dst_ref=at, send_sem=g_send, recv_sem=g_recv.at[way, stage, sub],
            device_id={"dp": far[way]}, device_id_type=MESH)

    def near_hop(o, way, stage):
        at = ct.at[block_rows(o, c)]
        return pltpu.make_async_remote_copy(
            src_ref=at, dst_ref=at, send_sem=g_send, recv_sem=g_recv.at[way, stage, SUBS],
            device_id={"dp": near[way]}, device_id_type=MESH)

    def source(way, distance):
        return (z - distance + nz) % nz if way == 0 else (z + distance) % nz

    def across(o, slot):
        at = ct.at[block_rows(o, c)]
        return pltpu.make_async_remote_copy(
            src_ref=at, dst_ref=at, send_sem=g_send, recv_sem=gs_recv.at[slot],
            device_id={"dp": other}, device_id_type=MESH)

    pending = []

    def launch(desc):
        desc.start()

    for sub in range(SUBS):
        for way in (0, 1):
            launch(far_hop(z, way, 0, sub))
    for way in (0, 1):
        launch(near_hop(z, way, 0))
    launch(across(z, 0))

    def square(o, core):
        v = ct[block_rows(o, core), :].astype(F32)
        return jnp.sum((v * v).reshape(own // 8, 8, cent), axis=0)

    load.wait()
    tile, short = 256, 128
    eye = (
        lax.broadcasted_iota(jnp.int32, (tile, tile), 0) == lax.broadcasted_iota(jnp.int32, (tile, tile), 1)
    ).astype(BF16)

    def prepare(b):
        at = pl.ds(b * short, short)
        v = x[at, :].astype(F32)
        u = (v * (1.0 / jnp.sqrt(jnp.sum(v * v, axis=1, keepdims=True) + 1e-06))).astype(BF16)
        x[at, :] = u

    def turn(b):
        at = pl.ds(b * short, short)
        for f in range(feat // tile):
            ut[pl.ds(f * tile, tile), at] = dot(
                eye, x[at, f * tile:(f + 1) * tile], ((1,), (1,))).astype(BF16)

    squares = square(z, c)
    behind = [(z, 0)]
    unit = 0
    for stage in range(stages):
        came = []
        for _ in range(rows // short // stages):
            prepare(unit)
            unit += 1
        for sub in range(SUBS):
            for way in (0, 1):
                if stage == stages - 1 and way == 1:
                    continue
                o = source(way, 2 * stage + 2)
                far_hop(o, way, stage, sub).wait_recv()
                if stage < stages - 1 and (stage < stages - 2 or way == 0):
                    launch(far_hop(o, way, stage + 1, sub))
                if sub == SUBS - 1:
                    if stage < stages - 1:
                        launch(near_hop(o, way, stage + 1))
                    launch(across(o, 2 + 4 * stage + way))
                    came.append((o, 2 + 4 * stage + way))
        for way in (0, 1):
            o = source(way, 2 * stage + 1)
            near_hop(o, way, stage).wait_recv()
            slot = 4 * stage + 4 + way if stage < stages - 1 else (1, 2 * half - 1)[way]
            launch(across(o, slot))
            came.append((o, slot))
        for o, slot in behind:
            across(o, slot).wait_recv()
            squares = squares + square(o, 1 - c)
        for o, slot in came:
            squares = squares + square(o, c)
        behind = came
    for o, slot in behind:
        across(o, slot).wait_recv()
        squares = squares + square(o, 1 - c)

    scale = LOGIT_SCALE * (1.0 / jnp.sqrt(jnp.sum(squares, axis=0, keepdims=True) + 1e-06))
    m_tile = rows // 4

    def product(b):
        return dot(x[b * m_tile:(b + 1) * m_tile, :], ct[...], ((1,), (0,)))

    acc = jnp.zeros((8, cent), F32)
    raw = product(0)
    for b in range(4):
        ahead = product(b + 1) if b < 3 else None
        v = jnp.exp(raw * scale)
        e[b * m_tile:(b + 1) * m_tile, :] = v
        acc = acc + jnp.sum(v.reshape(m_tile // 8, 8, cent), axis=0)
        raw = ahead

    def send_all(buf, sem, me, ids):
        for t in ids:
            pltpu.make_async_remote_copy(
                src_ref=buf.at[me], dst_ref=buf.at[me], send_sem=sem.at[0], recv_sem=sem.at[1],
                device_id=t, device_id_type=MESH).start()
        whole = buf.at[pl.ds(0, len(ids))]
        done = pltpu.make_async_remote_copy(
            src_ref=whole, dst_ref=whole, send_sem=sem.at[0], recv_sem=sem.at[1],
            device_id=ids[0], device_id_type=MESH)
        pending.append(done)
        return done

    def total(buf, ids):
        terms = [buf[k] for k in range(len(ids) + 1)]
        while len(terms) > 1:
            terms = [terms[k] + terms[k + 1] for k in range(0, len(terms), 2)]
        return terms[0]

    def exchange(buf, sem, me, ids, units=(), drain=None):
        done = send_all(buf, sem, me, ids)
        for b in units:
            turn(b)
        if drain:
            drain()
        done.wait_recv()
        return total(buf, ids)

    lane = lax.broadcasted_iota(jnp.int32, (8, LANES), 1)
    tiles = [(0, LANES), (LANES, rows // 8)]

    per_sweep = rows // short // SWEEPS
    for i in range(SWEEPS):
        turns = range(i * per_sweep, (i + 1) * per_sweep)
        col_x[i, d] = jnp.sum(acc, axis=0, keepdims=True)
        cv = 1.0 / (n_cent * exchange(col_x.at[i], cx_sem.at[i], d, dp_ids, turns[0:2]))
        cb = jnp.broadcast_to(cv, (8, cent))

        totals = []
        for lo, hi in tiles:
            def row_step(g, t):
                for k in range(UNIT):
                    q = e[pl.ds(pl.multiple_of((lo + g * UNIT + k) * 8, 8), 8), :] * cb
                    q = functools.reduce(
                        lambda a, b: a + b, [q[:, m * LANES:(m + 1) * LANES] for m in range(cent // LANES)])
                    t = jnp.where(lane == g * UNIT + k, jnp.sum(q, axis=1, keepdims=True), t)
                return t

            totals.append(lax.fori_loop(0, (hi - lo) // UNIT, row_step, jnp.zeros((8, LANES), F32)))
        row_x[i, p, 0] = totals[0][0:4]
        row_x[i, p, 1] = totals[0][4:8]
        row_x[i, p, 2] = totals[1][0:4] + pltpu.roll(totals[1], LANES // 2, 1)[4:8]
        rv = 1.0 / (n_rows * exchange(row_x.at[i], rx_sem.at[i], p, proto_ids, turns[2:]))
        r0 = jnp.concatenate([rv[0], rv[1]], axis=0)
        r1 = jnp.concatenate([rv[2], pltpu.roll(rv[2], LANES // 2, 1)], axis=0)

        final = i == SWEEPS - 1
        nc = jnp.broadcast_to(n_rows * cv, (8, cent))
        acc = jnp.zeros((8, cent), F32)
        for (lo, hi), r in zip(tiles, (r0, r1)):
            def col_step(g, st):
                a, r = st
                for k in range(0, UNIT, 2):
                    at = pl.multiple_of((lo + g * UNIT + k) * 8, 16)
                    pair = [e[pl.ds(at + 8 * m, 8), :] * jnp.broadcast_to(r[:, k + m:k + m + 1], (8, cent))
                            for m in range(2)]
                    a = a + pair[0] + pair[1]
                    if final:
                        w[pl.ds(at, 16), :] = jnp.concatenate([v * nc for v in pair], axis=0).astype(BF16)
                return a, pltpu.roll(r, LANES - UNIT, 1)

            acc, _ = lax.fori_loop(0, (hi - lo) // UNIT, col_step, (acc, r))

    def swap(rel):
        return pltpu.make_async_remote_copy(
            src_ref=s.at[rel, pl.ds(pl.multiple_of((1 - c) * own, own), own)], dst_ref=sib.at[rel],
            send_sem=sx_send, recv_sem=sx_recv.at[rel],
            device_id={"dp": other}, device_id_type=MESH)

    def make_sums(rels):
        u = [ut[pl.ds(pl.multiple_of(((z + rel) % nz) * 2 * own, 2 * own), 2 * own), :] for rel in rels]
        v = dot(jnp.concatenate(u, axis=0) if len(u) > 1 else u[0], w[...], ((1,), (0,)))
        for k, rel in enumerate(rels):
            s[rel] = v[k * 2 * own:(k + 1) * 2 * own]
            launch(swap(rel))

    wide = cent // PARTS
    flows = []
    for hops in (half, half - 1):
        for m in range(PARTS // 2):
            for way in (0, 1):
                first = way == (0 if hops == half else 1)
                flows.append((way, m if first else PARTS // 2 + m, hops))

    def parent(q, hops):
        up = (hops - q) // 2
        return hops - 2 * up - 2 if up < JOINS else q - 1

    def link(way, part, hops, q):
        step = q - parent(q, hops)
        return pltpu.make_async_remote_copy(
            src_ref=leave.at[way, part, q - 1], dst_ref=ring.at[way, part, q - 1],
            send_sem=r_send, recv_sem=r_recv.at[way, part, q - 1],
            device_id={"dp": (near if step == 1 else far)[way]}, device_id_type=MESH)

    own_rows = pl.ds(pl.multiple_of(c * own, own), own)
    ready = set()

    def gathered(way, part, hops, q):
        rel = (q if way == 0 else nz - q) % nz
        if rel not in ready:
            swap(rel).wait_recv()
            ready.add(rel)
        cols = pl.ds(part * wide, wide)
        v = s[rel, own_rows, cols] + sib[rel, :, cols]
        return v + children(way, part, hops, q) if q else v

    def children(way, part, hops, q):
        v = 0.0
        for child in range(1, hops + 1):
            if parent(child, hops) == q:
                link(way, part, hops, child).wait_recv()
                v = v + ring[way, part, child - 1]
        return v

    def pass_on(distances):
        for way, part, hops in flows:
            for q in distances(hops):
                leave[way, part, q - 1] = gathered(way, part, hops, q)
                launch(link(way, part, hops, q))

    mass_a[in_group] = jnp.sum(acc, axis=0, keepdims=True)
    mass_first = send_all(mass_a, ma_sem, in_group, group_ids)
    make_sums([half])
    make_sums([half - 1, half + 1])
    make_sums([half - 2, half + 2])
    make_sums([half - 3, half + 3])
    make_sums([half - 4, half + 4])
    pass_on(lambda hops: (hops, hops - 1))
    pass_on(lambda hops: (hops - 3,))
    mass_first.wait_recv()
    mass_b[level] = total(mass_a, group_ids)
    mass_second = send_all(mass_b, mb_sem, level, level_ids)
    make_sums([half - 5, half + 5])
    make_sums([half - 6, half + 6])
    pass_on(lambda hops: (hops - 2,))
    pass_on(lambda hops: (hops - 5,))
    make_sums([half - 7, half + 7])
    make_sums([0])
    for up in (4, 6, 7):
        pass_on(lambda hops: (hops - up,) if hops > up else ())
    parts = []
    for part in range(PARTS):
        v = gathered(0, part, half, 0)
        for way, q, hops in flows:
            if q == part:
                v = v + children(way, part, hops, 0)
        parts.append(v)
    sums = jnp.concatenate(parts, axis=1)
    len_x[d] = jnp.sum(sums * sums, axis=0, keepdims=True)

    def drain():
        for ref, sem in ((ct.at[pl.ds(0, (2 * nz - 1) * own)], g_send), (sib, sx_send),
                         (sib.at[pl.ds(0, nz - 1)], r_send)):
            pltpu.make_async_remote_copy(
                src_ref=ref, dst_ref=ref, send_sem=sem, recv_sem=sem,
                device_id={"dp": other}, device_id_type=MESH).wait_send()
        for desc in pending:
            desc.wait_send()
        pending.clear()

    lengths = exchange(len_x, lx_sem, d, dp_ids, drain=drain)
    out[...] = sums * (1.0 / jnp.sqrt(lengths + 1e-06))
    mass_second.wait_recv()
    mass_out[...] = n_cent * cv * total(mass_b, level_ids)


def hand_over(sums, mass, sums_out, mass_out):
    sums_out[...] = sums[...]
    mass_out[...] = mass[...]


def solution(mesh):
    n_dp, n_proto = mesh.shape["dp"], mesh.shape["proto"]
    nz = n_dp // 2
    half = nz // 2
    levels = n_dp // GROUP

    def per_device(embeddings, centroids):
        rows, feat = embeddings.shape
        cent = centroids.shape[0]
        own = feat // n_dp
        dma, vmem = pltpu.SemaphoreType.DMA, pltpu.VMEM
        whole, anywhere = pl.BlockSpec(memory_space=pltpu.VMEM), pl.BlockSpec(memory_space=pl.ANY)
        shapes = (jax.ShapeDtypeStruct((own, cent), F32), jax.ShapeDtypeStruct((1, cent), F32))
        sums, mass = pl.pallas_call(
            functools.partial(kernel, (n_dp, n_proto, rows, feat, cent)),
            out_shape=shapes,
            in_specs=[anywhere, whole],
            out_specs=(whole, whole),
            scratch_shapes=[
                vmem((rows, feat), BF16),
                vmem((feat, rows), BF16),
                vmem((feat, cent), BF16),
                vmem((rows, cent), F32),
                vmem((rows, cent), BF16),
                vmem((nz, 2 * own, cent), F32),
                vmem((SWEEPS, n_dp, 1, cent), F32),
                vmem((SWEEPS, n_proto, 3, 4, LANES), F32),
                vmem((GROUP, 1, cent), F32),
                vmem((levels, 1, cent), F32),
                vmem((n_dp, 1, cent), F32),
                vmem((nz, own, cent), F32),
                vmem((2, PARTS, half, own, cent // PARTS), F32),
                vmem((2, PARTS, half, own, cent // PARTS), F32),
                dma,
                dma, dma((2, half // 2, SUBS + 1)), dma((nz,)),
                dma((SWEEPS, 2)), dma((SWEEPS, 2)), dma((2,)), dma((2,)), dma((2,)),
                dma, dma((nz,)), dma, dma((2, PARTS, half)),
            ],
            compiler_params=pltpu.CompilerParams(
                collective_id=0, has_side_effects=True, vmem_limit_bytes=56 * 1024 * 1024),
            cost_estimate=pl.CostEstimate(
                flops=4 * rows * feat * cent, bytes_accessed=2 * rows * feat, transcendentals=rows * cent),
        )(embeddings, centroids.T)
        new_centroids, mass = pl.pallas_call(
            hand_over, out_shape=shapes, in_specs=[whole, whole], out_specs=(whole, whole))(sums, mass)
        return new_centroids, mass.reshape(cent)

    return jax.shard_map(
        per_device,
        mesh=mesh,
        in_specs=(P("dp", None), P("proto", "dp")),
        out_specs=(P("dp", "proto"), P("proto")),
        check_vma=False,
    )
```

```python
import functools

import jax
import jax.numpy as jnp
from jax import lax
from jax.experimental import pallas as pl
from jax.experimental.pallas import tpu as pltpu
from jax.sharding import PartitionSpec as P

SWEEPS = 3
LOGIT_SCALE = 40.0
F32, BF16 = jnp.float32, jnp.bfloat16
MESH = pl.DeviceIdType.MESH
GROUP = 8
SUBS = 3
PARTS = 4
JOINS = 4
LOADS = 3
UNIT = 64
LANES = 128


def dot(a, b, dims):
    return lax.dot_general(a, b, (dims, ((), ())), preferred_element_type=F32)


def kernel(sizes, emb, cen, out, mass_out, x, ut, ct, e, w, s, col_x, row_x, mass_a, mass_b, len_x, sib, leave, ring,
           sem_in, g_send, g_recv, gs_recv, cx_sem, rx_sem, ma_sem, mb_sem, lx_sem,
           sx_send, sx_recv, r_send, r_recv):
    n_dp, n_proto, rows, feat, cent = sizes
    nz = n_dp // 2
    half = nz // 2
    own = feat // n_dp
    n_rows = rows * n_dp
    n_cent = cent * n_proto
    levels = n_dp // GROUP

    d = lax.axis_index("dp")
    p = lax.axis_index("proto")
    z, c = d // 2, d % 2
    other = d + 1 - 2 * c
    right = ((z + 1) % nz) * 2 + c
    left = ((z + nz - 1) % nz) * 2 + c
    near = (right, left)
    far = ((d + 4) % n_dp, (d + n_dp - 4) % n_dp)
    in_group = d % GROUP
    level = d // GROUP
    group_ids = [{"dp": level * GROUP + (in_group + j) % GROUP} for j in range(1, GROUP)]
    level_ids = [{"dp": (d + GROUP * j) % n_dp} for j in range(1, levels)]
    dp_ids = [{"dp": (d + j) % n_dp} for j in sorted(range(1, n_dp), key=lambda j: -min(j, n_dp - j))]
    side = int(n_proto**0.5)
    moves = [(a, b) for a in range(side) for b in range(side) if a or b]
    moves.sort(key=lambda m: -sum(min(k, side - k) for k in m))
    proto_ids = [{"proto": (p // side + a) % side * side + (p % side + b) % side} for a, b in moves]

    loads = []
    for k in range(LOADS):
        chunk = pl.ds(k * (rows // LOADS), rows // LOADS)
        loads.append(pltpu.make_async_copy(emb.at[chunk], x.at[chunk], sem_in.at[k]))
        loads[k].start()

    barrier = pltpu.get_barrier_semaphore()
    partners = [{"dp": t} for t in near + far + (other,)] + proto_ids
    for t in partners:
        pl.semaphore_signal(barrier, inc=1, device_id=t, device_id_type=MESH)

    def block_rows(o, core):
        return pl.ds(pl.multiple_of((o * 2 + core) * own, own), own)

    ct[block_rows(z, c), :] = cen[...]
    pl.semaphore_wait(barrier, len(partners))

    piece = own // SUBS
    stages = half // 2

    def far_hop(o, way, stage, sub):
        at = ct.at[pl.ds(pl.multiple_of((o * 2 + c) * own + sub * piece, piece), piece)]
        return pltpu.make_async_remote_copy(
            src_ref=at, dst_ref=at, send_sem=g_send, recv_sem=g_recv.at[way, stage, sub],
            device_id={"dp": far[way]}, device_id_type=MESH)

    def near_hop(o, way, stage):
        at = ct.at[block_rows(o, c)]
        return pltpu.make_async_remote_copy(
            src_ref=at, dst_ref=at, send_sem=g_send, recv_sem=g_recv.at[way, stage, SUBS],
            device_id={"dp": near[way]}, device_id_type=MESH)

    def source(way, distance):
        return (z - distance + nz) % nz if way == 0 else (z + distance) % nz

    def across(o, slot):
        at = ct.at[block_rows(o, c)]
        return pltpu.make_async_remote_copy(
            src_ref=at, dst_ref=at, send_sem=g_send, recv_sem=gs_recv.at[slot],
            device_id={"dp": other}, device_id_type=MESH)

    pending = []

    def launch(desc):
        desc.start()

    for sub in range(SUBS):
        for way in (0, 1):
            launch(far_hop(z, way, 0, sub))
    for way in (0, 1):
        launch(near_hop(z, way, 0))
    launch(across(z, 0))

    def square(o, core):
        v = ct[block_rows(o, core), :].astype(F32)
        return jnp.sum((v * v).reshape(own // 8, 8, cent), axis=0)

    tile, short = 256, 128
    eye = (
        lax.broadcasted_iota(jnp.int32, (tile, tile), 0) == lax.broadcasted_iota(jnp.int32, (tile, tile), 1)
    ).astype(BF16)

    def prepare(b):
        at = pl.ds(b * short, short)
        v = x[at, :].astype(F32)
        u = (v * (1.0 / jnp.sqrt(jnp.sum(v * v, axis=1, keepdims=True) + 1e-06))).astype(BF16)
        x[at, :] = u

    def turn(b):
        at = pl.ds(b * short, short)
        for f in range(feat // tile):
            ut[pl.ds(f * tile, tile), at] = dot(
                eye, x[at, f * tile:(f + 1) * tile], ((1,), (1,))).astype(BF16)

    squares = square(z, c)
    behind = [(z, 0)]
    unit = 0
    for stage in range(stages):
        came = []
        if stage > 0:
            loads[stage - 1].wait()
            for _ in range(rows // short // LOADS):
                prepare(unit)
                unit += 1
        for sub in range(SUBS):
            for way in (0, 1):
                if stage == stages - 1 and way == 1:
                    continue
                o = source(way, 2 * stage + 2)
                far_hop(o, way, stage, sub).wait_recv()
                if stage < stages - 1 and (stage < stages - 2 or way == 0):
                    launch(far_hop(o, way, stage + 1, sub))
                if sub == SUBS - 1:
                    if stage < stages - 1:
                        launch(near_hop(o, way, stage + 1))
                    launch(across(o, 2 + 4 * stage + way))
                    came.append((o, 2 + 4 * stage + way))
        for way in (0, 1):
            o = source(way, 2 * stage + 1)
            near_hop(o, way, stage).wait_recv()
            slot = 4 * stage + 4 + way if stage < stages - 1 else (1, 2 * half - 1)[way]
            launch(across(o, slot))
            came.append((o, slot))
        for o, slot in behind:
            across(o, slot).wait_recv()
            squares = squares + square(o, 1 - c)
        for o, slot in came:
            squares = squares + square(o, c)
        behind = came
    for o, slot in behind:
        across(o, slot).wait_recv()
        squares = squares + square(o, 1 - c)

    scale = LOGIT_SCALE * (1.0 / jnp.sqrt(jnp.sum(squares, axis=0, keepdims=True) + 1e-06))
    m_tile = rows // 4

    def product(b):
        return dot(x[b * m_tile:(b + 1) * m_tile, :], ct[...], ((1,), (0,)))

    acc = jnp.zeros((8, cent), F32)
    raw = product(0)
    for b in range(4):
        ahead = product(b + 1) if b < 3 else None
        v = jnp.exp(raw * scale)
        e[b * m_tile:(b + 1) * m_tile, :] = v
        acc = acc + jnp.sum(v.reshape(m_tile // 8, 8, cent), axis=0)
        raw = ahead

    def send_all(buf, sem, me, ids):
        for t in ids:
            pltpu.make_async_remote_copy(
                src_ref=buf.at[me], dst_ref=buf.at[me], send_sem=sem.at[0], recv_sem=sem.at[1],
                device_id=t, device_id_type=MESH).start()
        whole = buf.at[pl.ds(0, len(ids))]
        done = pltpu.make_async_remote_copy(
            src_ref=whole, dst_ref=whole, send_sem=sem.at[0], recv_sem=sem.at[1],
            device_id=ids[0], device_id_type=MESH)
        pending.append(done)
        return done

    def total(buf, ids):
        terms = [buf[k] for k in range(len(ids) + 1)]
        while len(terms) > 1:
            terms = [terms[k] + terms[k + 1] for k in range(0, len(terms), 2)]
        return terms[0]

    def exchange(buf, sem, me, ids, units=(), drain=None):
        done = send_all(buf, sem, me, ids)
        for b in units:
            turn(b)
        if drain:
            drain()
        done.wait_recv()
        return total(buf, ids)

    lane = lax.broadcasted_iota(jnp.int32, (8, LANES), 1)
    tiles = [(0, LANES), (LANES, rows // 8)]

    per_sweep = rows // short // SWEEPS
    for i in range(SWEEPS):
        turns = range(i * per_sweep, (i + 1) * per_sweep)
        col_x[i, d] = jnp.sum(acc, axis=0, keepdims=True)
        cv = 1.0 / (n_cent * exchange(col_x.at[i], cx_sem.at[i], d, dp_ids, turns[0:2]))
        cb = jnp.broadcast_to(cv, (8, cent))

        totals = []
        for lo, hi in tiles:
            def row_step(g, t):
                for k in range(UNIT):
                    q = e[pl.ds(pl.multiple_of((lo + g * UNIT + k) * 8, 8), 8), :] * cb
                    q = functools.reduce(
                        lambda a, b: a + b, [q[:, m * LANES:(m + 1) * LANES] for m in range(cent // LANES)])
                    t = jnp.where(lane == g * UNIT + k, jnp.sum(q, axis=1, keepdims=True), t)
                return t

            totals.append(lax.fori_loop(0, (hi - lo) // UNIT, row_step, jnp.zeros((8, LANES), F32)))
        row_x[i, p, 0] = totals[0][0:4]
        row_x[i, p, 1] = totals[0][4:8]
        row_x[i, p, 2] = totals[1][0:4] + pltpu.roll(totals[1], LANES // 2, 1)[4:8]
        rv = 1.0 / (n_rows * exchange(row_x.at[i], rx_sem.at[i], p, proto_ids, turns[2:]))
        r0 = jnp.concatenate([rv[0], rv[1]], axis=0)
        r1 = jnp.concatenate([rv[2], pltpu.roll(rv[2], LANES // 2, 1)], axis=0)

        final = i == SWEEPS - 1
        nc = jnp.broadcast_to(n_rows * cv, (8, cent))
        acc = jnp.zeros((8, cent), F32)
        for (lo, hi), r in zip(tiles, (r0, r1)):
            def col_step(g, st):
                a, r = st
                for k in range(0, UNIT, 2):
                    at = pl.multiple_of((lo + g * UNIT + k) * 8, 16)
                    pair = [e[pl.ds(at + 8 * m, 8), :] * jnp.broadcast_to(r[:, k + m:k + m + 1], (8, cent))
                            for m in range(2)]
                    a = a + pair[0] + pair[1]
                    if final:
                        w[pl.ds(at, 16), :] = jnp.concatenate([v * nc for v in pair], axis=0).astype(BF16)
                return a, pltpu.roll(r, LANES - UNIT, 1)

            acc, _ = lax.fori_loop(0, (hi - lo) // UNIT, col_step, (acc, r))

    def swap(rel):
        return pltpu.make_async_remote_copy(
            src_ref=s.at[rel, pl.ds(pl.multiple_of((1 - c) * own, own), own)], dst_ref=sib.at[rel],
            send_sem=sx_send, recv_sem=sx_recv.at[rel],
            device_id={"dp": other}, device_id_type=MESH)

    def make_sums(rels):
        u = [ut[pl.ds(pl.multiple_of(((z + rel) % nz) * 2 * own, 2 * own), 2 * own), :] for rel in rels]
        v = dot(jnp.concatenate(u, axis=0) if len(u) > 1 else u[0], w[...], ((1,), (0,)))
        for k, rel in enumerate(rels):
            s[rel] = v[k * 2 * own:(k + 1) * 2 * own]
            launch(swap(rel))

    wide = cent // PARTS
    flows = []
    for hops in (half, half - 1):
        for m in range(PARTS // 2):
            for way in (0, 1):
                first = way == (0 if hops == half else 1)
                flows.append((way, m if first else PARTS // 2 + m, hops))

    def parent(q, hops):
        up = (hops - q) // 2
        return max(hops - 2 * up - 2, 0) if up < JOINS else q - 1

    def link(way, part, hops, q):
        step = q - parent(q, hops)
        return pltpu.make_async_remote_copy(
            src_ref=leave.at[way, part, q - 1], dst_ref=ring.at[way, part, q - 1],
            send_sem=r_send, recv_sem=r_recv.at[way, part, q - 1],
            device_id={"dp": (near if step == 1 else far)[way]}, device_id_type=MESH)

    own_rows = pl.ds(pl.multiple_of(c * own, own), own)
    ready = set()

    def gathered(way, part, hops, q):
        rel = (q if way == 0 else nz - q) % nz
        if rel not in ready:
            swap(rel).wait_recv()
            ready.add(rel)
        cols = pl.ds(part * wide, wide)
        v = s[rel, own_rows, cols] + sib[rel, :, cols]
        return v + children(way, part, hops, q) if q else v

    def children(way, part, hops, q):
        v = 0.0
        for child in range(1, hops + 1):
            if parent(child, hops) == q:
                link(way, part, hops, child).wait_recv()
                v = v + ring[way, part, child - 1]
        return v

    def pass_on(distances):
        for way, part, hops in flows:
            for q in distances(hops):
                leave[way, part, q - 1] = gathered(way, part, hops, q)
                launch(link(way, part, hops, q))

    mass_a[in_group] = jnp.sum(acc, axis=0, keepdims=True)
    mass_first = send_all(mass_a, ma_sem, in_group, group_ids)
    make_sums([half])
    make_sums([half - 1, half + 1])
    make_sums([half - 2, half + 2])
    make_sums([half - 3, half + 3])
    make_sums([half - 4, half + 4])
    pass_on(lambda hops: (hops, hops - 1))
    pass_on(lambda hops: (hops - 3,))
    mass_first.wait_recv()
    mass_b[level] = total(mass_a, group_ids)
    mass_second = send_all(mass_b, mb_sem, level, level_ids)
    make_sums([half - 5, half + 5])
    make_sums([half - 6, half + 6])
    pass_on(lambda hops: (hops - 2,))
    pass_on(lambda hops: (hops - 5,))
    make_sums([half - 7, half + 7])
    make_sums([0])
    for up in (4, 7, 6):
        pass_on(lambda hops: (hops - up,) if hops > up else ())
    parts = []
    for part in range(PARTS):
        v = gathered(0, part, half, 0)
        for way, q, hops in flows:
            if q == part:
                v = v + children(way, part, hops, 0)
        parts.append(v)
    sums = jnp.concatenate(parts, axis=1)
    len_x[d] = jnp.sum(sums * sums, axis=0, keepdims=True)

    def drain():
        for ref, sem in ((ct.at[pl.ds(0, (2 * nz - 1) * own)], g_send), (sib, sx_send),
                         (sib.at[pl.ds(0, nz - 1)], r_send)):
            pltpu.make_async_remote_copy(
                src_ref=ref, dst_ref=ref, send_sem=sem, recv_sem=sem,
                device_id={"dp": other}, device_id_type=MESH).wait_send()
        for desc in pending:
            desc.wait_send()
        pending.clear()

    lengths = exchange(len_x, lx_sem, d, dp_ids, drain=drain)
    out[...] = sums * (1.0 / jnp.sqrt(lengths + 1e-06))
    mass_second.wait_recv()
    mass_out[...] = n_cent * cv * total(mass_b, level_ids)


def hand_over(sums, mass, sums_out, mass_out):
    sums_out[...] = sums[...]
    mass_out[...] = mass[...]


def solution(mesh):
    n_dp, n_proto = mesh.shape["dp"], mesh.shape["proto"]
    nz = n_dp // 2
    half = nz // 2
    levels = n_dp // GROUP

    def per_device(embeddings, centroids):
        rows, feat = embeddings.shape
        cent = centroids.shape[0]
        own = feat // n_dp
        dma, vmem = pltpu.SemaphoreType.DMA, pltpu.VMEM
        whole, anywhere = pl.BlockSpec(memory_space=pltpu.VMEM), pl.BlockSpec(memory_space=pl.ANY)
        shapes = (jax.ShapeDtypeStruct((own, cent), F32), jax.ShapeDtypeStruct((1, cent), F32))
        sums, mass = pl.pallas_call(
            functools.partial(kernel, (n_dp, n_proto, rows, feat, cent)),
            out_shape=shapes,
            in_specs=[anywhere, whole],
            out_specs=(whole, whole),
            scratch_shapes=[
                vmem((rows, feat), BF16),
                vmem((feat, rows), BF16),
                vmem((feat, cent), BF16),
                vmem((rows, cent), F32),
                vmem((rows, cent), BF16),
                vmem((nz, 2 * own, cent), F32),
                vmem((SWEEPS, n_dp, 1, cent), F32),
                vmem((SWEEPS, n_proto, 3, 4, LANES), F32),
                vmem((GROUP, 1, cent), F32),
                vmem((levels, 1, cent), F32),
                vmem((n_dp, 1, cent), F32),
                vmem((nz, own, cent), F32),
                vmem((2, PARTS, half, own, cent // PARTS), F32),
                vmem((2, PARTS, half, own, cent // PARTS), F32),
                dma((LOADS,)),
                dma, dma((2, half // 2, SUBS + 1)), dma((nz,)),
                dma((SWEEPS, 2)), dma((SWEEPS, 2)), dma((2,)), dma((2,)), dma((2,)),
                dma, dma((nz,)), dma, dma((2, PARTS, half)),
            ],
            compiler_params=pltpu.CompilerParams(
                collective_id=0, has_side_effects=True, vmem_limit_bytes=56 * 1024 * 1024),
            cost_estimate=pl.CostEstimate(
                flops=4 * rows * feat * cent, bytes_accessed=2 * rows * feat, transcendentals=rows * cent),
        )(embeddings, centroids.T)
        new_centroids, mass = pl.pallas_call(
            hand_over, out_shape=shapes, in_specs=[whole, whole], out_specs=(whole, whole))(sums, mass)
        return new_centroids, mass.reshape(cent)

    return jax.shard_map(
        per_device,
        mesh=mesh,
        in_specs=(P("dp", None), P("proto", "dp")),
        out_specs=(P("dp", "proto"), P("proto")),
        check_vma=False,
    )
```

```python
import functools

import jax
import jax.numpy as jnp
from jax import lax
from jax.experimental import pallas as pl
from jax.experimental.pallas import tpu as pltpu
from jax.sharding import PartitionSpec as P

SWEEPS = 3
LOGIT_SCALE = 40.0
F32, BF16 = jnp.float32, jnp.bfloat16
MESH = pl.DeviceIdType.MESH
GROUP = 8
SUBS = 3
PARTS = 4
DEPTH = 5
LOADS = 3
UNIT = 64
LANES = 128


def dot(a, b, dims):
    return lax.dot_general(a, b, (dims, ((), ())), preferred_element_type=F32)


def kernel(sizes, emb, cen, out, mass_out, x, ut, ct, e, w, s, col_x, row_x, mass_a, mass_b, len_x, sib, leave, ring,
           sem_in, g_send, g_recv, gs_recv, cx_sem, rx_sem, ma_sem, mb_sem, lx_sem,
           sx_send, sx_recv, r_send, r_recv):
    n_dp, n_proto, rows, feat, cent = sizes
    nz = n_dp // 2
    half = nz // 2
    own = feat // n_dp
    n_rows = rows * n_dp
    n_cent = cent * n_proto
    levels = n_dp // GROUP

    d = lax.axis_index("dp")
    p = lax.axis_index("proto")
    z, c = d // 2, d % 2
    other = d + 1 - 2 * c
    right = ((z + 1) % nz) * 2 + c
    left = ((z + nz - 1) % nz) * 2 + c
    near = (right, left)
    far = ((d + 4) % n_dp, (d + n_dp - 4) % n_dp)
    in_group = d % GROUP
    level = d // GROUP
    group_ids = [{"dp": level * GROUP + (in_group + j) % GROUP} for j in range(1, GROUP)]
    level_ids = [{"dp": (d + GROUP * j) % n_dp} for j in range(1, levels)]
    dp_ids = [{"dp": (d + j) % n_dp} for j in sorted(range(1, n_dp), key=lambda j: -min(j, n_dp - j))]
    side = int(n_proto**0.5)
    moves = [(a, b) for a in range(side) for b in range(side) if a or b]
    moves.sort(key=lambda m: -sum(min(k, side - k) for k in m))
    proto_ids = [{"proto": (p // side + a) % side * side + (p % side + b) % side} for a, b in moves]

    loads = []
    for k in range(LOADS):
        chunk = pl.ds(k * (rows // LOADS), rows // LOADS)
        loads.append(pltpu.make_async_copy(emb.at[chunk], x.at[chunk], sem_in.at[k]))
        loads[k].start()

    barrier = pltpu.get_barrier_semaphore()
    partners = [{"dp": t} for t in near + far + (other,)] + proto_ids
    for t in partners:
        pl.semaphore_signal(barrier, inc=1, device_id=t, device_id_type=MESH)

    def block_rows(o, core):
        return pl.ds(pl.multiple_of((o * 2 + core) * own, own), own)

    ct[block_rows(z, c), :] = cen[...]
    pl.semaphore_wait(barrier, len(partners))

    piece = own // SUBS
    stages = half // 2

    def far_hop(o, way, stage, sub):
        at = ct.at[pl.ds(pl.multiple_of((o * 2 + c) * own + sub * piece, piece), piece)]
        return pltpu.make_async_remote_copy(
            src_ref=at, dst_ref=at, send_sem=g_send, recv_sem=g_recv.at[way, stage, sub],
            device_id={"dp": far[way]}, device_id_type=MESH)

    def near_hop(o, way, stage):
        at = ct.at[block_rows(o, c)]
        return pltpu.make_async_remote_copy(
            src_ref=at, dst_ref=at, send_sem=g_send, recv_sem=g_recv.at[way, stage, SUBS],
            device_id={"dp": near[way]}, device_id_type=MESH)

    def source(way, distance):
        return (z - distance + nz) % nz if way == 0 else (z + distance) % nz

    def across(o, slot):
        at = ct.at[block_rows(o, c)]
        return pltpu.make_async_remote_copy(
            src_ref=at, dst_ref=at, send_sem=g_send, recv_sem=gs_recv.at[slot],
            device_id={"dp": other}, device_id_type=MESH)

    pending = []

    def launch(desc):
        desc.start()

    for sub in range(SUBS):
        for way in (0, 1):
            launch(far_hop(z, way, 0, sub))
    for way in (0, 1):
        launch(near_hop(z, way, 0))
    launch(across(z, 0))

    def square(o, core):
        v = ct[block_rows(o, core), :].astype(F32)
        return jnp.sum((v * v).reshape(own // 8, 8, cent), axis=0)

    tile, short = 256, 128
    eye = (
        lax.broadcasted_iota(jnp.int32, (tile, tile), 0) == lax.broadcasted_iota(jnp.int32, (tile, tile), 1)
    ).astype(BF16)

    def prepare(b):
        at = pl.ds(b * short, short)
        v = x[at, :].astype(F32)
        u = (v * (1.0 / jnp.sqrt(jnp.sum(v * v, axis=1, keepdims=True) + 1e-06))).astype(BF16)
        x[at, :] = u

    def turn(b):
        at = pl.ds(b * short, short)
        for f in range(feat // tile):
            ut[pl.ds(f * tile, tile), at] = dot(
                eye, x[at, f * tile:(f + 1) * tile], ((1,), (1,))).astype(BF16)

    squares = square(z, c)
    behind = [(z, 0)]
    unit = 0
    opposite = ((0, 1), (2,))
    for stage in range(stages):
        came = []
        if stage > 0:
            loads[stage - 1].wait()
            for _ in range(rows // short // LOADS):
                prepare(unit)
                unit += 1
        for sub in range(SUBS):
            for way in (0, 1):
                if stage == stages - 1 and sub not in opposite[way]:
                    continue
                o = source(way, 2 * stage + 2)
                far_hop(o, way, stage, sub).wait_recv()
                if stage < stages - 1 and (stage < stages - 2 or sub in opposite[way]):
                    launch(far_hop(o, way, stage + 1, sub))
                if sub == SUBS - 1:
                    if stage < stages - 1:
                        launch(near_hop(o, way, stage + 1))
                    slot = 2 + 4 * stage + (way if stage < stages - 1 else 0)
                    launch(across(o, slot))
                    came.append((o, slot))
        for way in (0, 1):
            o = source(way, 2 * stage + 1)
            near_hop(o, way, stage).wait_recv()
            slot = 4 * stage + 4 + way if stage < stages - 1 else (1, 2 * half - 1)[way]
            launch(across(o, slot))
            came.append((o, slot))
        for o, slot in behind:
            across(o, slot).wait_recv()
            squares = squares + square(o, 1 - c)
        for o, slot in came:
            squares = squares + square(o, c)
        behind = came
    for o, slot in behind:
        across(o, slot).wait_recv()
        squares = squares + square(o, 1 - c)

    scale = LOGIT_SCALE * (1.0 / jnp.sqrt(jnp.sum(squares, axis=0, keepdims=True) + 1e-06))
    m_tile = rows // 4

    def product(b):
        return dot(x[b * m_tile:(b + 1) * m_tile, :], ct[...], ((1,), (0,)))

    acc = jnp.zeros((8, cent), F32)
    raw = product(0)
    for b in range(4):
        ahead = product(b + 1) if b < 3 else None
        v = jnp.exp(raw * scale)
        e[b * m_tile:(b + 1) * m_tile, :] = v
        acc = acc + jnp.sum(v.reshape(m_tile // 8, 8, cent), axis=0)
        raw = ahead

    def send_all(buf, sem, me, ids):
        for t in ids:
            pltpu.make_async_remote_copy(
                src_ref=buf.at[me], dst_ref=buf.at[me], send_sem=sem.at[0], recv_sem=sem.at[1],
                device_id=t, device_id_type=MESH).start()
        whole = buf.at[pl.ds(0, len(ids))]
        done = pltpu.make_async_remote_copy(
            src_ref=whole, dst_ref=whole, send_sem=sem.at[0], recv_sem=sem.at[1],
            device_id=ids[0], device_id_type=MESH)
        pending.append(done)
        return done

    def total(buf, ids):
        terms = [buf[k] for k in range(len(ids) + 1)]
        while len(terms) > 1:
            terms = [terms[k] + terms[k + 1] for k in range(0, len(terms), 2)]
        return terms[0]

    def exchange(buf, sem, me, ids, units=(), drain=None):
        done = send_all(buf, sem, me, ids)
        for b in units:
            turn(b)
        if drain:
            drain()
        done.wait_recv()
        return total(buf, ids)

    lane = lax.broadcasted_iota(jnp.int32, (8, LANES), 1)
    tiles = [(0, LANES), (LANES, rows // 8)]

    per_sweep = rows // short // SWEEPS
    for i in range(SWEEPS):
        turns = range(i * per_sweep, (i + 1) * per_sweep)
        col_x[i, d] = jnp.sum(acc, axis=0, keepdims=True)
        cv = 1.0 / (n_cent * exchange(col_x.at[i], cx_sem.at[i], d, dp_ids, turns[0:2]))
        cb = jnp.broadcast_to(cv, (8, cent))

        totals = []
        for lo, hi in tiles:
            def row_step(g, t):
                for k in range(UNIT):
                    q = e[pl.ds(pl.multiple_of((lo + g * UNIT + k) * 8, 8), 8), :] * cb
                    q = functools.reduce(
                        lambda a, b: a + b, [q[:, m * LANES:(m + 1) * LANES] for m in range(cent // LANES)])
                    t = jnp.where(lane == g * UNIT + k, jnp.sum(q, axis=1, keepdims=True), t)
                return t

            totals.append(lax.fori_loop(0, (hi - lo) // UNIT, row_step, jnp.zeros((8, LANES), F32)))
        row_x[i, p, 0] = totals[0][0:4]
        row_x[i, p, 1] = totals[0][4:8]
        row_x[i, p, 2] = totals[1][0:4] + pltpu.roll(totals[1], LANES // 2, 1)[4:8]
        rv = 1.0 / (n_rows * exchange(row_x.at[i], rx_sem.at[i], p, proto_ids, turns[2:]))
        r0 = jnp.concatenate([rv[0], rv[1]], axis=0)
        r1 = jnp.concatenate([rv[2], pltpu.roll(rv[2], LANES // 2, 1)], axis=0)

        final = i == SWEEPS - 1
        nc = jnp.broadcast_to(n_rows * cv, (8, cent))
        acc = jnp.zeros((8, cent), F32)
        for (lo, hi), r in zip(tiles, (r0, r1)):
            def col_step(g, st):
                a, r = st
                for k in range(0, UNIT, 2):
                    at = pl.multiple_of((lo + g * UNIT + k) * 8, 16)
                    pair = [e[pl.ds(at + 8 * m, 8), :] * jnp.broadcast_to(r[:, k + m:k + m + 1], (8, cent))
                            for m in range(2)]
                    a = a + pair[0] + pair[1]
                    if final:
                        w[pl.ds(at, 16), :] = jnp.concatenate([v * nc for v in pair], axis=0).astype(BF16)
                return a, pltpu.roll(r, LANES - UNIT, 1)

            acc, _ = lax.fori_loop(0, (hi - lo) // UNIT, col_step, (acc, r))

    def swap(rel):
        return pltpu.make_async_remote_copy(
            src_ref=s.at[rel, pl.ds(pl.multiple_of((1 - c) * own, own), own)], dst_ref=sib.at[rel],
            send_sem=sx_send, recv_sem=sx_recv.at[rel],
            device_id={"dp": other}, device_id_type=MESH)

    def make_sums(rels):
        u = [ut[pl.ds(pl.multiple_of(((z + rel) % nz) * 2 * own, 2 * own), 2 * own), :] for rel in rels]
        v = dot(jnp.concatenate(u, axis=0) if len(u) > 1 else u[0], w[...], ((1,), (0,)))
        for k, rel in enumerate(rels):
            s[rel] = v[k * 2 * own:(k + 1) * 2 * own]
            launch(swap(rel))

    wide = cent // PARTS
    flows = []
    for hops in (half, half - 1):
        for m in range(PARTS // 2):
            for way in (0, 1):
                first = way == (0 if hops == half else 1)
                flows.append((way, m if first else PARTS // 2 + m, hops))

    def parent(q, hops):
        up = (hops - q) // 2
        return hops - 2 * up - 2 if up < hops - DEPTH else q - 1

    def link(way, part, hops, q):
        step = q - parent(q, hops)
        return pltpu.make_async_remote_copy(
            src_ref=leave.at[way, part, q - 1], dst_ref=ring.at[way, part, q - 1],
            send_sem=r_send, recv_sem=r_recv.at[way, part, q - 1],
            device_id={"dp": (near if step == 1 else far)[way]}, device_id_type=MESH)

    own_rows = pl.ds(pl.multiple_of(c * own, own), own)
    ready = set()

    def gathered(way, part, hops, q):
        rel = (q if way == 0 else nz - q) % nz
        if rel not in ready:
            swap(rel).wait_recv()
            ready.add(rel)
        cols = pl.ds(part * wide, wide)
        v = s[rel, own_rows, cols] + sib[rel, :, cols]
        return v + children(way, part, hops, q) if q else v

    def children(way, part, hops, q):
        v = 0.0
        for child in range(1, hops + 1):
            if parent(child, hops) == q:
                link(way, part, hops, child).wait_recv()
                v = v + ring[way, part, child - 1]
        return v

    def pass_on(distances):
        for way, part, hops in flows:
            for q in distances(hops):
                leave[way, part, q - 1] = gathered(way, part, hops, q)
                launch(link(way, part, hops, q))

    mass_a[in_group] = jnp.sum(acc, axis=0, keepdims=True)
    mass_first = send_all(mass_a, ma_sem, in_group, group_ids)
    make_sums([half])
    make_sums([half - 1, half + 1])
    make_sums([half - 2, half + 2])
    make_sums([half - 3, half + 3])
    make_sums([half - 4, half + 4])
    pass_on(lambda hops: (hops, hops - 1))
    pass_on(lambda hops: (hops - 3,))
    mass_first.wait_recv()
    mass_b[level] = total(mass_a, group_ids)
    mass_second = send_all(mass_b, mb_sem, level, level_ids)
    make_sums([half - 5, half + 5])
    make_sums([half - 6, half + 6])
    pass_on(lambda hops: (hops - 2,))
    pass_on(lambda hops: (3,) if hops == half else ())
    make_sums([half - 7, half + 7])
    make_sums([0])
    pass_on(lambda hops: (hops - 4,))
    pass_on(lambda hops: (2,))
    pass_on(lambda hops: (1,))
    parts = []
    for part in range(PARTS):
        v = gathered(0, part, half, 0)
        for way, q, hops in flows:
            if q == part:
                v = v + children(way, part, hops, 0)
        parts.append(v)
    sums = jnp.concatenate(parts, axis=1)
    len_x[d] = jnp.sum(sums * sums, axis=0, keepdims=True)

    def drain():
        for ref, sem in ((ct.at[pl.ds(0, (2 * nz - 1) * own)], g_send), (sib, sx_send),
                         (sib.at[pl.ds(0, nz - 1)], r_send)):
            pltpu.make_async_remote_copy(
                src_ref=ref, dst_ref=ref, send_sem=sem, recv_sem=sem,
                device_id={"dp": other}, device_id_type=MESH).wait_send()
        for desc in pending:
            desc.wait_send()
        pending.clear()

    lengths = exchange(len_x, lx_sem, d, dp_ids, drain=drain)
    out[...] = sums * (1.0 / jnp.sqrt(lengths + 1e-06))
    mass_second.wait_recv()
    mass_out[...] = n_cent * cv * total(mass_b, level_ids)


def hand_over(sums, mass, sums_out, mass_out):
    sums_out[...] = sums[...]
    mass_out[...] = mass[...]


def solution(mesh):
    n_dp, n_proto = mesh.shape["dp"], mesh.shape["proto"]
    nz = n_dp // 2
    half = nz // 2
    levels = n_dp // GROUP

    def per_device(embeddings, centroids):
        rows, feat = embeddings.shape
        cent = centroids.shape[0]
        own = feat // n_dp
        dma, vmem = pltpu.SemaphoreType.DMA, pltpu.VMEM
        whole, anywhere = pl.BlockSpec(memory_space=pltpu.VMEM), pl.BlockSpec(memory_space=pl.ANY)
        shapes = (jax.ShapeDtypeStruct((own, cent), F32), jax.ShapeDtypeStruct((1, cent), F32))
        sums, mass = pl.pallas_call(
            functools.partial(kernel, (n_dp, n_proto, rows, feat, cent)),
            out_shape=shapes,
            in_specs=[anywhere, whole],
            out_specs=(whole, whole),
            scratch_shapes=[
                vmem((rows, feat), BF16),
                vmem((feat, rows), BF16),
                vmem((feat, cent), BF16),
                vmem((rows, cent), F32),
                vmem((rows, cent), BF16),
                vmem((nz, 2 * own, cent), F32),
                vmem((SWEEPS, n_dp, 1, cent), F32),
                vmem((SWEEPS, n_proto, 3, 4, LANES), F32),
                vmem((GROUP, 1, cent), F32),
                vmem((levels, 1, cent), F32),
                vmem((n_dp, 1, cent), F32),
                vmem((nz, own, cent), F32),
                vmem((2, PARTS, half, own, cent // PARTS), F32),
                vmem((2, PARTS, half, own, cent // PARTS), F32),
                dma((LOADS,)),
                dma, dma((2, half // 2, SUBS + 1)), dma((nz,)),
                dma((SWEEPS, 2)), dma((SWEEPS, 2)), dma((2,)), dma((2,)), dma((2,)),
                dma, dma((nz,)), dma, dma((2, PARTS, half)),
            ],
            compiler_params=pltpu.CompilerParams(
                collective_id=0, has_side_effects=True, vmem_limit_bytes=56 * 1024 * 1024),
            cost_estimate=pl.CostEstimate(
                flops=4 * rows * feat * cent, bytes_accessed=2 * rows * feat, transcendentals=rows * cent),
        )(embeddings, centroids.T)
        new_centroids, mass = pl.pallas_call(
            hand_over, out_shape=shapes, in_specs=[whole, whole], out_specs=(whole, whole))(sums, mass)
        return new_centroids, mass.reshape(cent)

    return jax.shard_map(
        per_device,
        mesh=mesh,
        in_specs=(P("dp", None), P("proto", "dp")),
        out_specs=(P("dp", "proto"), P("proto")),
        check_vma=False,
    )
```

```python
import functools

import jax
import jax.numpy as jnp
from jax import lax
from jax.experimental import pallas as pl
from jax.experimental.pallas import tpu as pltpu
from jax.sharding import PartitionSpec as P

SWEEPS = 3
LOGIT_SCALE = 40.0
F32, BF16 = jnp.float32, jnp.bfloat16
MESH = pl.DeviceIdType.MESH
GROUP = 8
SUBS = 3
PARTS = 4
JOINS = 4
LOADS = 3
UNIT = 64
LANES = 128


def dot(a, b, dims):
    return lax.dot_general(a, b, (dims, ((), ())), preferred_element_type=F32)


def kernel(sizes, emb, cen, out, mass_out, x, ut, ct, e, w, s, col_x, row_x, mass_a, mass_b, len_x, sib, leave, ring,
           sem_in, g_send, g_recv, gs_recv, cx_sem, rx_sem, ma_sem, mb_sem, lx_sem,
           sx_send, sx_recv, r_send, r_recv):
    n_dp, n_proto, rows, feat, cent = sizes
    nz = n_dp // 2
    half = nz // 2
    own = feat // n_dp
    n_rows = rows * n_dp
    n_cent = cent * n_proto
    levels = n_dp // GROUP

    d = lax.axis_index("dp")
    p = lax.axis_index("proto")
    z, c = d // 2, d % 2
    other = d + 1 - 2 * c
    right = ((z + 1) % nz) * 2 + c
    left = ((z + nz - 1) % nz) * 2 + c
    near = (right, left)
    far = ((d + 4) % n_dp, (d + n_dp - 4) % n_dp)
    in_group = d % GROUP
    level = d // GROUP
    group_ids = [{"dp": level * GROUP + (in_group + j) % GROUP} for j in range(1, GROUP)]
    level_ids = [{"dp": (d + GROUP * j) % n_dp} for j in range(1, levels)]
    dp_ids = [{"dp": (d + j) % n_dp} for j in sorted(range(1, n_dp), key=lambda j: -min(j, n_dp - j))]
    side = int(n_proto**0.5)
    moves = [(a, b) for a in range(side) for b in range(side) if a or b]
    moves.sort(key=lambda m: -sum(min(k, side - k) for k in m))
    proto_ids = [{"proto": (p // side + a) % side * side + (p % side + b) % side} for a, b in moves]

    loads = []
    for k in range(LOADS):
        chunk = pl.ds(k * (rows // LOADS), rows // LOADS)
        loads.append(pltpu.make_async_copy(emb.at[chunk], x.at[chunk], sem_in.at[k]))
        loads[k].start()

    barrier = pltpu.get_barrier_semaphore()
    partners = [{"dp": t} for t in near + far + (other,)] + proto_ids
    for t in partners:
        pl.semaphore_signal(barrier, inc=1, device_id=t, device_id_type=MESH)

    def block_rows(o, core):
        return pl.ds(pl.multiple_of((o * 2 + core) * own, own), own)

    ct[block_rows(z, c), :] = cen[...]
    pl.semaphore_wait(barrier, len(partners))

    piece = own // SUBS
    stages = half // 2

    def far_hop(o, way, stage, sub):
        at = ct.at[pl.ds(pl.multiple_of((o * 2 + c) * own + sub * piece, piece), piece)]
        return pltpu.make_async_remote_copy(
            src_ref=at, dst_ref=at, send_sem=g_send, recv_sem=g_recv.at[way, stage, sub],
            device_id={"dp": far[way]}, device_id_type=MESH)

    def near_hop(o, way, stage):
        at = ct.at[block_rows(o, c)]
        return pltpu.make_async_remote_copy(
            src_ref=at, dst_ref=at, send_sem=g_send, recv_sem=g_recv.at[way, stage, SUBS],
            device_id={"dp": near[way]}, device_id_type=MESH)

    def source(way, distance):
        return (z - distance + nz) % nz if way == 0 else (z + distance) % nz

    def across(o, slot):
        at = ct.at[block_rows(o, c)]
        return pltpu.make_async_remote_copy(
            src_ref=at, dst_ref=at, send_sem=g_send, recv_sem=gs_recv.at[slot],
            device_id={"dp": other}, device_id_type=MESH)

    pending = []

    def launch(desc):
        desc.start()

    for sub in range(SUBS):
        for way in (0, 1):
            launch(far_hop(z, way, 0, sub))
    for way in (0, 1):
        launch(near_hop(z, way, 0))
    launch(across(z, 0))

    def square(o, core):
        v = ct[block_rows(o, core), :].astype(F32)
        return jnp.sum((v * v).reshape(own // 8, 8, cent), axis=0)

    tile, short = 256, 128
    eye = (
        lax.broadcasted_iota(jnp.int32, (tile, tile), 0) == lax.broadcasted_iota(jnp.int32, (tile, tile), 1)
    ).astype(BF16)

    def prepare(b):
        at = pl.ds(b * short, short)
        v = x[at, :].astype(F32)
        u = (v * (1.0 / jnp.sqrt(jnp.sum(v * v, axis=1, keepdims=True) + 1e-06))).astype(BF16)
        x[at, :] = u

    def turn(b):
        at = pl.ds(b * short, short)
        for f in range(feat // tile):
            ut[pl.ds(f * tile, tile), at] = dot(
                eye, x[at, f * tile:(f + 1) * tile], ((1,), (1,))).astype(BF16)

    squares = square(z, c)
    behind = [(z, 0)]
    unit = 0
    for stage in range(stages):
        came = []
        if stage > 0:
            loads[stage - 1].wait()
            for _ in range(rows // short // LOADS):
                prepare(unit)
                unit += 1
        for sub in range(SUBS):
            for way in (0, 1):
                if stage == stages - 1 and way == 1:
                    continue
                o = source(way, 2 * stage + 2)
                far_hop(o, way, stage, sub).wait_recv()
                if stage < stages - 1 and (stage < stages - 2 or way == 0):
                    launch(far_hop(o, way, stage + 1, sub))
                if sub == SUBS - 1:
                    if stage < stages - 1:
                        launch(near_hop(o, way, stage + 1))
                    launch(across(o, 2 + 4 * stage + way))
                    came.append((o, 2 + 4 * stage + way))
        for way in (0, 1):
            o = source(way, 2 * stage + 1)
            near_hop(o, way, stage).wait_recv()
            slot = 4 * stage + 4 + way if stage < stages - 1 else (1, 2 * half - 1)[way]
            launch(across(o, slot))
            came.append((o, slot))
        for o, slot in behind:
            across(o, slot).wait_recv()
            squares = squares + square(o, 1 - c)
        for o, slot in came:
            squares = squares + square(o, c)
        behind = came
    for o, slot in behind:
        across(o, slot).wait_recv()
        squares = squares + square(o, 1 - c)

    scale = LOGIT_SCALE * (1.0 / jnp.sqrt(jnp.sum(squares, axis=0, keepdims=True) + 1e-06))
    m_tile = rows // 2

    def product(b):
        return dot(x[b * m_tile:(b + 1) * m_tile, :], ct[...], ((1,), (0,)))

    acc = jnp.zeros((8, cent), F32)
    raw = product(0)
    for b in range(2):
        ahead = product(b + 1) if b < 1 else None
        v = jnp.exp(raw * scale)
        e[b * m_tile:(b + 1) * m_tile, :] = v
        acc = acc + jnp.sum(v.reshape(m_tile // 8, 8, cent), axis=0)
        raw = ahead

    def send_all(buf, sem, me, ids):
        for t in ids:
            pltpu.make_async_remote_copy(
                src_ref=buf.at[me], dst_ref=buf.at[me], send_sem=sem.at[0], recv_sem=sem.at[1],
                device_id=t, device_id_type=MESH).start()
        whole = buf.at[pl.ds(0, len(ids))]
        done = pltpu.make_async_remote_copy(
            src_ref=whole, dst_ref=whole, send_sem=sem.at[0], recv_sem=sem.at[1],
            device_id=ids[0], device_id_type=MESH)
        pending.append(done)
        return done

    def total(buf, ids):
        terms = [buf[k] for k in range(len(ids) + 1)]
        while len(terms) > 1:
            terms = [terms[k] + terms[k + 1] for k in range(0, len(terms), 2)]
        return terms[0]

    def exchange(buf, sem, me, ids, units=(), drain=None):
        done = send_all(buf, sem, me, ids)
        for b in units:
            turn(b)
        if drain:
            drain()
        done.wait_recv()
        return total(buf, ids)

    lane = lax.broadcasted_iota(jnp.int32, (8, LANES), 1)
    tiles = [(0, LANES), (LANES, rows // 8)]

    per_sweep = rows // short // SWEEPS
    for i in range(SWEEPS):
        turns = range(i * per_sweep, (i + 1) * per_sweep)
        col_x[i, d] = jnp.sum(acc, axis=0, keepdims=True)
        cv = 1.0 / (n_cent * exchange(col_x.at[i], cx_sem.at[i], d, dp_ids, turns[0:2]))
        cb = jnp.broadcast_to(cv, (8, cent))

        totals = []
        for lo, hi in tiles:
            def row_step(g, t):
                for k in range(UNIT):
                    q = e[pl.ds(pl.multiple_of((lo + g * UNIT + k) * 8, 8), 8), :] * cb
                    q = functools.reduce(
                        lambda a, b: a + b, [q[:, m * LANES:(m + 1) * LANES] for m in range(cent // LANES)])
                    t = jnp.where(lane == g * UNIT + k, jnp.sum(q, axis=1, keepdims=True), t)
                return t

            totals.append(lax.fori_loop(0, (hi - lo) // UNIT, row_step, jnp.zeros((8, LANES), F32)))
        row_x[i, p, 0] = totals[0][0:4]
        row_x[i, p, 1] = totals[0][4:8]
        row_x[i, p, 2] = totals[1][0:4] + pltpu.roll(totals[1], LANES // 2, 1)[4:8]
        rv = 1.0 / (n_rows * exchange(row_x.at[i], rx_sem.at[i], p, proto_ids, turns[2:]))
        r0 = jnp.concatenate([rv[0], rv[1]], axis=0)
        r1 = jnp.concatenate([rv[2], pltpu.roll(rv[2], LANES // 2, 1)], axis=0)

        final = i == SWEEPS - 1
        nc = jnp.broadcast_to(n_rows * cv, (8, cent))
        acc = jnp.zeros((8, cent), F32)
        for (lo, hi), r in zip(tiles, (r0, r1)):
            def col_step(g, st):
                a, r = st
                for k in range(0, UNIT, 2):
                    at = pl.multiple_of((lo + g * UNIT + k) * 8, 16)
                    pair = [e[pl.ds(at + 8 * m, 8), :] * jnp.broadcast_to(r[:, k + m:k + m + 1], (8, cent))
                            for m in range(2)]
                    a = a + pair[0] + pair[1]
                    if final:
                        w[pl.ds(at, 16), :] = jnp.concatenate([v * nc for v in pair], axis=0).astype(BF16)
                return a, pltpu.roll(r, LANES - UNIT, 1)

            acc, _ = lax.fori_loop(0, (hi - lo) // UNIT, col_step, (acc, r))

    def swap(rel):
        return pltpu.make_async_remote_copy(
            src_ref=s.at[rel, pl.ds(pl.multiple_of((1 - c) * own, own), own)], dst_ref=sib.at[rel],
            send_sem=sx_send, recv_sem=sx_recv.at[rel],
            device_id={"dp": other}, device_id_type=MESH)

    def make_sums(rels):
        u = [ut[pl.ds(pl.multiple_of(((z + rel) % nz) * 2 * own, 2 * own), 2 * own), :] for rel in rels]
        v = dot(jnp.concatenate(u, axis=0) if len(u) > 1 else u[0], w[...], ((1,), (0,)))
        for k, rel in enumerate(rels):
            s[rel] = v[k * 2 * own:(k + 1) * 2 * own]
            launch(swap(rel))

    wide = cent // PARTS
    flows = []
    for hops in (half, half - 1):
        for m in range(PARTS // 2):
            for way in (0, 1):
                first = way == (0 if hops == half else 1)
                flows.append((way, m if first else PARTS // 2 + m, hops))

    def parent(q, hops):
        up = (hops - q) // 2
        return max(hops - 2 * up - 2, 0) if up < JOINS else q - 1

    def link(way, part, hops, q):
        step = q - parent(q, hops)
        return pltpu.make_async_remote_copy(
            src_ref=leave.at[way, part, q - 1], dst_ref=ring.at[way, part, q - 1],
            send_sem=r_send, recv_sem=r_recv.at[way, part, q - 1],
            device_id={"dp": (near if step == 1 else far)[way]}, device_id_type=MESH)

    own_rows = pl.ds(pl.multiple_of(c * own, own), own)
    ready = set()

    def gathered(way, part, hops, q):
        rel = (q if way == 0 else nz - q) % nz
        if rel not in ready:
            swap(rel).wait_recv()
            ready.add(rel)
        cols = pl.ds(part * wide, wide)
        v = s[rel, own_rows, cols] + sib[rel, :, cols]
        return v + children(way, part, hops, q) if q else v

    def children(way, part, hops, q):
        v = 0.0
        for child in range(1, hops + 1):
            if parent(child, hops) == q:
                link(way, part, hops, child).wait_recv()
                v = v + ring[way, part, child - 1]
        return v

    def pass_on(distances):
        for way, part, hops in flows:
            for q in distances(hops):
                leave[way, part, q - 1] = gathered(way, part, hops, q)
                launch(link(way, part, hops, q))

    mass_a[in_group] = jnp.sum(acc, axis=0, keepdims=True)
    mass_first = send_all(mass_a, ma_sem, in_group, group_ids)
    make_sums([half])
    make_sums([half - 1, half + 1])
    make_sums([half - 2, half + 2])
    make_sums([half - 3, half + 3])
    make_sums([half - 4, half + 4])
    pass_on(lambda hops: (hops, hops - 1))
    pass_on(lambda hops: (hops - 3,))
    mass_first.wait_recv()
    mass_b[level] = total(mass_a, group_ids)
    mass_second = send_all(mass_b, mb_sem, level, level_ids)
    make_sums([half - 5, half + 5])
    make_sums([half - 6, half + 6])
    pass_on(lambda hops: (hops - 2,))
    pass_on(lambda hops: (hops - 5,))
    make_sums([half - 7, half + 7])
    make_sums([0])
    for up in (4, 7, 6):
        pass_on(lambda hops: (hops - up,) if hops > up else ())
    parts = []
    for part in range(PARTS):
        v = gathered(0, part, half, 0)
        for way, q, hops in flows:
            if q == part:
                v = v + children(way, part, hops, 0)
        parts.append(v)
    sums = jnp.concatenate(parts, axis=1)
    len_x[d] = jnp.sum(sums * sums, axis=0, keepdims=True)

    def drain():
        for ref, sem in ((ct.at[pl.ds(0, (2 * nz - 1) * own)], g_send), (sib, sx_send),
                         (sib.at[pl.ds(0, nz - 1)], r_send)):
            pltpu.make_async_remote_copy(
                src_ref=ref, dst_ref=ref, send_sem=sem, recv_sem=sem,
                device_id={"dp": other}, device_id_type=MESH).wait_send()
        for desc in pending:
            desc.wait_send()
        pending.clear()

    lengths = exchange(len_x, lx_sem, d, dp_ids, drain=drain)
    out[...] = sums * (1.0 / jnp.sqrt(lengths + 1e-06))
    mass_second.wait_recv()
    mass_out[...] = n_cent * cv * total(mass_b, level_ids)


def hand_over(sums, mass, sums_out, mass_out):
    sums_out[...] = sums[...]
    mass_out[...] = mass[...]


def solution(mesh):
    n_dp, n_proto = mesh.shape["dp"], mesh.shape["proto"]
    nz = n_dp // 2
    half = nz // 2
    levels = n_dp // GROUP

    def per_device(embeddings, centroids):
        rows, feat = embeddings.shape
        cent = centroids.shape[0]
        own = feat // n_dp
        dma, vmem = pltpu.SemaphoreType.DMA, pltpu.VMEM
        whole, anywhere = pl.BlockSpec(memory_space=pltpu.VMEM), pl.BlockSpec(memory_space=pl.ANY)
        shapes = (jax.ShapeDtypeStruct((own, cent), F32), jax.ShapeDtypeStruct((1, cent), F32))
        sums, mass = pl.pallas_call(
            functools.partial(kernel, (n_dp, n_proto, rows, feat, cent)),
            out_shape=shapes,
            in_specs=[anywhere, whole],
            out_specs=(whole, whole),
            scratch_shapes=[
                vmem((rows, feat), BF16),
                vmem((feat, rows), BF16),
                vmem((feat, cent), BF16),
                vmem((rows, cent), F32),
                vmem((rows, cent), BF16),
                vmem((nz, 2 * own, cent), F32),
                vmem((SWEEPS, n_dp, 1, cent), F32),
                vmem((SWEEPS, n_proto, 3, 4, LANES), F32),
                vmem((GROUP, 1, cent), F32),
                vmem((levels, 1, cent), F32),
                vmem((n_dp, 1, cent), F32),
                vmem((nz, own, cent), F32),
                vmem((2, PARTS, half, own, cent // PARTS), F32),
                vmem((2, PARTS, half, own, cent // PARTS), F32),
                dma((LOADS,)),
                dma, dma((2, half // 2, SUBS + 1)), dma((nz,)),
                dma((SWEEPS, 2)), dma((SWEEPS, 2)), dma((2,)), dma((2,)), dma((2,)),
                dma, dma((nz,)), dma, dma((2, PARTS, half)),
            ],
            compiler_params=pltpu.CompilerParams(
                collective_id=0, has_side_effects=True, vmem_limit_bytes=56 * 1024 * 1024),
            cost_estimate=pl.CostEstimate(
                flops=4 * rows * feat * cent, bytes_accessed=2 * rows * feat, transcendentals=rows * cent),
        )(embeddings, centroids.T)
        new_centroids, mass = pl.pallas_call(
            hand_over, out_shape=shapes, in_specs=[whole, whole], out_specs=(whole, whole))(sums, mass)
        return new_centroids, mass.reshape(cent)

    return jax.shard_map(
        per_device,
        mesh=mesh,
        in_specs=(P("dp", None), P("proto", "dp")),
        out_specs=(P("dp", "proto"), P("proto")),
        check_vma=False,
    )
```
